32 devices in a mesh: dp: 8 (over y, x, core), chan: 4 (over z).
Axes of the slice: x: 2, y: 2, z: 4, core: 2. Of those that a mesh axis runs over, the one named last changes fastest.
Arguments:
- images: bfloat16 [64, 81, 2048], P('dp', None, 'chan'), may hold values from -6 to 6
- groups: int32 [64], P('dp'), may hold values from 0 to 2, as said below
- cotangent: bfloat16 [64, 81, 2048], P('dp', None, 'chan'), may hold values from -6 to 6
- reduce_weight: float32 [512, 2048], P('chan'), may hold values from -0.125 to 0.125
- spatial_weight: float32 [512, 3, 3, 512], P('chan'), may hold values from -0.09375 to 0.09375
- expand_weight: float32 [512, 2048], P('chan'), may hold values from -0.25 to 0.25
- inner_norm: float32 [2, 2, 512], P(None, None, 'chan')
- outer_norm: float32 [2, 2048], P(None, 'chan')
- reduce_moments: float32 [2, 512, 2048], P(None, 'chan'), as said below
- spatial_moments: float32 [2, 512, 3, 3, 512], P(None, 'chan')
- expand_moments: float32 [2, 512, 2048], P(None, 'chan')
- inner_moments: float32 [2, 2, 2, 512], P(None, None, None, 'chan')
- outer_moments: float32 [2, 2, 2048], P(None, None, 'chan')
- reduce_ema: float32 [512, 2048], P('chan'), may hold values from -0.125 to 0.125
- spatial_ema: float32 [512, 3, 3, 512], P('chan'), may hold values from -0.09375 to 0.09375
- expand_ema: float32 [512, 2048], P('chan'), may hold values from -0.25 to 0.25
- inner_ema: float32 [2, 2, 512], P(None, None, 'chan')
- outer_ema: float32 [2, 2048], P(None, 'chan')
Outputs:
- output: float32 [64, 81, 2048], P('dp', None, 'chan')
- input_grad: float32 [64, 81, 2048], P('dp', None, 'chan')
- new_reduce_weight: float32 [512, 2048], P('chan')
- new_reduce_first: float32 [512, 2048], P('chan')
- new_reduce_second: float32 [512, 2048], P('chan')
- new_reduce_ema: float32 [512, 2048], P('chan')
- new_spatial_weight: float32 [512, 3, 3, 512], P('chan')
- new_spatial_first: float32 [512, 3, 3, 512], P('chan')
- new_spatial_second: float32 [512, 3, 3, 512], P('chan')
- new_spatial_ema: float32 [512, 3, 3, 512], P('chan')
- new_expand_weight: float32 [512, 2048], P('chan')
- new_expand_first: float32 [512, 2048], P('chan')
- new_expand_second: float32 [512, 2048], P('chan')
- new_expand_ema: float32 [512, 2048], P('chan')
- new_inner_norm: float32 [2, 2, 512], P(None, None, 'chan')
- new_inner_first: float32 [2, 2, 512], P(None, None, 'chan')
- new_inner_second: float32 [2, 2, 512], P(None, None, 'chan')
- new_inner_ema: float32 [2, 2, 512], P(None, None, 'chan')
- new_outer_norm: float32 [2, 2048], P(None, 'chan')
- new_outer_first: float32 [2, 2048], P(None, 'chan')
- new_outer_second: float32 [2, 2048], P(None, 'chan')
- new_outer_ema: float32 [2, 2048], P(None, 'chan')
The draws below stay inside these ranges and needn't reach their ends.
Inputs may be any that keep to these rules, and one draw needn't show every extreme that they name: `groups`: group g means a (5 + 2g) x (5 + 2g) image in the top-left corner of its 9 x 9 grid; the first image is of group 0 and the last of group 2. `reduce_moments`: second moments are positive.
All inputs are finite; a program needn't handle non-finite values.
Results may differ from the reference program's by a relative error of at most 0.023.
Values may be sent and summed in bfloat16 or wider, within the bound.
A program may use at most 128 MiB of HBM per device.

```python
import math
import jax
import jax.numpy as jnp
from jax import lax

WIDE = 2048
INNER = 512
MAP = 9
PIX = 81
IMG_DEV = 8
IMAGES = 64
STEP = 5


def moment_pair(key, shape):
    scale = math.sqrt(52.0 * IMAGES)
    first_key, second_key = jax.random.split(key)
    first = scale * jax.random.normal(first_key, shape, jnp.float32)
    second = scale * scale * jnp.exp(jax.random.uniform(second_key, shape, jnp.float32, 0.0, math.log(4.0)))
    return jnp.stack([first, second])


def norm_table(key, shape):
    gain_key, bias_key = jax.random.split(key)
    gains = jax.random.uniform(gain_key, shape, jnp.float32, 0.6, 1.6)
    biases = 0.4 * jax.random.normal(bias_key, shape, jnp.float32)
    return jnp.stack([gains, biases])


def block_offsets(key, lowest, highest):
    sign_key, size_key = jax.random.split(key)
    blocks = IMAGES // IMG_DEV
    signs = jnp.where(jax.random.bernoulli(sign_key, 0.5, (blocks, 1, 1, WIDE)), 1.0, -1.0)
    sizes = jax.random.uniform(size_key, (blocks, 1, 1, WIDE), jnp.float32, lowest, highest)
    return signs * sizes


def offset_field(key, lowest, highest):
    noise_key, offset_key = jax.random.split(key)
    blocks = IMAGES // IMG_DEV
    noise = jax.random.normal(noise_key, (blocks, IMG_DEV, PIX, WIDE), jnp.float32)
    values = noise + block_offsets(offset_key, lowest, highest)
    return jnp.clip(values, -6.0, 6.0).reshape(IMAGES, PIX, WIDE).astype(jnp.bfloat16)


def draw_images(key, part):
    key = jax.random.fold_in(key, 11)
    return offset_field(key, 0.7, 1.3)


def draw_cotangent(key, part):
    key = jax.random.fold_in(key, 12)
    return offset_field(key, 0.4, 0.8)


def draw_groups(key, part):
    key = jax.random.fold_in(key, 1)
    spread = jax.random.randint(key, (IMAGES,), 0, 120)
    place = jnp.arange(IMAGES, dtype=jnp.int32) // IMG_DEV
    last = max(IMAGES // IMG_DEV - 1, 1)
    shifted = spread + 180 * place // last
    chosen = jnp.minimum(shifted // 100, 2)
    index = jnp.arange(IMAGES, dtype=jnp.int32)
    chosen = jnp.where(index == 0, 0, jnp.where(index == IMAGES - 1, 2, chosen))
    return chosen.astype(jnp.int32)


def draw_inner_norm(key, part):
    key = jax.random.fold_in(key, 2)
    return norm_table(key, (2, INNER))


def draw_outer_norm(key, part):
    key = jax.random.fold_in(key, 3)
    return norm_table(key, (WIDE,))


def draw_reduce_moments(key, part):
    key = jax.random.fold_in(key, 4)
    return moment_pair(key, (INNER, WIDE))


def draw_spatial_moments(key, part):
    key = jax.random.fold_in(key, 5)
    return moment_pair(key, (INNER, 3, 3, INNER))


def draw_expand_moments(key, part):
    key = jax.random.fold_in(key, 6)
    return moment_pair(key, (INNER, WIDE))


def draw_inner_moments(key, part):
    key = jax.random.fold_in(key, 7)
    return moment_pair(key, (2, 2, INNER))


def draw_outer_moments(key, part):
    key = jax.random.fold_in(key, 8)
    return moment_pair(key, (2, WIDE))


def draw_inner_ema(key, part):
    key = jax.random.fold_in(key, 9)
    return norm_table(key, (2, INNER))


def draw_outer_ema(key, part):
    key = jax.random.fold_in(key, 10)
    return norm_table(key, (WIDE,))


def block_scale(own_key, dims, cuts, least, top_value):
    loudness = 1.0
    for dim, blocks in cuts:
        steps = jax.random.uniform(jax.random.fold_in(jax.random.fold_in(own_key, 6), dim), (blocks,), jnp.float32, least / len(cuts), top_value / len(cuts))
        loudness = loudness * jnp.repeat(jnp.exp(steps), dims[dim] // blocks).reshape((-1,) + (1,) * (len(dims) - 1 - dim))
    return loudness


def scatter_about(key, dims, scale, bound, cuts=(), held_as=jnp.bfloat16):
    values = jax.random.normal(key, dims, jnp.float32) * scale
    if len(cuts) > 0:
        values = block_scale(key, dims, cuts, -0.22, 0.18) * values
    return jnp.clip(values, min=-bound, max=bound).astype(held_as)


def setup_inputs(seed: int = 0) -> dict:
    keys = jax.random.split(jax.random.key(seed), 19)
    images = draw_images(jax.random.fold_in(keys[18], 71), 0)
    groups = draw_groups(jax.random.fold_in(keys[18], 71), 0)
    cotangent = draw_cotangent(jax.random.fold_in(keys[18], 71), 0)
    reduce_weight = scatter_about(keys[3], (INNER, WIDE), WIDE ** -0.5, 0.125, ((0, 4),), jnp.float32)
    spatial_weight = scatter_about(keys[4], (INNER, 3, 3, INNER), (9 * INNER) ** -0.5, 0.09375, ((0, 4),), jnp.float32)
    expand_weight = scatter_about(keys[5], (INNER, WIDE), INNER ** -0.5, 0.25, ((0, 4),), jnp.float32)
    inner_norm = draw_inner_norm(jax.random.fold_in(keys[18], 71), 0)
    outer_norm = draw_outer_norm(jax.random.fold_in(keys[18], 71), 0)
    reduce_moments = draw_reduce_moments(jax.random.fold_in(keys[18], 71), 0)
    spatial_moments = draw_spatial_moments(jax.random.fold_in(keys[18], 71), 0)
    expand_moments = draw_expand_moments(jax.random.fold_in(keys[18], 71), 0)
    inner_moments = draw_inner_moments(jax.random.fold_in(keys[18], 71), 0)
    outer_moments = draw_outer_moments(jax.random.fold_in(keys[18], 71), 0)
    reduce_ema = scatter_about(keys[13], (INNER, WIDE), WIDE ** -0.5, 0.125, ((0, 4),), jnp.float32)
    spatial_ema = scatter_about(keys[14], (INNER, 3, 3, INNER), (9 * INNER) ** -0.5, 0.09375, ((0, 4),), jnp.float32)
    expand_ema = scatter_about(keys[15], (INNER, WIDE), INNER ** -0.5, 0.25, ((0, 4),), jnp.float32)
    inner_ema = draw_inner_ema(jax.random.fold_in(keys[18], 71), 0)
    outer_ema = draw_outer_ema(jax.random.fold_in(keys[18], 71), 0)
    return {"images": images, "groups": groups, "cotangent": cotangent, "reduce_weight": reduce_weight, "spatial_weight": spatial_weight, "expand_weight": expand_weight, "inner_norm": inner_norm, "outer_norm": outer_norm, "reduce_moments": reduce_moments, "spatial_moments": spatial_moments, "expand_moments": expand_moments, "inner_moments": inner_moments, "outer_moments": outer_moments, "reduce_ema": reduce_ema, "spatial_ema": spatial_ema, "expand_ema": expand_ema, "inner_ema": inner_ema, "outer_ema": outer_ema}


@jax.custom_vjp
def low(v):
    return lax.optimization_barrier(v.astype(jnp.bfloat16)).astype(jnp.float32)

@jax.custom_vjp
def low_back(v):
    return v

def low_keep(v):
    return (low(v), None)

def low_pass(kept, grad):
    return (grad,)

def back_keep(v):
    return (v, None)

def back_low(kept, grad):
    return (low(grad),)
low.defvjp(low_keep, low_pass)
low_back.defvjp(back_keep, back_low)
norm_eps = 1e-05
adam_eps = 1e-08
beta_one = 0.5
beta_two = 0.5
decay_rate = 0.05
ema_rate = 0.75
norm_rate = 0.3

def pixel_mask(groups):
    side = 5 + 2 * groups
    place = jnp.arange(MAP * MAP, dtype=jnp.int32)
    inside = ((place // MAP)[None, :] < side[:, None]) & ((place % MAP)[None, :] < side[:, None])
    return inside.astype(jnp.float32)[:, :, None]

def batch_norm(values, mask, count, gain, bias):
    average = lax.optimization_barrier(jnp.sum(values * mask, axis=(0, 1))) / count
    centered = values - average
    variance = lax.optimization_barrier(jnp.sum(mask * centered * centered, axis=(0, 1))) / count
    return gain * centered * lax.rsqrt(variance + norm_eps) + bias

def unfold(acts):
    count_img = acts.shape[0]
    channels = acts.shape[-1]
    grid = acts.reshape(count_img, MAP, MAP, channels)
    padded = jnp.pad(grid, ((0, 0), (1, 1), (1, 1), (0, 0)))
    pieces = [padded[:, vertical:vertical + MAP, lateral:lateral + MAP, :] for vertical in range(3) for lateral in range(3)]
    return jnp.concatenate(pieces, axis=-1).reshape(count_img, MAP * MAP, 9 * channels)

def adamw(weight, moments, average, grad, rate, decay):
    first = beta_one * moments[0] + (1.0 - beta_one) * grad
    second = beta_two * moments[1] + (1.0 - beta_two) * grad * grad
    corr_one = 1.0 - beta_one ** STEP
    corr_two = 1.0 - beta_two ** STEP
    new_weight = weight - rate * (first / corr_one / (jnp.sqrt(second / corr_two) + adam_eps) + decay * weight)
    new_average = ema_rate * average + (1.0 - ema_rate) * new_weight
    return (new_weight, first, second, new_average)

def reference(images, groups, cotangent, reduce_weight, spatial_weight, expand_weight, inner_norm, outer_norm, reduce_moments, spatial_moments, expand_moments, inner_moments, outer_moments, reduce_ema, spatial_ema, expand_ema, inner_ema, outer_ema):
    highest = lax.Precision.HIGHEST
    mask = pixel_mask(groups)
    count = jnp.sum(mask)

    def forward(inputs, reduce_w, spatial_w, expand_w, inner_p, outer_p):
        first = low_back(jnp.einsum('ipc,kc->ipk', inputs, low(reduce_w), precision=highest))
        first_act = low(jax.nn.silu(batch_norm(first, mask, count, inner_p[0, 0], inner_p[1, 0])) * mask)
        spatial_flat = low(spatial_w).reshape(INNER, 9 * INNER)
        second = low_back(jnp.einsum('ipt,kt->ipk', unfold(first_act), spatial_flat, precision=highest))
        second_act = low(jax.nn.silu(batch_norm(second, mask, count, inner_p[0, 1], inner_p[1, 1])) * mask)
        third = low_back(jnp.einsum('ipk,kw->ipw', second_act, low(expand_w), precision=highest))
        summed = batch_norm(third, mask, count, outer_p[0], outer_p[1]) + inputs
        return jax.nn.silu(summed) * mask
    output, pull = jax.vjp(forward, images.astype(jnp.float32), reduce_weight, spatial_weight, expand_weight, inner_norm, outer_norm)
    grads = pull(cotangent.astype(jnp.float32))
    input_grad = grads[0]
    new_reduce = adamw(reduce_weight, reduce_moments, reduce_ema, grads[1], 2.0 / WIDE ** 0.5, decay_rate)
    new_spatial = adamw(spatial_weight, spatial_moments, spatial_ema, grads[2], 2.0 / (9 * INNER) ** 0.5, decay_rate)
    new_expand = adamw(expand_weight, expand_moments, expand_ema, grads[3], 2.0 / INNER ** 0.5, decay_rate)
    new_inner = adamw(inner_norm, inner_moments, inner_ema, grads[4], norm_rate, 0.0)
    new_outer = adamw(outer_norm, outer_moments, outer_ema, grads[5], norm_rate, 0.0)
    return (output, input_grad, new_reduce[0], new_reduce[1], new_reduce[2], new_reduce[3], new_spatial[0], new_spatial[1], new_spatial[2], new_spatial[3], new_expand[0], new_expand[1], new_expand[2], new_expand[3], new_inner[0], new_inner[1], new_inner[2], new_inner[3], new_outer[0], new_outer[1], new_outer[2], new_outer[3])
```

```python
import functools
import math

import jax
import jax.numpy as jnp
from jax import lax
from jax.experimental import pallas as pl
from jax.experimental.pallas import tpu as pltpu
from jax.sharding import PartitionSpec as P

MESH = pl.DeviceIdType.MESH
MAP = 9
PIX = MAP * MAP
TAPS = 9
PITCH = MAP + 1
STEP = 5
LANES = 128
CHUNK = 48

norm_eps = 1e-05
adam_eps = 1e-08
beta_one = 0.5
beta_two = 0.5
decay_rate = 0.05
ema_rate = 0.75
norm_rate = 0.3

F32 = jnp.float32
BF16 = jnp.bfloat16


def round_up(value, unit):
    return -(-value // unit) * unit


class Sizes:
    def __init__(self, mesh_dp, mesh_chan, images, reduce_weight):
        self.D, self.C = mesh_dp, mesh_chan
        self.Q = self.D // 2
        self.I, _, self.wp = images.shape
        self.ip, self.W = reduce_weight.shape
        self.K = self.ip * self.C
        self.KB = self.K // LANES
        self.WB = self.wp // LANES
        self.R = PIX * self.I
        self.RS = round_up(self.R, 16)
        self.RP = round_up(self.R, CHUNK)
        self.NW = self.WB * self.ip
        self.NS = TAPS * self.KB * self.ip
        self.PW = round_up(-(-self.NW // self.D), 16)
        self.PS = round_up(-(-self.NS // self.D), 16)
        self.PADROWS = ((MAP + 2) * PITCH + 2) * self.I


Z_PHASES = ["w2", "pre1", "act1", "par1", "act2", "par2", "grad2", "dlt2", "par3", "wsp", "zexp", "zred"]
D_PHASES = ["bn1", "bn2", "bn3", "bk3", "bk2", "bk1", "wdp"]
R_PHASES = [g + s for g in ("exp", "spa", "red") for s in ("core", "chip", "back", "pair")]
PHASES = Z_PHASES + D_PHASES + R_PHASES


def nt(a, b):
    return lax.dot_general(a, b, (((1,), (1,)), ((), ())), preferred_element_type=F32)


def nn(a, b):
    return lax.dot_general(a, b, (((1,), (0,)), ((), ())), preferred_element_type=F32)


def tn(a, b):
    return lax.dot_general(a, b, (((0,), (0,)), ((), ())), preferred_element_type=F32)


def sigmoid(v):
    return jax.nn.sigmoid(v)


def scratch_table(sz):
    C, D, Q, ip, wp, K, RP, I = sz.C, sz.D, sz.Q, sz.ip, sz.wp, sz.K, sz.RP, sz.I
    table = [
        ("xi", (I, PIX, wp), BF16),
        ("stage", (sz.WB, I * round_up(PIX, 8), LANES), F32),
        ("omap", (I, PIX, wp), F32),
        ("mask", (RP, LANES), F32),
        ("xb", (RP, wp), BF16),
        ("cotb", (RP, wp), BF16),
        ("w1f", (ip, sz.W), F32),
        ("w2f", (ip, sz.W), F32),
        ("w1s", (C, ip, wp), BF16),
        ("w1r", (C, ip, wp), BF16),
        ("w2s", (C, ip, wp), BF16),
        ("w2r", (C, ip, wp), BF16),
        ("wfull", (C, D * sz.PS, LANES), BF16),
        ("p1s", (C, RP, ip), BF16),
        ("p1r", (C, RP, ip), BF16),
        ("p2s", (C, RP, ip), BF16),
        ("p2r", (C, RP, ip), BF16),
        ("v1", (C, RP, ip), BF16),
        ("v2", (C, RP, ip), BF16),
        ("d2b", (C, RP, ip), BF16),
        ("pm1", (C, 8, ip), F32),
        ("pm2", (C, 8, ip), F32),
        ("pm3", (C, 8, ip), F32),
        ("st1", (D, 8, ip), F32),
        ("st2", (D, 8, ip), F32),
        ("st3", (D, 8, wp), F32),
        ("st4", (D, 8, wp), F32),
        ("st5", (D, 8, ip), F32),
        ("st6", (D, 8, K), F32),
        ("acc", (RP, ip), F32),
        ("pad", (sz.PADROWS, K), F32),
        ("cols", (TAPS, RP, K), BF16),
        ("act2", (RP, K), BF16),
        ("third", (RP, wp), F32),
        ("og", (RP, wp), F32),
        ("wide", (RP, wp), F32),
        ("tg", (RP, wp), BF16),
        ("big", (RP, K), F32),
        ("fag", (RP, K), F32),
        ("sgo", (RP, ip), BF16),
        ("fg", (RP, K), BF16),
    ]
    for name, z, part in (("exp", C, sz.PW), ("spa", 1, sz.PS), ("red", C, sz.PW)):
        table += [
            (name + "_gs", (2, Q, z, part, LANES), BF16),
            (name + "_rb", (Q, z, part, LANES), BF16),
            (name + "_sm", (Q, z, part, LANES), BF16),
            (name + "_rq", (Q, z, part, LANES), BF16),
            (name + "_tot", (z, part, LANES), BF16),
            (name + "_fin", (2, Q, z, part, LANES), BF16),
        ]
    return table


N_INPUTS, N_OUTPUTS = 8, 6


def block_kernel(sz, *refs):
    groups, images, cotangent, reduce_w, spatial_w, expand_w, inner_norm, outer_norm = refs[:8]
    out_hbm, ing_hbm, exp_hbm, spa_hbm, red_hbm, small_out = refs[8:14]
    table = scratch_table(sz)
    v = {name: ref for (name, _, _), ref in zip(table, refs[14:])}
    lsem, w1ssem, w1rsem, ssem, rsem = refs[14 + len(table) :]
    D, C, Q, I, K, KB, WB = sz.D, sz.C, sz.Q, sz.I, sz.K, sz.KB, sz.WB
    ip, wp, R, RS, RP = sz.ip, sz.wp, sz.R, sz.RS, sz.RP
    d = lax.axis_index("dp")
    c = lax.axis_index("chan")
    q = lax.div(d, 2)
    h = lax.rem(d, 2)
    zpeers = [lax.rem(c + k, C) for k in range(1, C)]
    dpeers = [lax.rem(d + k, D) for k in range(1, D)]
    qpeers = [lax.rem(q + k, Q) for k in range(1, Q)]
    sibling = d + 1 - 2 * h
    sem_of = {name: i for i, name in enumerate(PHASES)}
    sent = []

    def send(name, src, dst, device):
        pltpu.make_async_remote_copy(
            src_ref=src, dst_ref=dst, send_sem=ssem.at[sem_of[name]], recv_sem=rsem.at[sem_of[name]],
            device_id=device, device_id_type=MESH,
        ).start()

    def wait_bytes(ref, sem):
        pltpu.make_async_copy(ref, ref, sem).wait()

    def got(name, ref):
        wait_bytes(ref, rsem.at[sem_of[name]])
        sent.append((name, ref))

    barrier = pltpu.get_barrier_semaphore()
    for j in zpeers:
        pl.semaphore_signal(barrier, inc=1, device_id=(d, j), device_id_type=MESH)
    for e in dpeers:
        pl.semaphore_signal(barrier, inc=1, device_id=(e, c), device_id_type=MESH)

    xi, stage, omap, mask, xb, cotb = v["xi"], v["stage"], v["omap"], v["mask"], v["xb"], v["cotb"]
    w1f, w1s, w1r, w2f, w2s, w2r, wfull = (v[n] for n in ("w1f", "w1s", "w1r", "w2f", "w2s", "w2r", "wfull"))
    loads = [
        pltpu.make_async_copy(reduce_w, w1f, lsem.at[0]),
        pltpu.make_async_copy(images, xi, lsem.at[1]),
        pltpu.make_async_copy(expand_w, w2f, lsem.at[2]),
        pltpu.make_async_copy(spatial_w, wfull.at[c, pl.ds(0, sz.NS)], lsem.at[3]),
    ]
    for load in loads:
        load.start()

    def columns_of(ref, j):
        return ref[:, pl.ds(pl.multiple_of(j * wp, wp), wp)].astype(BF16)

    loads[0].wait()
    for j in zpeers:
        w1s[j] = columns_of(w1f, j)
    w1r[c] = columns_of(w1f, c)
    pl.semaphore_wait(barrier, C - 1 + D - 1)
    w1_copies = []
    for k, j in enumerate(zpeers):
        w1_copies.append(
            pltpu.make_async_remote_copy(
                src_ref=w1s.at[j], dst_ref=w1r.at[c], send_sem=w1ssem.at[k], recv_sem=w1rsem.at[k],
                device_id=(d, j), device_id_type=MESH,
            )
        )
        w1_copies[-1].start()

    row = lax.broadcasted_iota(jnp.int32, (I, LANES), 0)
    side = jnp.zeros((I, LANES), jnp.int32)
    for i in range(I):
        side = jnp.where(row == i, 5 + 2 * groups[i], side)
    cells_here = jnp.zeros((I, LANES), F32)
    for p in range(PIX):
        inside = (side > max(p // MAP, p % MAP)).astype(F32)
        mask[p * I : (p + 1) * I, :] = inside
        cells_here = cells_here + inside
    mask[R:RP, :] = jnp.zeros((RP - R, LANES), F32)
    count_here = jnp.sum(cells_here, axis=0, keepdims=True)
    img_rows = round_up(PIX, 8)

    def by_cell(src, dst):
        for i in range(I):
            values = src[i].astype(F32)
            for l in range(WB):
                stage[l, i * img_rows : i * img_rows + PIX, :] = values[:, l * LANES : (l + 1) * LANES]

        def pair(s, carry):
            for l in range(WB):
                both = [stage[l, pl.ds(2 * s + e, I, stride=img_rows), :] for e in range(2)]
                dst[pl.ds(pl.multiple_of(s * 2 * I, 2 * I), 2 * I), l * LANES : (l + 1) * LANES] = (
                    jnp.concatenate(both, axis=0).astype(BF16)
                )
            return carry

        lax.fori_loop(0, PIX // 2, pair, 0)
        for l in range(WB):
            last = stage[l, pl.ds(PIX - 1, I, stride=img_rows), :]
            rest = jnp.zeros((RP - R, LANES), F32)
            dst[R - I : RP, l * LANES : (l + 1) * LANES] = jnp.concatenate([last, rest], axis=0).astype(BF16)

    def by_image(src, dst):
        def cell(p, carry):
            for l in range(WB):
                stage[l, pl.ds(p, I, stride=img_rows), :] = src[
                    pl.ds(pl.multiple_of(p * I, I), I), l * LANES : (l + 1) * LANES
                ]
            return carry

        lax.fori_loop(0, PIX, cell, 0)
        for i in range(I):
            for l in range(WB):
                dst[i, :, l * LANES : (l + 1) * LANES] = stage[l, i * img_rows : i * img_rows + PIX, :]

    def lanes(values, width):
        if width <= LANES:
            return values[:, :width]
        return jnp.concatenate([values] * (width // LANES), axis=1)

    def mask_of(rows, width):
        return lanes(mask[rows, :], width)

    def over_chunks(body, carry=0):
        def step(s, carry):
            return body(pl.ds(pl.multiple_of(s * CHUNK, CHUNK), CHUNK), carry)

        return lax.fori_loop(0, RP // CHUNK, step, carry)

    def each_chunk(body):
        def step(rows, carry):
            body(rows)
            return carry

        over_chunks(step)

    def fold_rows(values):
        total = values[0:8]
        for s in range(1, values.shape[0] // 8):
            total = total + values[8 * s : 8 * s + 8]
        return total

    def total_of(values):
        return jnp.sum(values, axis=0, keepdims=True)

    def rows_of(*values):
        rest = jnp.zeros((8 - len(values), values[0].shape[1]), F32)
        return jnp.concatenate(list(values) + [rest], axis=0)

    loads[1].wait()
    by_cell(xi, xb)
    load_cot = pltpu.make_async_copy(cotangent, xi, lsem.at[4])
    load_cot.start()

    acc, p1s, p1r = v["acc"], v["p1s"], v["p1r"]
    for k in range(1, C):
        j = lax.rem(c - k + C, C)
        w1_copies[k - 1].wait_recv()
        p1s[j] = nt(xb[...], w1r[j]).astype(BF16)
        send("pre1", p1s.at[j, pl.ds(0, RS)], p1r.at[c, pl.ds(0, RS)], (d, j))
    acc[...] = nt(xb[...], w1r[c])
    loads[2].wait()
    for j in zpeers:
        w2s[j] = columns_of(w2f, j)
    w2r[c] = columns_of(w2f, c)
    for j in zpeers:
        send("w2", w2s.at[j], w2r.at[c], (d, j))
    load_cot.wait()
    by_cell(xi, cotb)
    loads[3].wait()

    def add_partials(name, recv):
        got(name, recv.at[pl.ds(0, C - 1), pl.ds(0, RS)])
        for j in zpeers:
            acc[0:RS, :] += recv[j, 0:RS, :].astype(F32)

    add_partials("pre1", p1r)

    def moments(src, width):
        def sums(rows, carry):
            return carry + fold_rows(src[rows, :] * mask_of(rows, width))

        mean = total_of(over_chunks(sums, jnp.zeros((8, width), F32))) / lanes(count_here, width)

        def squares(rows, carry):
            centered = src[rows, :] - mean
            return carry + fold_rows(mask_of(rows, width) * centered * centered)

        return mean, total_of(over_chunks(squares, jnp.zeros((8, width), F32)))

    def exchange_dp(name, table):
        for e in dpeers:
            send(name, table.at[d], table.at[d], (e, c))

    def combine(name, table):
        got(name, table.at[pl.ds(0, D - 1)])
        count = table[0, 2:3, :]
        average = count * table[0, 0:1, :]
        for e in range(1, D):
            count = count + table[e, 2:3, :]
            average = average + table[e, 2:3, :] * table[e, 0:1, :]
        average = average / count
        variance = jnp.zeros_like(average)
        for e in range(D):
            off = table[e, 0:1, :] - average
            variance = variance + (table[e, 1:2, :] + table[e, 2:3, :] * off * off)
        return average, lax.rsqrt(variance / count + norm_eps), count

    def sum_dp(name, table):
        got(name, table.at[pl.ds(0, D - 1)])
        total = table[0]
        for e in range(1, D):
            total = total + table[e]
        return total[0:1, :], total[1:2, :]

    def send_z(name, ref, rows=None):
        part = ref.at[c] if rows is None else ref.at[c, pl.ds(0, rows)]
        for j in zpeers:
            send(name, part, part, (d, j))

    def got_z(name, ref, rows=None):
        got(name, ref.at[pl.ds(0, C - 1)] if rows is None else ref.at[pl.ds(0, C - 1), pl.ds(0, rows)])

    def inner_forward(layer, bn, table, held, held_name, par, par_name):
        mean, spread = moments(acc, ip)
        table[d] = rows_of(mean, spread, lanes(count_here, ip))
        exchange_dp(bn, table)

        def center(rows):
            held[c, rows, :] = ((acc[rows, :] - mean) * mask_of(rows, ip)).astype(BF16)

        each_chunk(center)
        send_z(held_name, held, RS)
        average, inverse, count = combine(bn, table)
        par[c] = rows_of(
            inverse, (mean - average) * inverse,
            inner_norm[0, layer : layer + 1, :], inner_norm[1, layer : layer + 1, :],
        )
        send_z(par_name, par)
        got_z(held_name, held, RS)
        got_z(par_name, par)
        return count

    def joined(blocks, rows):
        return jnp.concatenate([blocks[j, rows, :].astype(F32) for j in range(C)], axis=1)

    def table_row(par, r):
        return jnp.concatenate([par[j, r : r + 1, :] for j in range(C)], axis=1)

    v1, v2, d2b, pm1, pm2, pm3 = (v[n] for n in ("v1", "v2", "d2b", "pm1", "pm2", "pm3"))
    for j in range(C):
        for ref in (v1, v2, d2b):
            ref[j, RS:RP, :] = jnp.zeros((RP - RS, ip), BF16)
    count_ip = inner_forward(0, "bn1", v["st1"], v1, "act1", pm1, "par1")

    def make_act(held, par, dst):
        inverse, shift, gain, bias = (table_row(par, r) for r in range(4))

        def step(rows):
            value = gain * (joined(held, rows) * inverse + shift) + bias
            dst[rows, :] = (value * sigmoid(value) * mask_of(rows, K)).astype(dst.dtype)

        each_chunk(step)

    big, pad, cols = v["big"], v["pad"], v["cols"]
    pad[...] = jnp.zeros_like(pad)
    make_act(v1, pm1, big)

    def fill_pad():
        for y in range(MAP):
            start = ((y + 1) * PITCH + 1) * I
            pad[start : start + MAP * I, :] = big[y * MAP * I : (y + 1) * MAP * I, :]

    def shifted(offset):
        pieces = [pad[pl.ds(pl.multiple_of(offset + y * PITCH * I, I), MAP * I), :] for y in range(MAP)]
        pieces.append(jnp.zeros((RP - R, K), F32))
        return jnp.concatenate(pieces, axis=0).astype(BF16)

    def weight_of(j, tap):
        pieces = [wfull[j, pl.ds(pl.multiple_of((tap * KB + kb) * ip, ip), ip), :] for kb in range(KB)]
        return jnp.concatenate(pieces, axis=1)

    fill_pad()
    acc[...] = jnp.zeros_like(acc)

    def second_step(tap, carry):
        cols[tap] = shifted((lax.div(tap, 3) * PITCH + lax.rem(tap, 3)) * I)
        acc[...] += nt(cols[tap], weight_of(c, tap))
        return carry

    lax.fori_loop(0, TAPS, second_step, 0)
    inner_forward(1, "bn2", v["st2"], v2, "act2", pm2, "par2")

    def part_of(j, e):
        return wfull.at[j, pl.ds(pl.multiple_of(e * sz.PS, 16), sz.PS)]

    for j in zpeers:
        send("wsp", part_of(c, d), part_of(c, d), (d, j))
    act2 = v["act2"]
    make_act(v2, pm2, act2)

    third, og, wide, tg = v["third"], v["og"], v["wide"], v["tg"]
    got_z("w2", w2r)
    third[...] = nn(act2[...], w2r[...].reshape(K, wp))
    mean3, spread3 = moments(third, wp)
    st3, st4, st5, st6 = v["st3"], v["st4"], v["st5"], v["st6"]
    st3[d] = rows_of(mean3, spread3, lanes(count_here, wp))
    exchange_dp("bn3", st3)
    average3, inverse3, count_wp = combine("bn3", st3)
    gain3, bias3 = outer_norm[0:1, :], outer_norm[1:2, :]

    def last_step(rows, carry):
        m = mask_of(rows, wp)
        normed = (third[rows, :] - average3) * inverse3
        third[rows, :] = normed
        summed = gain3 * normed + bias3 + xb[rows, :].astype(F32)
        s = sigmoid(summed)
        wide[rows, :] = summed * s * m
        grad = cotb[rows, :].astype(F32) * (s * (1.0 + summed * (1.0 - s))) * m
        og[rows, :] = grad
        return carry[0] + fold_rows(grad), carry[1] + fold_rows(grad * normed)

    zero_wp = jnp.zeros((8, wp), F32)
    sums = over_chunks(last_step, (zero_wp, zero_wp))
    st4[d] = rows_of(total_of(sums[0]), total_of(sums[1]))
    exchange_dp("bk3", st4)
    by_image(wide, omap)
    store_out = pltpu.make_async_copy(omap, out_hbm, lsem.at[5])
    store_out.start()
    bias_grad3, gain_grad3 = sum_dp("bk3", st4)
    scale3 = inverse3 * gain3

    def third_step(rows):
        back = mask_of(rows, wp) * ((bias_grad3 + third[rows, :] * gain_grad3) / count_wp)
        tg[rows, :] = (scale3 * (og[rows, :] - back)).astype(BF16)

    each_chunk(third_step)

    p2s, p2r = v["p2s"], v["p2r"]
    for k in range(1, C):
        j = lax.rem(c - k + C, C)
        p2s[j] = nt(tg[...], w2r[j]).astype(BF16)
        send("grad2", p2s.at[j, pl.ds(0, RS)], p2r.at[c, pl.ds(0, RS)], (d, j))
    acc[...] = nt(tg[...], w2r[c])

    class Reduction:
        def __init__(self, name, z, part):
            self.name, self.z, self.part = name, z, part
            self.gs, self.rb, self.sm, self.rq, self.tot, self.fin = (
                v[name + "_" + s] for s in ("gs", "rb", "sm", "rq", "tot", "fin")
            )

        def put(self, zi, block, value):
            row, end = block * ip, (block + 1) * ip
            while row < end:
                owner = row // self.part
                stop = min(end, (owner + 1) * self.part)
                at = row - owner * self.part
                self.gs[owner % 2, owner // 2, zi, at : at + stop - row, :] = value[
                    row - block * ip : stop - block * ip, :
                ]
                row = stop

        def pair(self):
            send(self.name + "core", self.gs.at[1 - h], self.rb, (sibling, c))

        def chips(self):
            got(self.name + "core", self.rb)
            for e in range(Q):
                self.sm[e] = (self.gs[h, e].astype(F32) + self.rb[e].astype(F32)).astype(BF16)
            for e in qpeers:
                send(self.name + "chip", self.sm.at[e], self.rq.at[q], (2 * e + h, c))

        def chan(self):
            got(self.name + "chip", self.rq.at[pl.ds(0, Q - 1)])
            total = self.sm[q].astype(F32)
            for e in qpeers:
                total = total + self.rq[e].astype(F32)
            self.tot[...] = total.astype(BF16)
            if self.z == 1:
                self.fin[h, q, 0] = self.tot[0]
            else:
                self.fin[h, q, c] = self.tot[c]
                for j in zpeers:
                    send("z" + self.name, self.tot.at[j], self.fin.at[h, q, c], (d, j))

        def back(self):
            if self.z > 1:
                got("z" + self.name, self.fin.at[h, q, pl.ds(0, C - 1)])
            for e in qpeers:
                send(self.name + "back", self.fin.at[h, q], self.fin.at[h, q], (2 * e + h, c))

        def other(self):
            got(self.name + "back", self.fin.at[h, pl.ds(0, Q - 1)])
            send(self.name + "pair", self.fin.at[h], self.fin.at[h], (sibling, c))

        def done(self):
            got(self.name + "pair", self.fin.at[0])

    exp_red = Reduction("exp", C, sz.PW)
    spa_red = Reduction("spa", 1, sz.PS)
    red_red = Reduction("red", C, sz.PW)
    for j in range(C):
        block = tn(act2[:, j * ip : (j + 1) * ip], tg[...]).astype(BF16)
        for wb in range(WB):
            exp_red.put(j, wb, block[:, wb * LANES : (wb + 1) * LANES])
    exp_red.pair()

    add_partials("grad2", p2r)
    inverse_own, shift_own, gain_own, bias_own = (pm2[c, r : r + 1, :] for r in range(4))

    def second_back(rows, carry):
        normed = v2[c, rows, :].astype(F32) * inverse_own + shift_own
        value = gain_own * normed + bias_own
        s = sigmoid(value)
        grad = acc[rows, :] * (s * (1.0 + value * (1.0 - s))) * mask_of(rows, ip)
        d2b[c, rows, :] = grad.astype(BF16)
        return carry[0] + fold_rows(grad), carry[1] + fold_rows(grad * normed)

    zero_ip = jnp.zeros((8, ip), F32)
    sums = over_chunks(second_back, (zero_ip, zero_ip))
    st5[d] = rows_of(total_of(sums[0]), total_of(sums[1]))
    exchange_dp("bk2", st5)
    send_z("dlt2", d2b, RS)
    exp_red.chips()
    got("wsp", wfull.at[pl.ds(0, C - 1), pl.ds(0, sz.PS)])
    for j in zpeers:
        for e in dpeers:
            send("wdp", part_of(j, d), part_of(j, d), (e, c))
    bias_grad2, gain_grad2 = sum_dp("bk2", st5)
    pm3[c] = rows_of(bias_grad2 / count_ip, gain_grad2 / count_ip)
    send_z("par3", pm3)
    sgo = v["sgo"]

    def own_second(rows):
        normed = v2[c, rows, :].astype(F32) * inverse_own + shift_own
        back = mask_of(rows, ip) * (pm3[c, 0:1, :] + normed * pm3[c, 1:2, :])
        sgo[rows, :] = (inverse_own * gain_own * (d2b[c, rows, :].astype(F32) - back)).astype(BF16)

    each_chunk(own_second)
    for tap in range(TAPS):
        block = tn(sgo[...], cols[tap]).astype(BF16)
        for kb in range(KB):
            spa_red.put(0, tap * KB + kb, block[:, kb * LANES : (kb + 1) * LANES])
    exp_red.chan()
    spa_red.pair()
    got_z("dlt2", d2b, RS)
    got_z("par3", pm3)
    inverse2, shift2, gain2 = (table_row(pm2, r) for r in range(3))
    bias_part, gain_part = table_row(pm3, 0), table_row(pm3, 1)
    scale2 = inverse2 * gain2

    def full_second(rows):
        normed = joined(v2, rows) * inverse2 + shift2
        back = mask_of(rows, K) * (bias_part + normed * gain_part)
        big[rows, :] = (scale2 * (joined(d2b, rows) - back)).astype(BF16).astype(F32)

    each_chunk(full_second)
    fill_pad()
    spa_red.chips()
    exp_red.back()
    got("wdp", wfull.at[pl.ds(0, C - 1), pl.ds(0, (D - 1) * sz.PS)])

    fag = v["fag"]
    fag[...] = jnp.zeros_like(fag)

    def first_act_step(tap, carry):
        offset = ((2 - lax.div(tap, 3)) * PITCH + 2 - lax.rem(tap, 3)) * I
        weight = jnp.concatenate([weight_of(j, tap) for j in range(C)], axis=0)
        fag[...] += nn(shifted(offset), weight)
        return carry

    lax.fori_loop(0, TAPS, first_act_step, 0)
    inverse1, shift1, gain1, bias1 = (table_row(pm1, r) for r in range(4))

    def first_back(rows, carry):
        normed = joined(v1, rows) * inverse1 + shift1
        value = gain1 * normed + bias1
        s = sigmoid(value)
        grad = fag[rows, :] * (s * (1.0 + value * (1.0 - s))) * mask_of(rows, K)
        fag[rows, :] = grad
        big[rows, :] = normed
        return carry[0] + fold_rows(grad), carry[1] + fold_rows(grad * normed)

    zero_k = jnp.zeros((8, K), F32)
    sums = over_chunks(first_back, (zero_k, zero_k))
    st6[d] = rows_of(total_of(sums[0]), total_of(sums[1]))
    exchange_dp("bk1", st6)
    spa_red.chan()
    spa_red.back()
    exp_red.other()
    bias_grad1, gain_grad1 = sum_dp("bk1", st6)
    scale1 = inverse1 * gain1
    count_k = lanes(count_ip[:, 0:1] + jnp.zeros((1, LANES), F32), K)
    fg = v["fg"]

    def first_step(rows):
        back = mask_of(rows, K) * ((bias_grad1 + big[rows, :] * gain_grad1) / count_k)
        fg[rows, :] = (scale1 * (fag[rows, :] - back)).astype(BF16)

    each_chunk(first_step)
    for j in range(C):
        block = tn(fg[:, j * ip : (j + 1) * ip], xb[...]).astype(BF16)
        for wb in range(WB):
            red_red.put(j, wb, block[:, wb * LANES : (wb + 1) * LANES])
    red_red.pair()
    wide[...] = nn(fg[...], w1r[...].reshape(K, wp)) + og[...]
    red_red.chips()
    spa_red.other()
    exp_red.done()
    store_out.wait()
    by_image(wide, omap)
    store_in = pltpu.make_async_copy(omap, ing_hbm, lsem.at[6])
    store_in.start()
    red_red.chan()
    red_red.back()
    store_exp = pltpu.make_async_copy(exp_red.fin, exp_hbm, lsem.at[7])
    store_exp.start()
    spa_red.done()
    store_spa = pltpu.make_async_copy(spa_red.fin, spa_hbm, lsem.at[8])
    store_spa.start()
    small_out[...] = jnp.zeros_like(small_out)
    small_out[0:1, 0:K] = gain_grad1
    small_out[1:2, 0:K] = bias_grad1
    small_out[2:3, 0:ip] = gain_grad2
    small_out[3:4, 0:ip] = bias_grad2
    small_out[4:5, 0:wp] = gain_grad3
    small_out[5:6, 0:wp] = bias_grad3
    red_red.other()
    red_red.done()
    store_red = pltpu.make_async_copy(red_red.fin, red_hbm, lsem.at[9])
    store_red.start()
    for copy in (store_in, store_exp, store_spa, store_red):
        copy.wait()
    for copy in w1_copies:
        copy.wait_send()
    for name, ref in sent:
        wait_bytes(ref, ssem.at[sem_of[name]])


def adamw(weight, moments, average, grad, rate, decay):
    first = beta_one * moments[0] + (1.0 - beta_one) * grad
    second = beta_two * moments[1] + (1.0 - beta_two) * grad * grad
    corr_one = 1.0 - beta_one**STEP
    corr_two = 1.0 - beta_two**STEP
    new_weight = weight - rate * (
        first / corr_one / (jnp.sqrt(second / corr_two) + adam_eps) + decay * weight
    )
    new_average = ema_rate * average + (1.0 - ema_rate) * new_weight
    return (new_weight, first, second, new_average)


def per_device(
    mesh_dp, mesh_chan,
    images, groups, cotangent, reduce_weight, spatial_weight, expand_weight, inner_norm, outer_norm,
    reduce_moments, spatial_moments, expand_moments, inner_moments, outer_moments,
    reduce_ema, spatial_ema, expand_ema, inner_ema, outer_ema,
):
    sz = Sizes(mesh_dp, mesh_chan, images, reduce_weight)
    ip, K, D = sz.ip, sz.K, sz.D
    spatial_low = (
        spatial_weight.reshape(ip, TAPS * sz.KB, LANES).transpose(1, 0, 2).reshape(sz.NS, LANES).astype(BF16)
    )
    wide_row = max(K, sz.wp)
    any_spec, vmem_spec = pl.BlockSpec(memory_space=pl.ANY), pl.BlockSpec(memory_space=pltpu.VMEM)
    output, input_grad, exp_sum, spa_sum, red_sum, small = pl.pallas_call(
        functools.partial(block_kernel, sz),
        out_shape=(
            jax.ShapeDtypeStruct(images.shape, F32),
            jax.ShapeDtypeStruct(images.shape, F32),
            jax.ShapeDtypeStruct((2, sz.Q, sz.C, sz.PW, LANES), BF16),
            jax.ShapeDtypeStruct((2, sz.Q, 1, sz.PS, LANES), BF16),
            jax.ShapeDtypeStruct((2, sz.Q, sz.C, sz.PW, LANES), BF16),
            jax.ShapeDtypeStruct((8, wide_row), F32),
        ),
        in_specs=[pl.BlockSpec(memory_space=pltpu.SMEM)] + [any_spec] * 5 + [vmem_spec] * 2,
        out_specs=(any_spec,) * 5 + (vmem_spec,),
        scratch_shapes=[pltpu.VMEM(shape, dtype) for _, shape, dtype in scratch_table(sz)]
        + [
            pltpu.SemaphoreType.DMA((10,)),
            pltpu.SemaphoreType.DMA((sz.C - 1,)),
            pltpu.SemaphoreType.DMA((sz.C - 1,)),
            pltpu.SemaphoreType.DMA((len(PHASES),)),
            pltpu.SemaphoreType.DMA((len(PHASES),)),
        ],
        compiler_params=pltpu.CompilerParams(
            collective_id=0, has_side_effects=True, vmem_limit_bytes=60 * 2**20
        ),
    )(groups, images, cotangent, reduce_weight, spatial_low, expand_weight, inner_norm, outer_norm)

    def whole(parts, z, n, cols):
        rows = parts.transpose(2, 1, 0, 3, 4).reshape(z, -1, LANES)[:, :n]
        rows = rows.reshape(z * n // ip, ip, LANES).transpose(1, 0, 2)
        return rows.reshape(ip, cols).astype(F32)

    exp_grad = whole(exp_sum, sz.C, sz.NW, sz.W)
    red_grad = whole(red_sum, sz.C, sz.NW, sz.W)
    spa_grad = whole(spa_sum, 1, sz.NS, TAPS * K).reshape(spatial_weight.shape)
    own = lax.axis_index("chan") * ip
    first_rows = lax.dynamic_slice(small[0:2, :K], (0, own), (2, ip))
    inner_grad = jnp.stack(
        [jnp.stack([first_rows[0], small[2, :ip]]), jnp.stack([first_rows[1], small[3, :ip]])]
    )
    outer_grad = small[4:6, : sz.wp]
    new_reduce = adamw(reduce_weight, reduce_moments, reduce_ema, red_grad, 2.0 / math.sqrt(sz.W), decay_rate)
    new_spatial = adamw(
        spatial_weight, spatial_moments, spatial_ema, spa_grad, 2.0 / math.sqrt(TAPS * K), decay_rate
    )
    new_expand = adamw(expand_weight, expand_moments, expand_ema, exp_grad, 2.0 / math.sqrt(K), decay_rate)
    new_inner = adamw(inner_norm, inner_moments, inner_ema, inner_grad, norm_rate, 0.0)
    new_outer = adamw(outer_norm, outer_moments, outer_ema, outer_grad, norm_rate, 0.0)
    return (output, input_grad, *new_reduce, *new_spatial, *new_expand, *new_inner, *new_outer)


def solution(mesh):
    placed = (
        P("dp", None, "chan"),
        P("dp"),
        P("dp", None, "chan"),
        P("chan", None),
        P("chan", None, None, None),
        P("chan", None),
        P(None, None, "chan"),
        P(None, "chan"),
        P(None, "chan", None),
        P(None, "chan", None, None, None),
        P(None, "chan", None),
        P(None, None, None, "chan"),
        P(None, None, "chan"),
        P("chan", None),
        P("chan", None, None, None),
        P("chan", None),
        P(None, None, "chan"),
        P(None, "chan"),
    )
    return jax.shard_map(
        functools.partial(per_device, mesh.shape["dp"], mesh.shape["chan"]),
        mesh=mesh,
        in_specs=placed,
        out_specs=(P("dp", None, "chan"),) * 2
        + (P("chan", None),) * 4
        + (P("chan", None, None, None),) * 4
        + (P("chan", None),) * 4
        + (P(None, None, "chan"),) * 4
        + (P(None, "chan"),) * 4,
        check_vma=False,
    )
```

```python
import functools
import math

import jax
import jax.numpy as jnp
from jax import lax
from jax.experimental import pallas as pl
from jax.experimental.pallas import tpu as pltpu
from jax.sharding import PartitionSpec as P

MESH = pl.DeviceIdType.MESH
MAP = 9
PIX = MAP * MAP
TAPS = 9
PITCH = MAP + 1
STEP = 5
LANES = 128
CHUNK = 48
VMEM_TOTAL = 62 * 2**20

norm_eps = 1e-05
adam_eps = 1e-08
beta_one = 0.5
beta_two = 0.5
decay_rate = 0.05
ema_rate = 0.75
norm_rate = 0.3

F32 = jnp.float32
BF16 = jnp.bfloat16


def round_up(value, unit):
    return -(-value // unit) * unit


class Sizes:
    def __init__(self, mesh_dp, mesh_chan, images, reduce_weight):
        self.D, self.C = mesh_dp, mesh_chan
        self.Q = self.D // 2
        self.I, _, self.wp = images.shape
        self.ip, self.W = reduce_weight.shape
        self.K = self.ip * self.C
        self.KB = self.K // LANES
        self.WB = self.wp // LANES
        self.R = PIX * self.I
        self.RS = round_up(self.R, 16)
        self.RP = round_up(self.R, CHUNK)
        self.NS = TAPS * self.ip
        self.PW = round_up(-(-self.ip // self.D), 16)
        self.PS = round_up(-(-self.NS // self.D), 16)
        self.PADROWS = ((MAP + 2) * PITCH + 2) * self.I


Z_PHASES = ["w2", "pre1", "act1", "par1", "act2", "par2", "grad2", "dlt2", "par3", "wsp", "zexp", "zred"]
D_PHASES = ["bn1", "bn2", "bn3", "bk3", "bk2", "bk1", "wdp"]
R_PHASES = [g + s for g in ("exp", "spa", "red") for s in ("core", "chip", "back", "pair")]
PHASES = Z_PHASES + D_PHASES + R_PHASES


def nt(a, b):
    return lax.dot_general(a, b, (((1,), (1,)), ((), ())), preferred_element_type=F32)


def nn(a, b):
    return lax.dot_general(a, b, (((1,), (0,)), ((), ())), preferred_element_type=F32)


def tn(a, b):
    return lax.dot_general(a, b, (((0,), (0,)), ((), ())), preferred_element_type=F32)


def sigmoid(v):
    return jax.nn.sigmoid(v)


def vmem_bytes(shape, dtype):
    *lead, rows, width = shape
    return math.prod(lead) * round_up(rows, 8) * round_up(width, LANES) * jnp.dtype(dtype).itemsize


def scratch_table(sz):
    C, D, Q, ip, wp, K, RP, I = sz.C, sz.D, sz.Q, sz.ip, sz.wp, sz.K, sz.RP, sz.I
    table = [
        ("xi", (sz.R, wp), BF16),
        ("coti", (sz.R, wp), BF16),
        ("mask", (RP, LANES), F32),
        ("xb", (RP, wp), BF16),
        ("cotb", (RP, wp), BF16),
        ("w1s", (C, ip, wp), BF16),
        ("w1r", (C, ip, wp), BF16),
        ("w2s", (C, ip, wp), BF16),
        ("w2r", (C, ip, wp), BF16),
        ("wfull", (C, D * sz.PS, K), BF16),
        ("p1s", (C, RP, ip), BF16),
        ("p1r", (C, RP, ip), BF16),
        ("p2r", (C, RP, ip), BF16),
        ("v1", (C, RP, ip), BF16),
        ("v2", (C, RP, ip), BF16),
        ("d2b", (C, RP, ip), BF16),
        ("pm1", (C, 8, ip), F32),
        ("pm2", (C, 8, ip), F32),
        ("pm3", (C, 8, ip), F32),
        ("own", (C, 8, ip), F32),
        ("st1", (D, 8, ip), F32),
        ("st2", (D, 8, ip), F32),
        ("st3", (D, 8, wp), F32),
        ("st4", (D, 8, wp), F32),
        ("st5", (D, 8, ip), F32),
        ("st6", (D, 8, K), F32),
        ("acc", (RP, ip), F32),
        ("pad", (sz.PADROWS, K), F32),
        ("cols", (TAPS, RP, K), BF16),
        ("act2", (RP, K), BF16),
        ("third", (RP, wp), F32),
        ("og", (RP, wp), F32),
        ("tg", (RP, wp), BF16),
        ("big", (RP, K), F32),
        ("fag", (RP, K), F32),
        ("sgo", (RP, ip), BF16),
        ("fg", (RP, K), BF16),
    ]
    for name, z, part, width in (("exp", C, sz.PW, wp), ("spa", 1, sz.PS, K), ("red", C, sz.PW, wp)):
        table += [
            (name + "_gs", (2, Q, z, part, width), BF16),
            (name + "_rb", (Q, z, part, width), BF16),
            (name + "_sm", (Q, z, part, width), BF16),
            (name + "_rq", (Q, z, part, width), BF16),
            (name + "_tot", (z, part, width), BF16),
            (name + "_fin", (2, Q, z, part, width), BF16),
        ]
    return table


def block_kernel(sz, *refs):
    groups, images, cotangent, inner_norm, outer_norm, inner_moments, outer_moments, inner_ema, outer_ema = refs[:9]
    states_hbm = [refs[9:12], refs[12:15], refs[15:18]]
    output, input_grad, red_state, spa_state, exp_state, inner_state, outer_state = refs[18:25]
    table = scratch_table(sz)
    v = {name: ref for (name, _, _), ref in zip(table, refs[25:])}
    lsem, stsem, w1ssem, w1rsem, ssem, rsem = refs[25 + len(table) :]
    D, C, Q, I, K, KB, WB = sz.D, sz.C, sz.Q, sz.I, sz.K, sz.KB, sz.WB
    ip, wp, R, RS, RP = sz.ip, sz.wp, sz.R, sz.RS, sz.RP
    d = lax.axis_index("dp")
    c = lax.axis_index("chan")
    q = lax.div(d, 2)
    h = lax.rem(d, 2)
    zpeers = [lax.rem(c + k, C) for k in range(1, C)]
    dpeers = [lax.rem(d + k, D) for k in range(1, D)]
    qpeers = [lax.rem(q + k, Q) for k in range(1, Q)]
    sibling = d + 1 - 2 * h
    sem_of = {name: i for i, name in enumerate(PHASES)}
    sent = []

    def send(name, src, dst, device):
        pltpu.make_async_remote_copy(
            src_ref=src, dst_ref=dst, send_sem=ssem.at[sem_of[name]], recv_sem=rsem.at[sem_of[name]],
            device_id=device, device_id_type=MESH,
        ).start()

    def wait_bytes(ref, sem):
        pltpu.make_async_copy(ref, ref, sem).wait()

    def got(name, ref):
        wait_bytes(ref, rsem.at[sem_of[name]])
        sent.append((name, ref))

    def sent_done(name):
        for entry in [e for e in sent if e[0] == name]:
            wait_bytes(entry[1], ssem.at[sem_of[name]])
            sent.remove(entry)

    barrier = pltpu.get_barrier_semaphore()
    for j in zpeers:
        pl.semaphore_signal(barrier, inc=1, device_id=(d, j), device_id_type=MESH)
    for e in dpeers:
        pl.semaphore_signal(barrier, inc=1, device_id=(e, c), device_id_type=MESH)

    xi, coti, mask, xb, cotb = (v[n] for n in ("xi", "coti", "mask", "xb", "cotb"))
    w1s, w1r, w2s, w2r, wfull = (v[n] for n in ("w1s", "w1r", "w2s", "w2r", "wfull"))
    w1f, wsf, w2f = red_state.at[0], spa_state.at[0], exp_state.at[0]
    loads = [
        pltpu.make_async_copy(states_hbm[0][0], w1f, lsem.at[0]),
        pltpu.make_async_copy(images, xi, lsem.at[1]),
        pltpu.make_async_copy(states_hbm[2][0], w2f, lsem.at[2]),
        pltpu.make_async_copy(states_hbm[1][0], wsf, lsem.at[3]),
        pltpu.make_async_copy(cotangent, coti, lsem.at[4]),
    ]
    for load in loads:
        load.start()
    state_loads = []
    for s, state in enumerate((red_state, spa_state, exp_state)):
        places = (state.at[pl.ds(1, 2)], state.at[3])
        for part, place in enumerate(places):
            state_loads.append(pltpu.make_async_copy(states_hbm[s][part + 1], place, stsem.at[2 * s + part]))

    def columns_of(ref, j):
        return ref[:, pl.ds(pl.multiple_of(j * wp, wp), wp)].astype(BF16)

    loads[0].wait()
    for j in zpeers:
        w1s[j] = columns_of(w1f, j)
    w1r[c] = columns_of(w1f, c)
    pl.semaphore_wait(barrier, C - 1 + D - 1)
    w1_copies = []
    for k, j in enumerate(zpeers):
        w1_copies.append(
            pltpu.make_async_remote_copy(
                src_ref=w1s.at[j], dst_ref=w1r.at[c], send_sem=w1ssem.at[k], recv_sem=w1rsem.at[k],
                device_id=(d, j), device_id_type=MESH,
            )
        )
        w1_copies[-1].start()

    row = lax.broadcasted_iota(jnp.int32, (I, LANES), 0)
    side = jnp.zeros((I, LANES), jnp.int32)
    for i in range(I):
        side = jnp.where(row == i, 5 + 2 * groups[i], side)
    cells_here = jnp.zeros((I, LANES), F32)
    for p in range(PIX):
        inside = (side > max(p // MAP, p % MAP)).astype(F32)
        mask[p * I : (p + 1) * I, :] = inside
        cells_here = cells_here + inside
    mask[R:RP, :] = jnp.zeros((RP - R, LANES), F32)
    count_here = jnp.sum(cells_here, axis=0, keepdims=True)

    def by_rows(src, dst):
        full = R // CHUNK * CHUNK

        def step(n, carry):
            rows = pl.ds(pl.multiple_of(n * CHUNK, CHUNK), CHUNK)
            dst[rows, :] = src[rows, :]
            return carry

        lax.fori_loop(0, R // CHUNK, step, 0)
        if RP > full:
            rest = [src[full:R, :].astype(F32)] if R > full else []
            rest.append(jnp.zeros((RP - R, src.shape[1]), F32))
            dst[full:RP, :] = jnp.concatenate(rest, axis=0).astype(BF16)

    def lanes(values, width):
        if width <= LANES:
            return values[:, :width]
        return jnp.concatenate([values] * (width // LANES), axis=1)

    def mask_of(rows, width):
        return lanes(mask[rows, :], width)

    def over_chunks(body, carry=0):
        def step(s, carry):
            return body(pl.ds(pl.multiple_of(s * CHUNK, CHUNK), CHUNK), carry)

        return lax.fori_loop(0, RP // CHUNK, step, carry)

    def each_chunk(body):
        def step(rows, carry):
            body(rows)
            return carry

        over_chunks(step)

    def fold_rows(values):
        total = values[0:8]
        for s in range(1, values.shape[0] // 8):
            total = total + values[8 * s : 8 * s + 8]
        return total

    def total_of(values):
        return jnp.sum(values, axis=0, keepdims=True)

    def rows_of(*values):
        rest = jnp.zeros((8 - len(values), values[0].shape[1]), F32)
        return jnp.concatenate(list(values) + [rest], axis=0)

    loads[1].wait()
    by_rows(xi, xb)

    acc, p1s, p1r = v["acc"], v["p1s"], v["p1r"]
    for k in range(1, C):
        j = lax.rem(c - k + C, C)
        w1_copies[k - 1].wait_recv()
        p1s[j] = nt(xb[...], w1r[j]).astype(BF16)
        send("pre1", p1s.at[j, pl.ds(0, RS)], p1r.at[c, pl.ds(0, RS)], (d, j))
    acc[...] = nt(xb[...], w1r[c])
    loads[2].wait()
    for j in zpeers:
        w2s[j] = columns_of(w2f, j)
    w2r[c] = columns_of(w2f, c)
    for j in zpeers:
        send("w2", w2s.at[j], w2r.at[c], (d, j))
    loads[4].wait()
    by_rows(coti, cotb)
    loads[3].wait()
    for t in range(TAPS):
        wfull[c, t * ip : (t + 1) * ip, :] = wsf[t].astype(BF16)
    for load in state_loads:
        load.start()

    def add_partials(name, recv):
        got(name, recv.at[pl.ds(0, C - 1), pl.ds(0, RS)])
        for j in zpeers:
            acc[0:RS, :] += recv[j, 0:RS, :].astype(F32)

    add_partials("pre1", p1r)

    def moments(src, width):
        def sums(rows, carry):
            return carry + fold_rows(src[rows, :] * mask_of(rows, width))

        mean = total_of(over_chunks(sums, jnp.zeros((8, width), F32))) / lanes(count_here, width)

        def squares(rows, carry):
            centered = src[rows, :] - mean
            return carry + fold_rows(mask_of(rows, width) * centered * centered)

        return mean, total_of(over_chunks(squares, jnp.zeros((8, width), F32)))

    def exchange_dp(name, table):
        for e in dpeers:
            send(name, table.at[d], table.at[d], (e, c))

    def combine(name, table):
        got(name, table.at[pl.ds(0, D - 1)])
        count = table[0, 2:3, :]
        average = count * table[0, 0:1, :]
        for e in range(1, D):
            count = count + table[e, 2:3, :]
            average = average + table[e, 2:3, :] * table[e, 0:1, :]
        average = average / count
        variance = jnp.zeros_like(average)
        for e in range(D):
            off = table[e, 0:1, :] - average
            variance = variance + (table[e, 1:2, :] + table[e, 2:3, :] * off * off)
        return average, lax.rsqrt(variance / count + norm_eps), count

    def sum_dp(name, table):
        got(name, table.at[pl.ds(0, D - 1)])
        total = table[0]
        for e in range(1, D):
            total = total + table[e]
        return total[0:1, :], total[1:2, :]

    def send_z(name, ref, rows=None):
        part = ref.at[c] if rows is None else ref.at[c, pl.ds(0, rows)]
        for j in zpeers:
            send(name, part, part, (d, j))

    def got_z(name, ref, rows=None):
        got(name, ref.at[pl.ds(0, C - 1)] if rows is None else ref.at[pl.ds(0, C - 1), pl.ds(0, rows)])

    def inner_forward(layer, bn, table, held, held_name, par, par_name):
        mean, spread = moments(acc, ip)
        table[d] = rows_of(mean, spread, lanes(count_here, ip))
        exchange_dp(bn, table)

        def center(rows):
            held[c, rows, :] = ((acc[rows, :] - mean) * mask_of(rows, ip)).astype(BF16)

        each_chunk(center)
        send_z(held_name, held, RS)
        average, inverse, count = combine(bn, table)
        par[c] = rows_of(
            inverse, (mean - average) * inverse,
            inner_norm[layer : layer + 1, :], inner_norm[2 + layer : 3 + layer, :],
        )
        send_z(par_name, par)
        got_z(held_name, held, RS)
        got_z(par_name, par)
        return count

    def joined(blocks, rows):
        return jnp.concatenate([blocks[j, rows, :].astype(F32) for j in range(C)], axis=1)

    def table_row(par, r):
        return jnp.concatenate([par[j, r : r + 1, :] for j in range(C)], axis=1)

    v1, v2, d2b, pm1, pm2, pm3 = (v[n] for n in ("v1", "v2", "d2b", "pm1", "pm2", "pm3"))
    for j in range(C):
        for ref in (v1, v2, d2b):
            ref[j, RS:RP, :] = jnp.zeros((RP - RS, ip), BF16)
    count_ip = inner_forward(0, "bn1", v["st1"], v1, "act1", pm1, "par1")

    def make_act(held, par, dst):
        inverse, shift, gain, bias = (table_row(par, r) for r in range(4))

        def step(rows):
            value = gain * (joined(held, rows) * inverse + shift) + bias
            dst[rows, :] = (value * sigmoid(value) * mask_of(rows, K)).astype(dst.dtype)

        each_chunk(step)

    big, pad, cols = v["big"], v["pad"], v["cols"]
    pad[...] = jnp.zeros_like(pad)
    make_act(v1, pm1, big)

    def fill_pad():
        for y in range(MAP):
            start = ((y + 1) * PITCH + 1) * I
            pad[start : start + MAP * I, :] = big[y * MAP * I : (y + 1) * MAP * I, :]

    def shifted(offset):
        pieces = [pad[pl.ds(pl.multiple_of(offset + y * PITCH * I, I), MAP * I), :] for y in range(MAP)]
        pieces.append(jnp.zeros((RP - R, K), F32))
        return jnp.concatenate(pieces, axis=0).astype(BF16)

    def weight_of(j, tap):
        return wfull[j, pl.ds(pl.multiple_of(tap * ip, ip), ip), :]

    fill_pad()
    acc[...] = jnp.zeros_like(acc)

    def second_step(tap, carry):
        cols[tap] = shifted((lax.div(tap, 3) * PITCH + lax.rem(tap, 3)) * I)
        acc[...] += nt(cols[tap], weight_of(c, tap))
        return carry

    lax.fori_loop(0, TAPS, second_step, 0)
    inner_forward(1, "bn2", v["st2"], v2, "act2", pm2, "par2")

    def part_of(j, e):
        return wfull.at[j, pl.ds(pl.multiple_of(e * sz.PS, 16), sz.PS)]

    for j in zpeers:
        send("wsp", part_of(c, d), part_of(c, d), (d, j))
    act2 = v["act2"]
    make_act(v2, pm2, act2)

    third, og, tg = v["third"], v["og"], v["tg"]
    got_z("w2", w2r)
    third[...] = nn(act2[...], w2r[...].reshape(K, wp))
    mean3, spread3 = moments(third, wp)
    st3, st4, st5, st6 = v["st3"], v["st4"], v["st5"], v["st6"]
    st3[d] = rows_of(mean3, spread3, lanes(count_here, wp))
    exchange_dp("bn3", st3)
    average3, inverse3, count_wp = combine("bn3", st3)
    gain3, bias3 = outer_norm[0:1, :], outer_norm[1:2, :]

    def last_step(rows, carry):
        m = mask_of(rows, wp)
        normed = (third[rows, :] - average3) * inverse3
        third[rows, :] = normed
        summed = gain3 * normed + bias3 + xb[rows, :].astype(F32)
        s = sigmoid(summed)
        here = summed * s * m
        output[rows, :] = here
        grad = cotb[rows, :].astype(F32) * (s * (1.0 + summed * (1.0 - s))) * m
        og[rows, :] = grad
        return carry[0] + fold_rows(grad), carry[1] + fold_rows(grad * normed)

    zero_wp = jnp.zeros((8, wp), F32)
    sums = over_chunks(last_step, (zero_wp, zero_wp))
    st4[d] = rows_of(total_of(sums[0]), total_of(sums[1]))
    exchange_dp("bk3", st4)
    bias_grad3, gain_grad3 = sum_dp("bk3", st4)
    scale3 = inverse3 * gain3

    def third_step(rows):
        back = mask_of(rows, wp) * ((bias_grad3 + third[rows, :] * gain_grad3) / count_wp)
        tg[rows, :] = (scale3 * (og[rows, :] - back)).astype(BF16)

    each_chunk(third_step)

    p2s, p2r = p1s, v["p2r"]
    sent_done("pre1")
    for k in range(1, C):
        j = lax.rem(c - k + C, C)
        p2s[j] = nt(tg[...], w2r[j]).astype(BF16)
        send("grad2", p2s.at[j, pl.ds(0, RS)], p2r.at[c, pl.ds(0, RS)], (d, j))
    acc[...] = nt(tg[...], w2r[c])

    class Reduction:
        def __init__(self, name, z, part):
            self.name, self.z, self.part = name, z, part
            self.gs, self.rb, self.sm, self.rq, self.tot, self.fin = (
                v[name + "_" + s] for s in ("gs", "rb", "sm", "rq", "tot", "fin")
            )

        def pieces(self, first, rows):
            row, end = first, first + rows
            while row < end:
                owner = row // self.part
                stop = min(end, (owner + 1) * self.part)
                yield owner, row - owner * self.part, row - first, stop - row
                row = stop

        def put(self, zi, first, value):
            for owner, there, here, n in self.pieces(first, value.shape[0]):
                self.gs[owner % 2, owner // 2, zi, there : there + n, :] = value[here : here + n, :]

        def take(self, zi, first, rows):
            found = [
                self.fin[owner % 2, owner // 2, zi, there : there + n, :].astype(F32)
                for owner, there, _, n in self.pieces(first, rows)
            ]
            return jnp.concatenate(found, axis=0)

        def pair(self):
            send(self.name + "core", self.gs.at[1 - h], self.rb, (sibling, c))

        def chips(self):
            got(self.name + "core", self.rb)
            for e in range(Q):
                self.sm[e] = (self.gs[h, e].astype(F32) + self.rb[e].astype(F32)).astype(BF16)
            for e in qpeers:
                send(self.name + "chip", self.sm.at[e], self.rq.at[q], (2 * e + h, c))

        def chan(self):
            got(self.name + "chip", self.rq.at[pl.ds(0, Q - 1)])
            total = self.sm[q].astype(F32)
            for e in qpeers:
                total = total + self.rq[e].astype(F32)
            self.tot[...] = total.astype(BF16)
            if self.z == 1:
                self.fin[h, q, 0] = self.tot[0]
            else:
                self.fin[h, q, c] = self.tot[c]
                for j in zpeers:
                    send("z" + self.name, self.tot.at[j], self.fin.at[h, q, c], (d, j))

        def back(self):
            if self.z > 1:
                got("z" + self.name, self.fin.at[h, q, pl.ds(0, C - 1)])
            for e in qpeers:
                send(self.name + "back", self.fin.at[h, q], self.fin.at[h, q], (2 * e + h, c))

        def other(self):
            got(self.name + "back", self.fin.at[h, pl.ds(0, Q - 1)])
            send(self.name + "pair", self.fin.at[h], self.fin.at[h], (sibling, c))

        def done(self):
            got(self.name + "pair", self.fin.at[0])

    exp_red = Reduction("exp", C, sz.PW)
    spa_red = Reduction("spa", 1, sz.PS)
    red_red = Reduction("red", C, sz.PW)
    for j in range(C):
        exp_red.put(j, 0, tn(act2[:, j * ip : (j + 1) * ip], tg[...]).astype(BF16))
    exp_red.pair()

    add_partials("grad2", p2r)
    inverse_own, shift_own, gain_own, bias_own = (pm2[c, r : r + 1, :] for r in range(4))

    def second_back(rows, carry):
        normed = v2[c, rows, :].astype(F32) * inverse_own + shift_own
        value = gain_own * normed + bias_own
        s = sigmoid(value)
        grad = acc[rows, :] * (s * (1.0 + value * (1.0 - s))) * mask_of(rows, ip)
        d2b[c, rows, :] = grad.astype(BF16)
        return carry[0] + fold_rows(grad), carry[1] + fold_rows(grad * normed)

    zero_ip = jnp.zeros((8, ip), F32)
    sums = over_chunks(second_back, (zero_ip, zero_ip))
    st5[d] = rows_of(total_of(sums[0]), total_of(sums[1]))
    exchange_dp("bk2", st5)
    send_z("dlt2", d2b, RS)
    exp_red.chips()
    got("wsp", wfull.at[pl.ds(0, C - 1), pl.ds(0, sz.PS)])
    for j in zpeers:
        for e in dpeers:
            send("wdp", part_of(j, d), part_of(j, d), (e, c))
    bias_grad2, gain_grad2 = sum_dp("bk2", st5)
    pm3[c] = rows_of(bias_grad2 / count_ip, gain_grad2 / count_ip)
    send_z("par3", pm3)
    sgo = v["sgo"]

    def own_second(rows):
        normed = v2[c, rows, :].astype(F32) * inverse_own + shift_own
        back = mask_of(rows, ip) * (pm3[c, 0:1, :] + normed * pm3[c, 1:2, :])
        sgo[rows, :] = (inverse_own * gain_own * (d2b[c, rows, :].astype(F32) - back)).astype(BF16)

    each_chunk(own_second)
    for tap in range(TAPS):
        spa_red.put(0, tap * ip, tn(sgo[...], cols[tap]).astype(BF16))
    exp_red.chan()
    spa_red.pair()
    got_z("dlt2", d2b, RS)
    got_z("par3", pm3)
    inverse2, shift2, gain2 = (table_row(pm2, r) for r in range(3))
    bias_part, gain_part = table_row(pm3, 0), table_row(pm3, 1)
    scale2 = inverse2 * gain2

    def full_second(rows):
        normed = joined(v2, rows) * inverse2 + shift2
        back = mask_of(rows, K) * (bias_part + normed * gain_part)
        big[rows, :] = (scale2 * (joined(d2b, rows) - back)).astype(BF16).astype(F32)

    each_chunk(full_second)
    fill_pad()
    spa_red.chips()
    exp_red.back()
    got("wdp", wfull.at[pl.ds(0, C - 1), pl.ds(0, (D - 1) * sz.PS)])

    fag = v["fag"]
    fag[...] = jnp.zeros_like(fag)

    def first_act_step(tap, carry):
        offset = ((2 - lax.div(tap, 3)) * PITCH + 2 - lax.rem(tap, 3)) * I
        weight = jnp.concatenate([weight_of(j, tap) for j in range(C)], axis=0)
        fag[...] += nn(shifted(offset), weight)
        return carry

    lax.fori_loop(0, TAPS, first_act_step, 0)
    inverse1, shift1, gain1, bias1 = (table_row(pm1, r) for r in range(4))

    def first_back(rows, carry):
        normed = joined(v1, rows) * inverse1 + shift1
        value = gain1 * normed + bias1
        s = sigmoid(value)
        grad = fag[rows, :] * (s * (1.0 + value * (1.0 - s))) * mask_of(rows, K)
        fag[rows, :] = grad
        big[rows, :] = normed
        return carry[0] + fold_rows(grad), carry[1] + fold_rows(grad * normed)

    zero_k = jnp.zeros((8, K), F32)
    sums = over_chunks(first_back, (zero_k, zero_k))
    st6[d] = rows_of(total_of(sums[0]), total_of(sums[1]))
    exchange_dp("bk1", st6)
    spa_red.chan()
    spa_red.back()
    exp_red.other()
    bias_grad1, gain_grad1 = sum_dp("bk1", st6)
    scale1 = inverse1 * gain1
    count_k = lanes(count_ip[:, 0:1] + jnp.zeros((1, LANES), F32), K)
    fg = v["fg"]

    def first_step(rows):
        back = mask_of(rows, K) * ((bias_grad1 + big[rows, :] * gain_grad1) / count_k)
        fg[rows, :] = (scale1 * (fag[rows, :] - back)).astype(BF16)

    each_chunk(first_step)
    for j in range(C):
        red_red.put(j, 0, tn(fg[:, j * ip : (j + 1) * ip], xb[...]).astype(BF16))
    red_red.pair()
    input_grad[...] = nn(fg[...], w1r[...].reshape(K, wp)) + og[...]
    red_red.chips()
    spa_red.other()

    def adam(state, at, grad, rate, decay):
        weight, moment, square, average = (state[(part, *at)] for part in range(4))
        first = beta_one * moment + (1.0 - beta_one) * grad
        second = beta_two * square + (1.0 - beta_two) * grad * grad
        scaled = first * (1.0 / (1.0 - beta_one**STEP))
        root = jnp.sqrt(second * (1.0 / (1.0 - beta_two**STEP))) + adam_eps
        updated = weight - rate * (scaled / root + decay * weight)
        state[(0, *at)] = updated
        state[(1, *at)] = first
        state[(2, *at)] = second
        state[(3, *at)] = ema_rate * average + (1.0 - ema_rate) * updated

    def adam_rows(red, state, rate):
        for j in range(C):
            for first in range(0, ip, 32):
                n = min(32, ip - first)
                adam(state, (slice(first, first + n), slice(j * wp, (j + 1) * wp)), red.take(j, first, n), rate, decay_rate)

    for load in state_loads:
        load.wait()
    red_red.chan()
    exp_red.done()
    adam_rows(exp_red, exp_state, 2.0 / math.sqrt(K))
    red_red.back()
    spa_red.done()
    for tap in range(TAPS):
        for first in range(0, ip, 32):
            n = min(32, ip - first)
            adam(
                spa_state, (tap, slice(first, first + n), slice(0, K)), spa_red.take(0, tap * ip + first, n),
                2.0 / math.sqrt(TAPS * K), decay_rate,
            )
        if tap == TAPS // 2:
            red_red.other()

    own = v["own"]
    for j in range(C):
        own[j] = rows_of(gain_grad1[:, j * ip : (j + 1) * ip], bias_grad1[:, j * ip : (j + 1) * ip])
    inner_grads = [own[c, 0:1, :], gain_grad2, own[c, 1:2, :], bias_grad2]
    outer_grads = [gain_grad3, bias_grad3]
    inner_state[0:4, :] = inner_norm[...]
    for m in range(2):
        for r in range(2):
            inner_state[4 + 4 * m + 2 * r : 6 + 4 * m + 2 * r, :] = inner_moments[m, r]
    inner_state[12:16, :] = inner_ema[...]
    outer_state[0:2, :] = outer_norm[...]
    outer_state[2:6, :] = outer_moments[...]
    outer_state[6:8, :] = outer_ema[...]

    def adam_small(state, n, grads):
        grad = jnp.concatenate(grads, axis=0)
        weight, moment, square, average = (state[part * n : (part + 1) * n, :] for part in range(4))
        first = beta_one * moment + (1.0 - beta_one) * grad
        second = beta_two * square + (1.0 - beta_two) * grad * grad
        scaled = first * (1.0 / (1.0 - beta_one**STEP))
        root = jnp.sqrt(second * (1.0 / (1.0 - beta_two**STEP))) + adam_eps
        updated = weight - norm_rate * (scaled / root)
        state[0:n, :] = updated
        state[n : 2 * n, :] = first
        state[2 * n : 3 * n, :] = second
        state[3 * n : 4 * n, :] = ema_rate * average + (1.0 - ema_rate) * updated

    adam_small(inner_state, 4, inner_grads)
    adam_small(outer_state, 2, outer_grads)
    red_red.done()
    adam_rows(red_red, red_state, 2.0 / math.sqrt(sz.W))
    for copy in w1_copies:
        copy.wait_send()
    for name, ref in sent:
        wait_bytes(ref, ssem.at[sem_of[name]])


def store_kernel(n, *refs):
    held, places, sem = refs[:7], refs[7 : 7 + n], refs[-1]
    output, input_grad, red_state, spa_state, exp_state, inner_state, outer_state = held
    parts = [output.at[pl.ds(0, places[0].shape[0])], input_grad.at[pl.ds(0, places[1].shape[0])]]
    for state in (red_state, spa_state, exp_state):
        parts += [state.at[part] for part in range(4)]
    copies = [pltpu.make_async_copy(src, dst, sem.at[i]) for i, (src, dst) in enumerate(zip(parts, places))]
    for copy in copies:
        copy.start()
    inner_places, outer_places = places[14:18], places[18:22]
    for part in range(4):
        inner_places[part][...] = inner_state[part * 4 : (part + 1) * 4, :]
        outer_places[part][...] = outer_state[part * 2 : (part + 1) * 2, :]
    for copy in copies:
        copy.wait()


def per_device(
    mesh_dp, mesh_chan,
    images, groups, cotangent, reduce_weight, spatial_weight, expand_weight, inner_norm, outer_norm,
    reduce_moments, spatial_moments, expand_moments, inner_moments, outer_moments,
    reduce_ema, spatial_ema, expand_ema, inner_ema, outer_ema,
):
    sz = Sizes(mesh_dp, mesh_chan, images, reduce_weight)
    ip, wp, K, C = sz.ip, sz.wp, sz.K, sz.C

    def by_cell(a):
        return a.transpose(1, 0, 2).reshape(sz.R, wp)

    def by_tap(a):
        return a.transpose(1, 2, 0, 3).reshape(TAPS, ip, K)

    any_spec, vmem_spec = pl.BlockSpec(memory_space=pl.ANY), pl.BlockSpec(memory_space=pltpu.VMEM)
    states = []
    for weight, moments, ema in (
        (reduce_weight, reduce_moments, reduce_ema),
        (by_tap(spatial_weight), spatial_moments.transpose(0, 2, 3, 1, 4).reshape(2, TAPS, ip, K), by_tap(spatial_ema)),
        (expand_weight, expand_moments, expand_ema),
    ):
        states += [weight, moments, ema]
    held_shapes = (
        (sz.RP, wp), (sz.RP, wp), (4, ip, sz.W), (4, TAPS, ip, K), (4, ip, sz.W), (16, ip), (8, wp),
    )
    held = pl.pallas_call(
        functools.partial(block_kernel, sz),
        out_shape=tuple(pltpu.VMEM(shape, F32) for shape in held_shapes),
        in_specs=[pl.BlockSpec(memory_space=pltpu.SMEM)] + [any_spec] * 2 + [vmem_spec] * 6 + [any_spec] * 9,
        out_specs=(vmem_spec,) * len(held_shapes),
        scratch_shapes=[pltpu.VMEM(shape, dtype) for _, shape, dtype in scratch_table(sz)]
        + [
            pltpu.SemaphoreType.DMA((5,)),
            pltpu.SemaphoreType.DMA((6,)),
            pltpu.SemaphoreType.DMA((C - 1,)),
            pltpu.SemaphoreType.DMA((C - 1,)),
            pltpu.SemaphoreType.DMA((len(PHASES),)),
            pltpu.SemaphoreType.DMA((len(PHASES),)),
        ],
        compiler_params=pltpu.CompilerParams(
            collective_id=0, has_side_effects=True, vmem_limit_bytes=VMEM_TOTAL - sum(vmem_bytes(shape, F32) for shape in held_shapes)
        ),
    )(
        groups, by_cell(images), by_cell(cotangent),
        inner_norm.reshape(4, ip), outer_norm, inner_moments, outer_moments.reshape(4, wp),
        inner_ema.reshape(4, ip), outer_ema, *states,
    )
    held = [pltpu.with_memory_space_constraint(a, pltpu.VMEM) for a in held]
    shapes = [(sz.R, wp)] * 2 + [(ip, sz.W)] * 4 + [(TAPS, ip, K)] * 4 + [(ip, sz.W)] * 4
    small = [(4, ip)] * 4 + [(2, wp)] * 4
    results = pl.pallas_call(
        functools.partial(store_kernel, len(shapes + small)),
        out_shape=tuple(jax.ShapeDtypeStruct(shape, F32) for shape in shapes + small),
        in_specs=[vmem_spec] * len(held),
        out_specs=(any_spec,) * len(shapes) + (vmem_spec,) * len(small),
        scratch_shapes=[pltpu.SemaphoreType.DMA((len(shapes),))],
        compiler_params=pltpu.CompilerParams(vmem_limit_bytes=2 * 2**20),
    )(*held)
    images_of = [a.reshape(PIX, sz.I, wp).transpose(1, 0, 2) for a in results[:2]]
    taps = [a.reshape(3, 3, ip, K).transpose(2, 0, 1, 3) for a in results[6:10]]
    inner = [a.reshape(2, 2, ip) for a in results[14:18]]
    return (*images_of, *results[2:6], *taps, *results[10:14], *inner, *results[18:22])


def solution(mesh):
    placed = (
        P("dp", None, "chan"),
        P("dp"),
        P("dp", None, "chan"),
        P("chan", None),
        P("chan", None, None, None),
        P("chan", None),
        P(None, None, "chan"),
        P(None, "chan"),
        P(None, "chan", None),
        P(None, "chan", None, None, None),
        P(None, "chan", None),
        P(None, None, None, "chan"),
        P(None, None, "chan"),
        P("chan", None),
        P("chan", None, None, None),
        P("chan", None),
        P(None, None, "chan"),
        P(None, "chan"),
    )
    return jax.shard_map(
        functools.partial(per_device, mesh.shape["dp"], mesh.shape["chan"]),
        mesh=mesh,
        in_specs=placed,
        out_specs=(P("dp", None, "chan"),) * 2
        + (P("chan", None),) * 4
        + (P("chan", None, None, None),) * 4
        + (P("chan", None),) * 4
        + (P(None, None, "chan"),) * 4
        + (P(None, "chan"),) * 4,
        check_vma=False,
    )
```

```python
import functools
import math

import jax
import jax.numpy as jnp
from jax import lax
from jax.experimental import pallas as pl
from jax.experimental.pallas import tpu as pltpu
from jax.sharding import PartitionSpec as P

MESH = pl.DeviceIdType.MESH
MAP = 9
PIX = MAP * MAP
TAPS = 9
PITCH = MAP + 1
STEP = 5
LANES = 128
CHUNK = 48
VMEM_TOTAL = 62 * 2**20

norm_eps = 1e-05
adam_eps = 1e-08
beta_one = 0.5
beta_two = 0.5
decay_rate = 0.05
ema_rate = 0.75
norm_rate = 0.3

F32 = jnp.float32
BF16 = jnp.bfloat16


def round_up(value, unit):
    return -(-value // unit) * unit


class Sizes:
    def __init__(self, mesh_dp, mesh_chan, images, reduce_weight):
        self.D, self.C = mesh_dp, mesh_chan
        self.Q = self.D // 2
        self.I, _, self.wp = images.shape
        self.ip, self.W = reduce_weight.shape
        self.K = self.ip * self.C
        self.KB = self.K // LANES
        self.WB = self.wp // LANES
        self.R = PIX * self.I
        self.RS = round_up(self.R, 16)
        self.RP = round_up(self.R, CHUNK)
        self.RT = 8 * CHUNK
        self.NS = TAPS * self.ip
        self.PW = round_up(-(-self.ip // self.D), 16)
        self.PS = round_up(-(-self.NS // self.D), 16)
        self.PADROWS = ((MAP + 2) * PITCH + 2) * self.I


Z_PHASES = ["w2", "pre1", "grad2", "wsp", "zexp", "zred"]
Z_PHASES += [name + part for name in ("act1", "act2", "dlt2") for part in ("top", "par", "low")]
D_PHASES = ["w2pair", "bn1", "bn2", "bn3", "bk3", "bk2", "bk1", "wchip", "wpair"]
R_PHASES = [g + s for g in ("exp", "spa", "red") for s in ("core", "chip", "back0", "back1", "pair")]


def phases(sz):
    each = [name + str(k) for name in ("w1", "w1pair") for k in range(sz.C - 1)]
    return Z_PHASES + D_PHASES + R_PHASES + each


def nt(a, b):
    return lax.dot_general(a, b, (((1,), (1,)), ((), ())), preferred_element_type=F32)


def nn(a, b):
    return lax.dot_general(a, b, (((1,), (0,)), ((), ())), preferred_element_type=F32)


def tn(a, b):
    return lax.dot_general(a, b, (((0,), (0,)), ((), ())), preferred_element_type=F32)


def sigmoid(v):
    return jax.nn.sigmoid(v)


def vmem_bytes(shape, dtype):
    *lead, rows, width = shape
    return math.prod(lead) * round_up(rows, 8) * round_up(width, LANES) * jnp.dtype(dtype).itemsize


def scratch_table(sz):
    C, D, Q, ip, wp, K, RP, I = sz.C, sz.D, sz.Q, sz.ip, sz.wp, sz.K, sz.RP, sz.I
    table = [
        ("xi", (sz.R, wp), BF16),
        ("coti", (sz.R, wp), BF16),
        ("mask", (RP, LANES), F32),
        ("xb", (RP, wp), BF16),
        ("cotb", (RP, wp), BF16),
        ("w1s", (C, ip, wp), BF16),
        ("w1r", (C, ip, wp), BF16),
        ("w2s", (C, ip, wp), BF16),
        ("w2r", (C, ip, wp), BF16),
        ("wfull", (C, D * sz.PS, K), BF16),
        ("p1s", (C, RP, ip), BF16),
        ("p1r", (C, RP, ip), BF16),
        ("v1", (C, RP, ip), BF16),
        ("v2", (C, RP, ip), BF16),
        ("d2b", (C, RP, ip), BF16),
        ("pm1", (C, 8, ip), F32),
        ("pm2", (C, 8, ip), F32),
        ("pm3", (C, 8, ip), F32),
        ("own", (C, 8, ip), F32),
        ("st1", (D, 8, ip), F32),
        ("st2", (D, 8, ip), F32),
        ("st3", (D, 8, wp), F32),
        ("st4", (D, 8, wp), F32),
        ("st5", (D, 8, ip), F32),
        ("st6", (D, 8, K), F32),
        ("acc", (RP, ip), F32),
        ("pad", (sz.PADROWS, K), F32),
        ("cols", (TAPS, RP, K), BF16),
        ("act2", (RP, K), BF16),
        ("third", (RP, wp), F32),
        ("og", (RP, wp), F32),
        ("tg", (RP, wp), BF16),
        ("big", (RP, K), F32),
        ("fag", (RP, K), F32),
        ("sgo", (RP, ip), BF16),
        ("fg", (RP, K), BF16),
    ]
    for name, z, part, width in (("exp", C, sz.PW, wp), ("spa", 1, sz.PS, K), ("red", C, sz.PW, wp)):
        table += [
            (name + "_gs", (2, Q, z, part, width), BF16),
            (name + "_rb", (Q, z, part, width), BF16),
            (name + "_sm", (Q, z, part, width), BF16),
            (name + "_rq", (Q, z, part, width), BF16),
            (name + "_tot", (z, part, width), BF16),
            (name + "_fin", (2, Q, z, part, width), BF16),
        ]
    return table


def block_kernel(sz, *refs):
    groups, images, cotangent, inner_norm, outer_norm, inner_moments, outer_moments, inner_ema, outer_ema = refs[:9]
    states_hbm = [refs[9:12], refs[12:15], refs[15:18]]
    output, input_grad, red_state, spa_state, exp_state, inner_state, outer_state = refs[18:25]
    table = scratch_table(sz)
    v = {name: ref for (name, _, _), ref in zip(table, refs[25:])}
    lsem, stsem, ssem, rsem = refs[25 + len(table) :]
    D, C, Q, I, K, KB, WB = sz.D, sz.C, sz.Q, sz.I, sz.K, sz.KB, sz.WB
    ip, wp, R, RS, RP = sz.ip, sz.wp, sz.R, sz.RS, sz.RP
    d = lax.axis_index("dp")
    c = lax.axis_index("chan")
    q = lax.div(d, 2)
    h = lax.rem(d, 2)
    zpeers = [lax.rem(c + k, C) for k in range(1, C)]
    dpeers = [lax.rem(d + k, D) for k in range(1, D)]
    qpeers = [lax.rem(q + k, Q) for k in range(1, Q)]
    sibling = d + 1 - 2 * h
    sem_of = {name: i for i, name in enumerate(phases(sz))}
    sent = []

    def send(name, src, dst, device):
        pltpu.make_async_remote_copy(
            src_ref=src, dst_ref=dst, send_sem=ssem.at[sem_of[name]], recv_sem=rsem.at[sem_of[name]],
            device_id=device, device_id_type=MESH,
        ).start()

    def wait_bytes(ref, sem):
        pltpu.make_async_copy(ref, ref, sem).wait()

    def got(name, ref):
        wait_bytes(ref, rsem.at[sem_of[name]])
        sent.append((name, ref))

    def sent_done(name):
        for entry in [e for e in sent if e[0] == name]:
            wait_bytes(entry[1], ssem.at[sem_of[name]])
            sent.remove(entry)

    barrier = pltpu.get_barrier_semaphore()
    for j in zpeers:
        pl.semaphore_signal(barrier, inc=1, device_id=(d, j), device_id_type=MESH)
    for e in dpeers:
        pl.semaphore_signal(barrier, inc=1, device_id=(e, c), device_id_type=MESH)

    xi, coti, mask, xb, cotb = (v[n] for n in ("xi", "coti", "mask", "xb", "cotb"))
    w1s, w1r, w2s, w2r, wfull = (v[n] for n in ("w1s", "w1r", "w2s", "w2r", "wfull"))
    w1f, wsf, w2f = red_state.at[0], spa_state.at[0], exp_state.at[0]
    loads = [
        pltpu.make_async_copy(states_hbm[0][0], w1f, lsem.at[0]),
        pltpu.make_async_copy(images, xi, lsem.at[1]),
        pltpu.make_async_copy(states_hbm[2][0], w2f, lsem.at[2]),
        pltpu.make_async_copy(states_hbm[1][0], wsf, lsem.at[3]),
        pltpu.make_async_copy(cotangent, coti, lsem.at[4]),
    ]
    for load in loads:
        load.start()
    state_loads = []
    for s, state in enumerate((red_state, spa_state, exp_state)):
        places = (state.at[pl.ds(1, 2)], state.at[3])
        for part, place in enumerate(places):
            state_loads.append(pltpu.make_async_copy(states_hbm[s][part + 1], place, stsem.at[2 * s + part]))

    def columns_of(ref, j):
        return ref[:, pl.ds(pl.multiple_of(j * wp, wp), wp)].astype(BF16)

    loads[0].wait()
    for j in zpeers:
        w1s[j] = columns_of(w1f, j)
    w1r[c] = columns_of(w1f, c)
    pl.semaphore_wait(barrier, C - 1 + D - 1)

    def half(ref, j, side):
        return ref.at[j, pl.ds(pl.multiple_of(side * (ip // 2), 16), ip // 2)]

    for k, j in enumerate(zpeers):
        send("w1" + str(k), half(w1s, j, h), half(w1r, c, h), (d, j))

    row = lax.broadcasted_iota(jnp.int32, (I, LANES), 0)
    side = jnp.zeros((I, LANES), jnp.int32)
    for i in range(I):
        side = jnp.where(row == i, 5 + 2 * groups[i], side)
    cells_here = jnp.zeros((I, LANES), F32)
    for p in range(PIX):
        inside = (side > max(p // MAP, p % MAP)).astype(F32)
        mask[p * I : (p + 1) * I, :] = inside
        cells_here = cells_here + inside
    mask[R:RP, :] = jnp.zeros((RP - R, LANES), F32)
    count_here = jnp.sum(cells_here, axis=0, keepdims=True)

    def by_rows(src, dst):
        full = R // CHUNK * CHUNK

        def step(n, carry):
            rows = pl.ds(pl.multiple_of(n * CHUNK, CHUNK), CHUNK)
            dst[rows, :] = src[rows, :]
            return carry

        lax.fori_loop(0, R // CHUNK, step, 0)
        if RP > full:
            rest = [src[full:R, :].astype(F32)] if R > full else []
            rest.append(jnp.zeros((RP - R, src.shape[1]), F32))
            dst[full:RP, :] = jnp.concatenate(rest, axis=0).astype(BF16)

    def lanes(values, width):
        if width <= LANES:
            return values[:, :width]
        return jnp.concatenate([values] * (width // LANES), axis=1)

    def mask_of(rows, width):
        return lanes(mask[rows, :], width)

    def over_chunks(body, carry=0):
        def step(s, carry):
            return body(pl.ds(pl.multiple_of(s * CHUNK, CHUNK), CHUNK), carry)

        return lax.fori_loop(0, RP // CHUNK, step, carry)

    def each_chunk(body):
        def step(rows, carry):
            body(rows)
            return carry

        over_chunks(step)

    def fold_rows(values):
        total = values[0:8]
        for s in range(1, values.shape[0] // 8):
            total = total + values[8 * s : 8 * s + 8]
        return total

    def total_of(values):
        return jnp.sum(values, axis=0, keepdims=True)

    def rows_of(*values):
        rest = jnp.zeros((8 - len(values), values[0].shape[1]), F32)
        return jnp.concatenate(list(values) + [rest], axis=0)

    loads[1].wait()
    by_rows(xi, xb)

    acc, p1s, p1r = v["acc"], v["p1s"], v["p1r"]
    sources = [lax.rem(c - k + C, C) for k in range(1, C)]
    for k, j in enumerate(sources):
        got("w1" + str(k), half(w1r, j, h))
        send("w1pair" + str(k), half(w1r, j, h), half(w1r, j, h), (sibling, c))
    for k, j in enumerate(sources):
        got("w1pair" + str(k), half(w1r, j, 1 - h))
        p1s[j] = nt(xb[...], w1r[j]).astype(BF16)
        send("pre1", p1s.at[j, pl.ds(0, RS)], p1r.at[c, pl.ds(0, RS)], (d, j))
    acc[...] = nt(xb[...], w1r[c])
    loads[2].wait()
    for j in zpeers:
        w2s[j] = columns_of(w2f, j)
    w2r[c] = columns_of(w2f, c)
    loads[4].wait()
    by_rows(coti, cotb)
    loads[3].wait()
    for t in range(TAPS):
        wfull[c, t * ip : (t + 1) * ip, :] = wsf[t].astype(BF16)
    for load in state_loads:
        load.start()

    def add_partials(name, recv):
        got(name, recv.at[pl.ds(0, C - 1), pl.ds(0, RS)])
        for j in zpeers:
            acc[0:RS, :] += recv[j, 0:RS, :].astype(F32)

    add_partials("pre1", p1r)

    def moments(src, width):
        def sums(rows, carry):
            return carry + fold_rows(src[rows, :] * mask_of(rows, width))

        mean = total_of(over_chunks(sums, jnp.zeros((8, width), F32))) / lanes(count_here, width)

        def squares(rows, carry):
            centered = src[rows, :] - mean
            return carry + fold_rows(mask_of(rows, width) * centered * centered)

        return mean, total_of(over_chunks(squares, jnp.zeros((8, width), F32)))

    def exchange_dp(name, table):
        for e in dpeers:
            send(name, table.at[d], table.at[d], (e, c))

    def combine(name, table):
        got(name, table.at[pl.ds(0, D - 1)])
        count = table[0, 2:3, :]
        average = count * table[0, 0:1, :]
        for e in range(1, D):
            count = count + table[e, 2:3, :]
            average = average + table[e, 2:3, :] * table[e, 0:1, :]
        average = average / count
        variance = jnp.zeros_like(average)
        for e in range(D):
            off = table[e, 0:1, :] - average
            variance = variance + (table[e, 1:2, :] + table[e, 2:3, :] * off * off)
        return average, lax.rsqrt(variance / count + norm_eps), count

    def sum_dp(name, table):
        got(name, table.at[pl.ds(0, D - 1)])
        total = table[0]
        for e in range(1, D):
            total = total + table[e]
        return total[0:1, :], total[1:2, :]

    def send_z(name, ref, rows=None):
        part = ref.at[c] if rows is None else ref.at[c, pl.ds(0, rows)]
        for j in zpeers:
            send(name, part, part, (d, j))

    def got_z(name, ref, rows=None):
        got(name, ref.at[pl.ds(0, C - 1)] if rows is None else ref.at[pl.ds(0, C - 1), pl.ds(0, rows)])

    def joined(blocks, rows):
        return jnp.concatenate([blocks[j, rows, :].astype(F32) for j in range(C)], axis=1)

    def table_row(par, r):
        return jnp.concatenate([par[j, r : r + 1, :] for j in range(C)], axis=1)

    def own_part(values):
        own = v["own"]
        for j in range(C):
            own[j, 0 : values.shape[0], :] = values[:, j * ip : (j + 1) * ip]
        return own[c, 0 : values.shape[0], :]

    top_rows, low_rows = pl.ds(0, sz.RT), pl.ds(sz.RT, RS - sz.RT)

    def send_part(name, held, rows):
        for j in zpeers:
            send(name, held.at[c, rows], held.at[c, rows], (d, j))

    def got_part(name, held, rows):
        got(name, held.at[pl.ds(0, C - 1), rows])

    def inner_forward(layer, bn, table, held, name, par):
        mean, spread = moments(acc, ip)
        table[d] = rows_of(mean, spread, lanes(count_here, ip))
        exchange_dp(bn, table)

        def center(rows):
            held[c, rows, :] = ((acc[rows, :] - mean) * mask_of(rows, ip)).astype(BF16)

        each_chunk(center)
        send_part(name + "top", held, top_rows)
        average, inverse, count = combine(bn, table)
        par[c] = rows_of(
            inverse, (mean - average) * inverse,
            inner_norm[layer : layer + 1, :], inner_norm[2 + layer : 3 + layer, :],
        )
        send_z(name + "par", par)
        send_part(name + "low", held, low_rows)
        got_part(name + "top", held, top_rows)
        got_z(name + "par", par)
        got_part(name + "low", held, low_rows)
        return count

    v1, v2, d2b, pm1, pm2, pm3 = (v[n] for n in ("v1", "v2", "d2b", "pm1", "pm2", "pm3"))
    for j in range(C):
        for ref in (v1, v2, d2b):
            ref[j, RS:RP, :] = jnp.zeros((RP - RS, ip), BF16)
    count_ip = inner_forward(0, "bn1", v["st1"], v1, "act1", pm1)
    count_k = lanes(lanes(count_ip, min(ip, LANES))[:, 0:1] + jnp.zeros((1, LANES), F32), K)

    def make_act(held, par, dst):
        inverse, shift, gain, bias = (table_row(par, r) for r in range(4))

        def step(rows):
            value = gain * (joined(held, rows) * inverse + shift) + bias
            dst[rows, :] = (value * sigmoid(value) * mask_of(rows, K)).astype(dst.dtype)

        each_chunk(step)

    for j in zpeers:
        send("w2", half(w2s, j, h), half(w2r, c, h), (d, j))
    big, pad, cols = v["big"], v["pad"], v["cols"]
    pad[...] = jnp.zeros_like(pad)
    make_act(v1, pm1, big)

    def fill_pad():
        for y in range(MAP):
            start = ((y + 1) * PITCH + 1) * I
            pad[start : start + MAP * I, :] = big[y * MAP * I : (y + 1) * MAP * I, :]

    def shifted(offset):
        pieces = [pad[pl.ds(pl.multiple_of(offset + y * PITCH * I, I), MAP * I), :] for y in range(MAP)]
        pieces.append(jnp.zeros((RP - R, K), F32))
        return jnp.concatenate(pieces, axis=0).astype(BF16)

    def weight_of(j, tap):
        return wfull[j, pl.ds(pl.multiple_of(tap * ip, ip), ip), :]

    fill_pad()
    acc[...] = jnp.zeros_like(acc)

    def second_step(tap, carry):
        cols[tap] = shifted((lax.div(tap, 3) * PITCH + lax.rem(tap, 3)) * I)
        acc[...] += nt(cols[tap], weight_of(c, tap))
        return carry

    lax.fori_loop(0, TAPS, second_step, 0)
    got("w2", w2r.at[pl.ds(0, C - 1), pl.ds(0, ip // 2)])
    for j in zpeers:
        send("w2pair", half(w2r, j, h), half(w2r, j, h), (sibling, c))
    inner_forward(1, "bn2", v["st2"], v2, "act2", pm2)

    def part_of(j, e):
        return wfull.at[j, pl.ds(pl.multiple_of(e * sz.PS, 16), sz.PS)]

    for j in zpeers:
        send("wsp", part_of(c, d), part_of(c, d), (d, j))
    act2 = v["act2"]
    make_act(v2, pm2, act2)

    third, og, tg = v["third"], v["og"], v["tg"]
    got("w2pair", w2r.at[pl.ds(0, C - 1), pl.ds(0, ip // 2)])
    third[...] = nn(act2[...], w2r[...].reshape(K, wp))
    mean3, spread3 = moments(third, wp)
    st3, st4, st5, st6 = v["st3"], v["st4"], v["st5"], v["st6"]
    st3[d] = rows_of(mean3, spread3, lanes(count_here, wp))
    exchange_dp("bn3", st3)
    average3, inverse3, count_wp = combine("bn3", st3)
    gain3, bias3 = outer_norm[0:1, :], outer_norm[1:2, :]

    def last_step(rows, carry):
        m = mask_of(rows, wp)
        normed = (third[rows, :] - average3) * inverse3
        third[rows, :] = normed
        summed = gain3 * normed + bias3 + xb[rows, :].astype(F32)
        s = sigmoid(summed)
        here = summed * s * m
        output[rows, :] = here
        grad = cotb[rows, :].astype(F32) * (s * (1.0 + summed * (1.0 - s))) * m
        og[rows, :] = grad
        return carry[0] + fold_rows(grad), carry[1] + fold_rows(grad * normed)

    zero_wp = jnp.zeros((8, wp), F32)
    sums = over_chunks(last_step, (zero_wp, zero_wp))
    st4[d] = rows_of(total_of(sums[0]), total_of(sums[1]))
    exchange_dp("bk3", st4)
    bias_grad3, gain_grad3 = sum_dp("bk3", st4)
    scale3 = inverse3 * gain3

    def third_step(rows):
        back = mask_of(rows, wp) * ((bias_grad3 + third[rows, :] * gain_grad3) / count_wp)
        tg[rows, :] = (scale3 * (og[rows, :] - back)).astype(BF16)

    each_chunk(third_step)

    got("wsp", wfull.at[pl.ds(0, C - 1), pl.ds(0, sz.PS)])
    for j in zpeers:
        for e in qpeers:
            send("wchip", part_of(j, d), part_of(j, d), (2 * e + h, c))

    p2s, p2r = p1s, p1r
    sent_done("pre1")
    for k in range(1, C):
        j = lax.rem(c - k + C, C)
        p2s[j] = nt(tg[...], w2r[j]).astype(BF16)
        send("grad2", p2s.at[j, pl.ds(0, RS)], p2r.at[c, pl.ds(0, RS)], (d, j))
    acc[...] = nt(tg[...], w2r[c])

    class Reduction:
        def __init__(self, name, z, part):
            self.name, self.z, self.part = name, z, part
            self.gs, self.rb, self.sm, self.rq, self.tot, self.fin = (
                v[name + "_" + s] for s in ("gs", "rb", "sm", "rq", "tot", "fin")
            )

        def pieces(self, first, rows):
            row, end = first, first + rows
            while row < end:
                owner = row // self.part
                stop = min(end, (owner + 1) * self.part)
                yield owner, row - owner * self.part, row - first, stop - row
                row = stop

        def put(self, zi, first, value):
            for owner, there, here, n in self.pieces(first, value.shape[0]):
                self.gs[owner % 2, owner // 2, zi, there : there + n, :] = value[here : here + n, :]

        def take(self, zi, first, rows):
            found = [
                self.fin[owner % 2, owner // 2, zi, there : there + n, :].astype(F32)
                for owner, there, _, n in self.pieces(first, rows)
            ]
            return jnp.concatenate(found, axis=0)

        def pair(self):
            send(self.name + "core", self.gs.at[1 - h], self.rb, (sibling, c))

        def chips(self):
            got(self.name + "core", self.rb)
            for e in range(Q):
                self.sm[e] = (self.gs[h, e].astype(F32) + self.rb[e].astype(F32)).astype(BF16)
            for e in qpeers:
                send(self.name + "chip", self.sm.at[e], self.rq.at[q], (2 * e + h, c))

        def chan(self):
            got(self.name + "chip", self.rq.at[pl.ds(0, Q - 1)])
            total = self.sm[q].astype(F32)
            for e in qpeers:
                total = total + self.rq[e].astype(F32)
            self.tot[...] = total.astype(BF16)
            if self.z == 1:
                self.fin[h, q, 0] = self.tot[0]
            else:
                self.fin[h, q, c] = self.tot[c]
                for j in zpeers:
                    send("z" + self.name, self.tot.at[j], self.fin.at[h, q, c], (d, j))

        def halves(self, side, other):
            cut = round_up(self.part // 2, 16)
            rows = pl.ds(0, cut) if side == 0 else pl.ds(cut, self.part - cut)
            return self.fin.at[h, other, slice(None), rows]

        def back(self, side):
            if side == 0 and self.z > 1:
                got("z" + self.name, self.fin.at[h, q, pl.ds(0, C - 1)])
            if side == 1 and self.part <= 16:
                return
            for e in qpeers:
                send(self.name + "back" + str(side), self.halves(side, q), self.halves(side, q), (2 * e + h, c))

        def other(self):
            cut = round_up(self.part // 2, 16)
            got(self.name + "back0", self.fin.at[h, pl.ds(0, Q - 1), slice(None), pl.ds(0, cut)])
            if self.part > 16:
                got(self.name + "back1", self.fin.at[h, pl.ds(0, Q - 1), slice(None), pl.ds(cut, self.part - cut)])
            send(self.name + "pair", self.fin.at[h], self.fin.at[h], (sibling, c))

        def done(self):
            got(self.name + "pair", self.fin.at[0])

    exp_red = Reduction("exp", C, sz.PW)
    spa_red = Reduction("spa", 1, sz.PS)
    red_red = Reduction("red", C, sz.PW)
    for j in range(C):
        exp_red.put(j, 0, tn(act2[:, j * ip : (j + 1) * ip], tg[...]).astype(BF16))
    exp_red.pair()

    add_partials("grad2", p2r)
    inverse_own, shift_own, gain_own, bias_own = (pm2[c, r : r + 1, :] for r in range(4))

    def second_back(rows, carry):
        normed = v2[c, rows, :].astype(F32) * inverse_own + shift_own
        value = gain_own * normed + bias_own
        s = sigmoid(value)
        grad = acc[rows, :] * (s * (1.0 + value * (1.0 - s))) * mask_of(rows, ip)
        d2b[c, rows, :] = grad.astype(BF16)
        return carry[0] + fold_rows(grad), carry[1] + fold_rows(grad * normed)

    zero_ip = jnp.zeros((8, ip), F32)
    sums = over_chunks(second_back, (zero_ip, zero_ip))
    st5[d] = rows_of(total_of(sums[0]), total_of(sums[1]))
    exchange_dp("bk2", st5)
    send_part("dlt2top", d2b, top_rows)
    bias_own2, gain_own2 = sum_dp("bk2", st5)
    pm3[c] = rows_of(bias_own2 / count_ip, gain_own2 / count_ip)
    send_z("dlt2par", pm3)
    send_part("dlt2low", d2b, low_rows)
    exp_red.chips()
    sgo = v["sgo"]

    def own_second(rows):
        normed = v2[c, rows, :].astype(F32) * inverse_own + shift_own
        back = mask_of(rows, ip) * (pm3[c, 0:1, :] + normed * pm3[c, 1:2, :])
        sgo[rows, :] = (inverse_own * gain_own * (d2b[c, rows, :].astype(F32) - back)).astype(BF16)

    each_chunk(own_second)
    for tap in range(TAPS):
        spa_red.put(0, tap * ip, tn(sgo[...], cols[tap]).astype(BF16))
    spa_red.pair()
    got("wchip", wfull.at[pl.ds(0, C - 1), pl.ds(0, (Q - 1) * sz.PS)])
    for j in zpeers:
        for e in range(Q):
            send("wpair", part_of(j, 2 * e + h), part_of(j, 2 * e + h), (sibling, c))
    exp_red.chan()
    spa_red.chips()
    got_part("dlt2top", d2b, top_rows)
    got_z("dlt2par", pm3)
    got_part("dlt2low", d2b, low_rows)
    inverse2, shift2, gain2 = (table_row(pm2, r) for r in range(3))
    bias_part, gain_part = table_row(pm3, 0), table_row(pm3, 1)
    scale2 = inverse2 * gain2

    def full_second(rows):
        normed = joined(v2, rows) * inverse2 + shift2
        back = mask_of(rows, K) * (bias_part + normed * gain_part)
        big[rows, :] = (scale2 * (joined(d2b, rows) - back)).astype(BF16).astype(F32)

    each_chunk(full_second)
    fill_pad()
    exp_red.back(0)
    exp_red.back(1)
    got("wpair", wfull.at[pl.ds(0, C - 1), pl.ds(0, Q * sz.PS)])

    def adam(state, at, grad, rate, decay):
        weight, moment, square, average = (state[(part, *at)] for part in range(4))
        first = beta_one * moment + (1.0 - beta_one) * grad
        second = beta_two * square + (1.0 - beta_two) * grad * grad
        scaled = first * (1.0 / (1.0 - beta_one**STEP))
        root = jnp.sqrt(second * (1.0 / (1.0 - beta_two**STEP))) + adam_eps
        updated = weight - rate * (scaled / root + decay * weight)
        state[(0, *at)] = updated
        state[(1, *at)] = first
        state[(2, *at)] = second
        state[(3, *at)] = ema_rate * average + (1.0 - ema_rate) * updated

    def adam_rows(red, state, rate):
        for j in range(C):
            for first in range(0, ip, 32):
                n = min(32, ip - first)
                adam(state, (slice(first, first + n), slice(j * wp, (j + 1) * wp)), red.take(j, first, n), rate, decay_rate)

    fag = v["fag"]
    fag[...] = jnp.zeros_like(fag)

    def first_act_step(tap, carry):
        offset = ((2 - lax.div(tap, 3)) * PITCH + 2 - lax.rem(tap, 3)) * I
        weight = jnp.concatenate([weight_of(j, tap) for j in range(C)], axis=0)
        fag[...] += nn(shifted(offset), weight)
        return carry

    lax.fori_loop(0, TAPS // 2, first_act_step, 0)
    exp_red.other()
    lax.fori_loop(TAPS // 2, TAPS, first_act_step, 0)
    inverse1, shift1, gain1, bias1 = (table_row(pm1, r) for r in range(4))

    def first_back(rows, carry):
        normed = joined(v1, rows) * inverse1 + shift1
        value = gain1 * normed + bias1
        s = sigmoid(value)
        grad = fag[rows, :] * (s * (1.0 + value * (1.0 - s))) * mask_of(rows, K)
        fag[rows, :] = grad
        big[rows, :] = normed
        return carry[0] + fold_rows(grad), carry[1] + fold_rows(grad * normed)

    zero_k = jnp.zeros((8, K), F32)
    sums = over_chunks(first_back, (zero_k, zero_k))
    st6[d] = rows_of(total_of(sums[0]), total_of(sums[1]))
    exchange_dp("bk1", st6)
    spa_red.chan()
    for load in state_loads:
        load.wait()
    exp_red.done()
    adam_rows(exp_red, exp_state, 2.0 / math.sqrt(K))
    bias_grad1, gain_grad1 = sum_dp("bk1", st6)
    scale1 = inverse1 * gain1
    spa_red.back(0)
    fg = v["fg"]

    def first_step(rows):
        back = mask_of(rows, K) * ((bias_grad1 + big[rows, :] * gain_grad1) / count_k)
        fg[rows, :] = (scale1 * (fag[rows, :] - back)).astype(BF16)

    each_chunk(first_step)
    for j in range(C):
        red_red.put(j, 0, tn(fg[:, j * ip : (j + 1) * ip], xb[...]).astype(BF16))
    red_red.pair()
    input_grad[...] = nn(fg[...], w1r[...].reshape(K, wp)) + og[...]
    red_red.chips()

    def adam_spatial(first_tap, last_tap):
        for tap in range(first_tap, last_tap):
            for first in range(0, ip, 32):
                n = min(32, ip - first)
                adam(
                    spa_state, (tap, slice(first, first + n), slice(0, K)), spa_red.take(0, tap * ip + first, n),
                    2.0 / math.sqrt(TAPS * K), decay_rate,
                )

    red_red.chan()
    spa_red.back(1)
    spa_red.other()
    red_red.back(0)
    red_red.back(1)
    spa_red.done()
    adam_spatial(0, TAPS // 2)
    red_red.other()
    adam_spatial(TAPS // 2, TAPS)

    first_grads = own_part(jnp.concatenate([gain_grad1, bias_grad1], axis=0))
    inner_grads = [first_grads[0:1, :], gain_own2, first_grads[1:2, :], bias_own2]
    outer_grads = [gain_grad3, bias_grad3]
    inner_state[0:4, :] = inner_norm[...]
    for m in range(2):
        for r in range(2):
            inner_state[4 + 4 * m + 2 * r : 6 + 4 * m + 2 * r, :] = inner_moments[m, r]
    inner_state[12:16, :] = inner_ema[...]
    outer_state[0:2, :] = outer_norm[...]
    outer_state[2:6, :] = outer_moments[...]
    outer_state[6:8, :] = outer_ema[...]

    def adam_small(state, n, grads):
        grad = jnp.concatenate(grads, axis=0)
        weight, moment, square, average = (state[part * n : (part + 1) * n, :] for part in range(4))
        first = beta_one * moment + (1.0 - beta_one) * grad
        second = beta_two * square + (1.0 - beta_two) * grad * grad
        scaled = first * (1.0 / (1.0 - beta_one**STEP))
        root = jnp.sqrt(second * (1.0 / (1.0 - beta_two**STEP))) + adam_eps
        updated = weight - norm_rate * (scaled / root)
        state[0:n, :] = updated
        state[n : 2 * n, :] = first
        state[2 * n : 3 * n, :] = second
        state[3 * n : 4 * n, :] = ema_rate * average + (1.0 - ema_rate) * updated

    adam_small(inner_state, 4, inner_grads)
    adam_small(outer_state, 2, outer_grads)
    red_red.done()
    adam_rows(red_red, red_state, 2.0 / math.sqrt(sz.W))
    for name, ref in sent:
        wait_bytes(ref, ssem.at[sem_of[name]])


def store_kernel(n, *refs):
    held, places, sem = refs[:7], refs[7 : 7 + n], refs[-1]
    output, input_grad, red_state, spa_state, exp_state, inner_state, outer_state = held
    parts = [output.at[pl.ds(0, places[0].shape[0])], input_grad.at[pl.ds(0, places[1].shape[0])]]
    for state in (red_state, spa_state, exp_state):
        parts += [state.at[part] for part in range(4)]
    copies = [pltpu.make_async_copy(src, dst, sem.at[i]) for i, (src, dst) in enumerate(zip(parts, places))]
    for copy in copies:
        copy.start()
    inner_places, outer_places = places[14:18], places[18:22]
    for part in range(4):
        inner_places[part][...] = inner_state[part * 4 : (part + 1) * 4, :]
        outer_places[part][...] = outer_state[part * 2 : (part + 1) * 2, :]
    for copy in copies:
        copy.wait()


def per_device(
    mesh_dp, mesh_chan,
    images, groups, cotangent, reduce_weight, spatial_weight, expand_weight, inner_norm, outer_norm,
    reduce_moments, spatial_moments, expand_moments, inner_moments, outer_moments,
    reduce_ema, spatial_ema, expand_ema, inner_ema, outer_ema,
):
    sz = Sizes(mesh_dp, mesh_chan, images, reduce_weight)
    ip, wp, K, C = sz.ip, sz.wp, sz.K, sz.C

    def by_cell(a):
        return a.transpose(1, 0, 2).reshape(sz.R, wp)

    def by_tap(a):
        return a.transpose(1, 2, 0, 3).reshape(TAPS, ip, K)

    any_spec, vmem_spec = pl.BlockSpec(memory_space=pl.ANY), pl.BlockSpec(memory_space=pltpu.VMEM)
    states = []
    for weight, moments, ema in (
        (reduce_weight, reduce_moments, reduce_ema),
        (by_tap(spatial_weight), spatial_moments.transpose(0, 2, 3, 1, 4).reshape(2, TAPS, ip, K), by_tap(spatial_ema)),
        (expand_weight, expand_moments, expand_ema),
    ):
        states += [weight, moments, ema]
    held_shapes = (
        (sz.RP, wp), (sz.RP, wp), (4, ip, sz.W), (4, TAPS, ip, K), (4, ip, sz.W), (16, ip), (8, wp),
    )
    held = pl.pallas_call(
        functools.partial(block_kernel, sz),
        out_shape=tuple(pltpu.VMEM(shape, F32) for shape in held_shapes),
        in_specs=[pl.BlockSpec(memory_space=pltpu.SMEM)] + [any_spec] * 2 + [vmem_spec] * 6 + [any_spec] * 9,
        out_specs=(vmem_spec,) * len(held_shapes),
        scratch_shapes=[pltpu.VMEM(shape, dtype) for _, shape, dtype in scratch_table(sz)]
        + [
            pltpu.SemaphoreType.DMA((5,)),
            pltpu.SemaphoreType.DMA((6,)),
            pltpu.SemaphoreType.DMA((len(phases(sz)),)),
            pltpu.SemaphoreType.DMA((len(phases(sz)),)),
        ],
        compiler_params=pltpu.CompilerParams(
            collective_id=0, has_side_effects=True, vmem_limit_bytes=VMEM_TOTAL - sum(vmem_bytes(shape, F32) for shape in held_shapes)
        ),
    )(
        groups, by_cell(images), by_cell(cotangent),
        inner_norm.reshape(4, ip), outer_norm, inner_moments, outer_moments.reshape(4, wp),
        inner_ema.reshape(4, ip), outer_ema, *states,
    )
    held = [pltpu.with_memory_space_constraint(a, pltpu.VMEM) for a in held]
    shapes = [(sz.R, wp)] * 2 + [(ip, sz.W)] * 4 + [(TAPS, ip, K)] * 4 + [(ip, sz.W)] * 4
    small = [(4, ip)] * 4 + [(2, wp)] * 4
    results = pl.pallas_call(
        functools.partial(store_kernel, len(shapes + small)),
        out_shape=tuple(jax.ShapeDtypeStruct(shape, F32) for shape in shapes + small),
        in_specs=[vmem_spec] * len(held),
        out_specs=(any_spec,) * len(shapes) + (vmem_spec,) * len(small),
        scratch_shapes=[pltpu.SemaphoreType.DMA((len(shapes),))],
        compiler_params=pltpu.CompilerParams(vmem_limit_bytes=2 * 2**20),
    )(*held)
    images_of = [a.reshape(PIX, sz.I, wp).transpose(1, 0, 2) for a in results[:2]]
    taps = [a.reshape(3, 3, ip, K).transpose(2, 0, 1, 3) for a in results[6:10]]
    inner = [a.reshape(2, 2, ip) for a in results[14:18]]
    return (*images_of, *results[2:6], *taps, *results[10:14], *inner, *results[18:22])


def solution(mesh):
    placed = (
        P("dp", None, "chan"),
        P("dp"),
        P("dp", None, "chan"),
        P("chan", None),
        P("chan", None, None, None),
        P("chan", None),
        P(None, None, "chan"),
        P(None, "chan"),
        P(None, "chan", None),
        P(None, "chan", None, None, None),
        P(None, "chan", None),
        P(None, None, None, "chan"),
        P(None, None, "chan"),
        P("chan", None),
        P("chan", None, None, None),
        P("chan", None),
        P(None, None, "chan"),
        P(None, "chan"),
    )
    return jax.shard_map(
        functools.partial(per_device, mesh.shape["dp"], mesh.shape["chan"]),
        mesh=mesh,
        in_specs=placed,
        out_specs=(P("dp", None, "chan"),) * 2
        + (P("chan", None),) * 4
        + (P("chan", None, None, None),) * 4
        + (P("chan", None),) * 4
        + (P(None, None, "chan"),) * 4
        + (P(None, "chan"),) * 4,
        check_vma=False,
    )
```

```python
import functools
import math

import jax
import jax.numpy as jnp
from jax import lax
from jax.experimental import pallas as pl
from jax.experimental.pallas import tpu as pltpu
from jax.sharding import PartitionSpec as P

MESH = pl.DeviceIdType.MESH
MAP = 9
PIX = MAP * MAP
TAPS = 9
PITCH = MAP + 1
STEP = 5
LANES = 128
CHUNK = 48
CELLS_TOP = 4
VMEM_TOTAL = 62 * 2**20

norm_eps = 1e-05
adam_eps = 1e-08
beta_one = 0.5
beta_two = 0.5
decay_rate = 0.05
ema_rate = 0.75
norm_rate = 0.3

F32 = jnp.float32
BF16 = jnp.bfloat16


def round_up(value, unit):
    return -(-value // unit) * unit


class Sizes:
    def __init__(self, mesh_dp, mesh_chan, images, reduce_weight):
        self.D, self.C = mesh_dp, mesh_chan
        self.Q = self.D // 2
        self.I, _, self.wp = images.shape
        self.ip, self.W = reduce_weight.shape
        self.K = self.ip * self.C
        self.KB = self.K // LANES
        self.WB = self.wp // LANES
        self.R = PIX * self.I
        self.RS = round_up(self.R, 16)
        self.RP = round_up(self.R, CHUNK)
        self.RT = 8 * CHUNK
        self.NS = TAPS * self.ip
        self.PW = round_up(-(-self.ip // self.D), 16)
        self.PS = round_up(-(-self.NS // self.D), 16)
        self.PADROWS = ((MAP + 2) * PITCH + 2) * self.I


Z_PHASES = ["w2", "pre1", "grad2", "zexp", "zred"]
Z_PHASES += [name + part for name in ("act1", "act2", "dlt2") for part in ("top", "par", "low")]
D_PHASES = ["w2chip", "w2pair", "bn1", "bn2", "bn3", "bk3", "bk2", "bk1"]
R_PHASES = [g + s for g in ("exp", "spa", "red") for s in ("core", "chip", "back0", "back1", "pair")]


def phases(sz):
    each = [name + str(k) for name in ("w1", "w1pair", "wsp", "wchip0", "wchip1", "wpair") for k in range(sz.C - 1)]
    return Z_PHASES + D_PHASES + R_PHASES + each


def nt(a, b):
    return lax.dot_general(a, b, (((1,), (1,)), ((), ())), preferred_element_type=F32)


def nn(a, b):
    return lax.dot_general(a, b, (((1,), (0,)), ((), ())), preferred_element_type=F32)


def tn(a, b):
    return lax.dot_general(a, b, (((0,), (0,)), ((), ())), preferred_element_type=F32)


def sigmoid(v):
    return jax.nn.sigmoid(v)


def vmem_bytes(shape, dtype):
    *lead, rows, width = shape
    return math.prod(lead) * round_up(rows, 8) * round_up(width, LANES) * jnp.dtype(dtype).itemsize


def scratch_table(sz):
    C, D, Q, ip, wp, K, RP, I = sz.C, sz.D, sz.Q, sz.ip, sz.wp, sz.K, sz.RP, sz.I
    table = [
        ("xi", (sz.R, wp), BF16),
        ("coti", (sz.R, wp), BF16),
        ("mask", (RP, LANES), F32),
        ("xb", (RP, wp), BF16),
        ("cotb", (RP, wp), BF16),
        ("w1s", (C, ip, wp), BF16),
        ("w1r", (C, ip, wp), BF16),
        ("w2s", (C, D * sz.PW, wp), BF16),
        ("w2r", (C, D * sz.PW, wp), BF16),
        ("wfull", (C, D * sz.PS, K), BF16),
        ("p1s", (C, RP, ip), BF16),
        ("p1r", (C, RP, ip), BF16),
        ("v1", (C, RP, ip), BF16),
        ("v2", (C, RP, ip), BF16),
        ("d2b", (C, RP, ip), BF16),
        ("pm1", (C, 8, ip), F32),
        ("pm2", (C, 8, ip), F32),
        ("pm3", (C, 8, ip), F32),
        ("own", (C, 8, ip), F32),
        ("st1", (D, 8, ip), F32),
        ("st2", (D, 8, ip), F32),
        ("st3", (D, 8, wp), F32),
        ("st4", (D, 8, wp), F32),
        ("st5", (D, 8, ip), F32),
        ("st6", (D, 8, K), F32),
        ("acc", (RP, ip), F32),
        ("pad", (sz.PADROWS, K), F32),
        ("cols", (TAPS, RP, K), BF16),
        ("act2", (RP, K), BF16),
        ("third", (RP, wp), F32),
        ("og", (RP, wp), F32),
        ("tg", (RP, wp), BF16),
        ("big", (RP, K), F32),
        ("fag", (RP, K), F32),
        ("sgo", (RP, ip), BF16),
        ("fg", (RP, K), BF16),
    ]
    for name, z, part, width in (("exp", C, sz.PW, wp), ("spa", 1, sz.PS, K), ("red", C, sz.PW, wp)):
        table += [
            *([] if name == "red" else [
                (name + "_gs", (2, Q, z, part, width), BF16),
                (name + "_rb", (Q, z, part, width), BF16),
            ]),
            (name + "_sm", (Q, z, part, width), BF16),
            (name + "_rq", (Q, z, part, width), BF16),
            (name + "_tot", (z, part, width), BF16),
            (name + "_fin", (2, Q, z, part, width), BF16),
        ]
    return table


def block_kernel(sz, *refs):
    groups, images, cotangent, inner_norm, outer_norm, inner_moments, outer_moments, inner_ema, outer_ema = refs[:9]
    states_hbm = [refs[9:12], refs[12:15], refs[15:18]]
    output, input_grad, red_state, spa_state, exp_state, inner_state, outer_state = refs[18:25]
    table = scratch_table(sz)
    v = {name: ref for (name, _, _), ref in zip(table, refs[25:])}
    lsem, stsem, ssem, rsem = refs[25 + len(table) :]
    D, C, Q, I, K, KB, WB = sz.D, sz.C, sz.Q, sz.I, sz.K, sz.KB, sz.WB
    ip, wp, R, RS, RP = sz.ip, sz.wp, sz.R, sz.RS, sz.RP
    d = lax.axis_index("dp")
    c = lax.axis_index("chan")
    q = lax.div(d, 2)
    h = lax.rem(d, 2)
    zpeers = [lax.rem(c + k, C) for k in range(1, C)]
    dpeers = [lax.rem(d + k, D) for k in range(1, D)]
    qpeers = [lax.rem(q + k, Q) for k in range(1, Q)]
    sibling = d + 1 - 2 * h
    sem_of = {name: i for i, name in enumerate(phases(sz))}
    sent = []

    def send(name, src, dst, device):
        pltpu.make_async_remote_copy(
            src_ref=src, dst_ref=dst, send_sem=ssem.at[sem_of[name]], recv_sem=rsem.at[sem_of[name]],
            device_id=device, device_id_type=MESH,
        ).start()

    def wait_bytes(ref, sem):
        pltpu.make_async_copy(ref, ref, sem).wait()

    def got(name, ref):
        wait_bytes(ref, rsem.at[sem_of[name]])
        sent.append((name, ref))

    def sent_done(name):
        for entry in [e for e in sent if e[0] == name]:
            wait_bytes(entry[1], ssem.at[sem_of[name]])
            sent.remove(entry)

    barrier = pltpu.get_barrier_semaphore()
    for j in zpeers:
        pl.semaphore_signal(barrier, inc=1, device_id=(d, j), device_id_type=MESH)
    for e in dpeers:
        pl.semaphore_signal(barrier, inc=1, device_id=(e, c), device_id_type=MESH)

    xi, coti, mask, xb, cotb = (v[n] for n in ("xi", "coti", "mask", "xb", "cotb"))
    w1s, w1r, w2s, w2r, wfull = (v[n] for n in ("w1s", "w1r", "w2s", "w2r", "wfull"))
    w1f, wsf, w2f = red_state.at[0], spa_state.at[0], exp_state.at[0]
    loads = [
        pltpu.make_async_copy(states_hbm[0][0], w1f, lsem.at[0]),
        pltpu.make_async_copy(images, xi, lsem.at[1]),
        pltpu.make_async_copy(states_hbm[2][0], w2f, lsem.at[2]),
        pltpu.make_async_copy(states_hbm[1][0], wsf, lsem.at[3]),
        pltpu.make_async_copy(cotangent, coti, lsem.at[4]),
    ]
    for load in loads:
        load.start()
    state_loads = []
    for s, state in enumerate((red_state, spa_state, exp_state)):
        places = (state.at[pl.ds(1, 2)], state.at[3])
        for part, place in enumerate(places):
            state_loads.append(pltpu.make_async_copy(states_hbm[s][part + 1], place, stsem.at[2 * s + part]))

    def columns_of(ref, j):
        return ref[:, pl.ds(pl.multiple_of(j * wp, wp), wp)].astype(BF16)

    loads[0].wait()
    for j in zpeers:
        w1s[j] = columns_of(w1f, j)
    w1r[c] = columns_of(w1f, c)
    pl.semaphore_wait(barrier, C - 1 + D - 1)

    def half(ref, j, side):
        return ref.at[j, pl.ds(pl.multiple_of(side * (ip // 2), 16), ip // 2)]

    for k, j in enumerate(zpeers):
        send("w1" + str(k), half(w1s, j, h), half(w1r, c, h), (d, j))

    row = lax.broadcasted_iota(jnp.int32, (I, LANES), 0)
    side = jnp.zeros((I, LANES), jnp.int32)
    for i in range(I):
        side = jnp.where(row == i, 5 + 2 * groups[i], side)
    cells_here = jnp.zeros((I, LANES), F32)
    for p in range(PIX):
        inside = (side > max(p // MAP, p % MAP)).astype(F32)
        mask[p * I : (p + 1) * I, :] = inside
        cells_here = cells_here + inside
    mask[R:RP, :] = jnp.zeros((RP - R, LANES), F32)
    count_here = jnp.sum(cells_here, axis=0, keepdims=True)

    def by_rows(src, dst):
        full = R // CHUNK * CHUNK

        def step(n, carry):
            rows = pl.ds(pl.multiple_of(n * CHUNK, CHUNK), CHUNK)
            dst[rows, :] = src[rows, :]
            return carry

        lax.fori_loop(0, R // CHUNK, step, 0)
        if RP > full:
            rest = [src[full:R, :].astype(F32)] if R > full else []
            rest.append(jnp.zeros((RP - R, src.shape[1]), F32))
            dst[full:RP, :] = jnp.concatenate(rest, axis=0).astype(BF16)

    def lanes(values, width):
        if width <= LANES:
            return values[:, :width]
        return jnp.concatenate([values] * (width // LANES), axis=1)

    def mask_of(rows, width):
        return lanes(mask[rows, :], width)

    everywhere, top_part, low_part = (0, RP // CHUNK), (0, sz.RT // CHUNK), (sz.RT // CHUNK, RP // CHUNK)

    def over_chunks(body, carry=0, part=everywhere):
        def step(s, carry):
            return body(pl.ds(pl.multiple_of(s * CHUNK, CHUNK), CHUNK), carry)

        return lax.fori_loop(*part, step, carry)

    def each_chunk(body, part=everywhere):
        def step(rows, carry):
            body(rows)
            return carry

        over_chunks(step, part=part)

    def fold_rows(values):
        total = values[0:8]
        for s in range(1, values.shape[0] // 8):
            total = total + values[8 * s : 8 * s + 8]
        return total

    def total_of(values):
        return jnp.sum(values, axis=0, keepdims=True)

    def rows_of(*values):
        rest = jnp.zeros((8 - len(values), values[0].shape[1]), F32)
        return jnp.concatenate(list(values) + [rest], axis=0)

    loads[1].wait()
    by_rows(xi, xb)

    acc, p1s, p1r = v["acc"], v["p1s"], v["p1r"]
    sources = [lax.rem(c - k + C, C) for k in range(1, C)]
    for k, j in enumerate(sources):
        got("w1" + str(k), half(w1r, j, h))
        send("w1pair" + str(k), half(w1r, j, h), half(w1r, j, h), (sibling, c))
    for k, j in enumerate(sources):
        got("w1pair" + str(k), half(w1r, j, 1 - h))
        p1s[j] = nt(xb[...], w1r[j]).astype(BF16)
        send("pre1", p1s.at[j, pl.ds(0, RS)], p1r.at[c, pl.ds(0, RS)], (d, j))
    acc[...] = nt(xb[...], w1r[c])
    loads[2].wait()
    for j in zpeers:
        w2s[j, 0:ip, :] = columns_of(w2f, j)
    w2r[c, 0:ip, :] = columns_of(w2f, c)
    loads[4].wait()
    by_rows(coti, cotb)
    loads[3].wait()
    for t in range(TAPS):
        wfull[c, t * ip : (t + 1) * ip, :] = wsf[t].astype(BF16)
    for load in state_loads:
        load.start()

    def share(ref, j, e, n):
        return ref.at[j, pl.ds(pl.multiple_of(e * n, 16), n)]

    def part_of(j, e):
        return share(wfull, j, e, sz.PS)

    def fetch_spatial(k):
        send("wsp" + str(k), part_of(c, d), part_of(c, d), (d, zpeers[k]))

    cut = round_up(sz.PS // 2, 16)

    def part_side(j, e, side):
        start = pl.multiple_of(e * sz.PS + side * cut, 16)
        return wfull.at[j, pl.ds(start, cut if side == 0 else sz.PS - cut)]

    def spread_chips(k, side):
        j = sources[k]
        if side == 0:
            got("wsp" + str(k), part_of(j, d))
        for e in qpeers:
            send("wchip" + str(side) + str(k), part_side(j, d, side), part_side(j, d, side), (2 * e + h, c))

    def spread_pair(k):
        j = sources[k]
        got("wchip0" + str(k), wfull.at[j, pl.ds(0, (Q - 1) * cut)])
        got("wchip1" + str(k), wfull.at[j, pl.ds(0, (Q - 1) * (sz.PS - cut))])
        for e in range(Q):
            send("wpair" + str(k), part_of(j, 2 * e + h), part_of(j, 2 * e + h), (sibling, c))

    def spread_done(k):
        got("wpair" + str(k), wfull.at[0, pl.ds(0, Q * sz.PS)])

    late = list(reversed(range(1, C - 1)))

    def add_partials(name, recv):
        got(name, recv.at[pl.ds(0, C - 1), pl.ds(0, RS)])
        for j in zpeers:
            acc[0:RS, :] += recv[j, 0:RS, :].astype(F32)

    add_partials("pre1", p1r)

    def moments(src, width):
        def sums(rows, carry):
            return carry + fold_rows(src[rows, :] * mask_of(rows, width))

        mean = total_of(over_chunks(sums, jnp.zeros((8, width), F32))) / lanes(count_here, width)

        def squares(rows, carry):
            centered = src[rows, :] - mean
            return carry + fold_rows(mask_of(rows, width) * centered * centered)

        return mean, total_of(over_chunks(squares, jnp.zeros((8, width), F32)))

    def exchange_dp(name, table):
        for e in dpeers:
            send(name, table.at[d], table.at[d], (e, c))

    def combine(name, table):
        got(name, table.at[pl.ds(0, D - 1)])
        count = table[0, 2:3, :]
        average = count * table[0, 0:1, :]
        for e in range(1, D):
            count = count + table[e, 2:3, :]
            average = average + table[e, 2:3, :] * table[e, 0:1, :]
        average = average / count
        variance = jnp.zeros_like(average)
        for e in range(D):
            off = table[e, 0:1, :] - average
            variance = variance + (table[e, 1:2, :] + table[e, 2:3, :] * off * off)
        return average, lax.rsqrt(variance / count + norm_eps), count

    def sum_dp(name, table):
        got(name, table.at[pl.ds(0, D - 1)])
        total = table[0]
        for e in range(1, D):
            total = total + table[e]
        return total[0:1, :], total[1:2, :]

    def send_z(name, ref, rows=None):
        part = ref.at[c] if rows is None else ref.at[c, pl.ds(0, rows)]
        for j in zpeers:
            send(name, part, part, (d, j))

    def got_z(name, ref, rows=None):
        got(name, ref.at[pl.ds(0, C - 1)] if rows is None else ref.at[pl.ds(0, C - 1), pl.ds(0, rows)])

    def joined(blocks, rows):
        return jnp.concatenate([blocks[j, rows, :].astype(F32) for j in range(C)], axis=1)

    def table_row(par, r):
        return jnp.concatenate([par[j, r : r + 1, :] for j in range(C)], axis=1)

    def own_part(values):
        own = v["own"]
        for j in range(C):
            own[j, 0 : values.shape[0], :] = values[:, j * ip : (j + 1) * ip]
        return own[c, 0 : values.shape[0], :]

    top_rows, low_rows = pl.ds(0, sz.RT), pl.ds(sz.RT, RS - sz.RT)

    def send_part(name, held, rows):
        for j in zpeers:
            send(name, held.at[c, rows], held.at[c, rows], (d, j))

    def got_part(name, held, rows):
        got(name, held.at[pl.ds(0, C - 1), rows])

    def inner_forward(layer, bn, table, held, name, par, top_work, low_work, meanwhile=lambda: None):
        mean, spread = moments(acc, ip)
        table[d] = rows_of(mean, spread, lanes(count_here, ip))
        exchange_dp(bn, table)

        def center(rows):
            held[c, rows, :] = ((acc[rows, :] - mean) * mask_of(rows, ip)).astype(BF16)

        each_chunk(center)
        send_part(name + "top", held, top_rows)
        average, inverse, count = combine(bn, table)
        par[c] = rows_of(
            inverse, (mean - average) * inverse,
            inner_norm[layer : layer + 1, :], inner_norm[2 + layer : 3 + layer, :],
        )
        send_z(name + "par", par)
        send_part(name + "low", held, low_rows)
        meanwhile()
        got_part(name + "top", held, top_rows)
        got_z(name + "par", par)
        top_work()
        got_part(name + "low", held, low_rows)
        low_work()
        return count

    v1, v2, d2b, pm1, pm2, pm3 = (v[n] for n in ("v1", "v2", "d2b", "pm1", "pm2", "pm3"))
    for j in range(C):
        for ref in (v1, v2, d2b):
            ref[j, RS:RP, :] = jnp.zeros((RP - RS, ip), BF16)
    def make_act(held, par, dst, part):
        inverse, shift, gain, bias = (table_row(par, r) for r in range(4))

        def step(rows):
            value = gain * (joined(held, rows) * inverse + shift) + bias
            dst[rows, :] = (value * sigmoid(value) * mask_of(rows, K)).astype(dst.dtype)

        each_chunk(step, part)

    big, pad, cols = v["big"], v["pad"], v["cols"]
    pad[...] = jnp.zeros_like(pad)
    top_cells, low_cells = range(CELLS_TOP + 1), range(CELLS_TOP + 1, MAP)
    top_out, low_out = range(CELLS_TOP), range(CELLS_TOP, MAP)

    def fill_pad(cells):
        for y in cells:
            start = ((y + 1) * PITCH + 1) * I
            pad[start : start + MAP * I, :] = big[y * MAP * I : (y + 1) * MAP * I, :]

    def out_rows(cells):
        return slice(0, CELLS_TOP * MAP * I) if cells is top_out else slice(CELLS_TOP * MAP * I, RP)

    def shifted(offset, cells):
        pieces = [pad[pl.ds(pl.multiple_of(offset + y * PITCH * I, I), MAP * I), :] for y in cells]
        if cells is low_out:
            pieces.append(jnp.zeros((RP - R, K), F32))
        return jnp.concatenate(pieces, axis=0).astype(BF16)

    def weight_of(j, tap):
        return wfull[j, pl.ds(pl.multiple_of(tap * ip, ip), ip), :]

    def second_conv(cells):
        rows = out_rows(cells)
        acc[rows, :] = jnp.zeros((rows.stop - rows.start, ip), F32)

        def second_step(tap, carry):
            cols[tap, rows, :] = shifted((lax.div(tap, 3) * PITCH + lax.rem(tap, 3)) * I, cells)
            acc[rows, :] += nt(cols[tap, rows, :], weight_of(c, tap))
            return carry

        lax.fori_loop(0, TAPS, second_step, 0)

    def first_top():
        make_act(v1, pm1, big, top_part)
        fill_pad(top_cells)
        second_conv(top_out)

    def first_low():
        for j in zpeers:
            send("w2", share(w2s, j, d, sz.PW), share(w2r, c, d, sz.PW), (d, j))
        fetch_spatial(0)
        make_act(v1, pm1, big, low_part)
        fill_pad(low_cells)
        second_conv(low_out)

    count_ip = inner_forward(0, "bn1", v["st1"], v1, "act1", pm1, first_top, first_low)
    count_k = lanes(lanes(count_ip, min(ip, LANES))[:, 0:1] + jnp.zeros((1, LANES), F32), K)

    def hand_on():
        got("w2", w2r.at[pl.ds(0, C - 1), pl.ds(0, sz.PW)])
        for j in zpeers:
            for e in qpeers:
                send("w2chip", share(w2r, j, d, sz.PW), share(w2r, j, d, sz.PW), (2 * e + h, c))
        spread_chips(0, 0)
        spread_chips(0, 1)
        got("w2chip", w2r.at[pl.ds(0, C - 1), pl.ds(0, (Q - 1) * sz.PW)])
        for j in zpeers:
            for e in range(Q):
                send("w2pair", share(w2r, j, 2 * e + h, sz.PW), share(w2r, j, 2 * e + h, sz.PW), (sibling, c))
        spread_pair(0)

    act2 = v["act2"]
    third, og, tg = v["third"], v["og"], v["tg"]

    def third_conv(part):
        make_act(v2, pm2, act2, part)
        rows = slice(part[0] * CHUNK, part[1] * CHUNK)
        third[rows, :] = nn(act2[rows, :], jnp.concatenate([w2r[j, 0:ip, :] for j in range(C)], axis=0))

    def second_top():
        got("w2pair", w2r.at[pl.ds(0, C - 1), pl.ds(0, Q * sz.PW)])
        third_conv(top_part)

    def second_low():
        for k in late:
            fetch_spatial(k)
        third_conv(low_part)

    inner_forward(1, "bn2", v["st2"], v2, "act2", pm2, second_top, second_low, hand_on)
    mean3, spread3 = moments(third, wp)
    st3, st4, st5, st6 = v["st3"], v["st4"], v["st5"], v["st6"]
    st3[d] = rows_of(mean3, spread3, lanes(count_here, wp))
    exchange_dp("bn3", st3)
    average3, inverse3, count_wp = combine("bn3", st3)
    gain3, bias3 = outer_norm[0:1, :], outer_norm[1:2, :]

    def last_step(rows, carry):
        m = mask_of(rows, wp)
        normed = (third[rows, :] - average3) * inverse3
        third[rows, :] = normed
        summed = gain3 * normed + bias3 + xb[rows, :].astype(F32)
        s = sigmoid(summed)
        here = summed * s * m
        output[rows, :] = here
        grad = cotb[rows, :].astype(F32) * (s * (1.0 + summed * (1.0 - s))) * m
        og[rows, :] = grad
        return carry[0] + fold_rows(grad), carry[1] + fold_rows(grad * normed)

    zero_wp = jnp.zeros((8, wp), F32)
    sums = over_chunks(last_step, (zero_wp, zero_wp))
    st4[d] = rows_of(total_of(sums[0]), total_of(sums[1]))
    exchange_dp("bk3", st4)
    bias_grad3, gain_grad3 = sum_dp("bk3", st4)
    scale3 = inverse3 * gain3

    def third_step(rows):
        back = mask_of(rows, wp) * ((bias_grad3 + third[rows, :] * gain_grad3) / count_wp)
        tg[rows, :] = (scale3 * (og[rows, :] - back)).astype(BF16)

    each_chunk(third_step)

    p2s, p2r = p1s, p1r
    sent_done("pre1")
    for k in range(1, C):
        j = lax.rem(c - k + C, C)
        p2s[j] = nt(tg[...], w2r[j, 0:ip, :]).astype(BF16)
        send("grad2", p2s.at[j, pl.ds(0, RS)], p2r.at[c, pl.ds(0, RS)], (d, j))
    for k in late:
        spread_chips(k, 0)
        if k > 1:
            spread_chips(k, 1)
    acc[...] = nt(tg[...], w2r[c, 0:ip, :])

    class Reduction:
        def __init__(self, name, z, part):
            self.name, self.z, self.part = name, z, part
            self.gs, self.rb, self.sm, self.rq, self.tot, self.fin = (
                v[("exp" if name == "red" and s in ("gs", "rb") else name) + "_" + s]
                for s in ("gs", "rb", "sm", "rq", "tot", "fin")
            )

        def pieces(self, first, rows):
            row, end = first, first + rows
            while row < end:
                owner = row // self.part
                stop = min(end, (owner + 1) * self.part)
                yield owner, row - owner * self.part, row - first, stop - row
                row = stop

        def put(self, zi, first, value):
            for owner, there, here, n in self.pieces(first, value.shape[0]):
                self.gs[owner % 2, owner // 2, zi, there : there + n, :] = value[here : here + n, :]

        def take(self, zi, first, rows):
            found = [
                self.fin[owner % 2, owner // 2, zi, there : there + n, :].astype(F32)
                for owner, there, _, n in self.pieces(first, rows)
            ]
            return jnp.concatenate(found, axis=0)

        def pair(self):
            send(self.name + "core", self.gs.at[1 - h], self.rb, (sibling, c))

        def chips(self):
            got(self.name + "core", self.rb)
            for e in range(Q):
                self.sm[e] = (self.gs[h, e].astype(F32) + self.rb[e].astype(F32)).astype(BF16)
            for e in qpeers:
                send(self.name + "chip", self.sm.at[e], self.rq.at[q], (2 * e + h, c))

        def chan(self):
            got(self.name + "chip", self.rq.at[pl.ds(0, Q - 1)])
            total = self.sm[q].astype(F32)
            for e in qpeers:
                total = total + self.rq[e].astype(F32)
            self.tot[...] = total.astype(BF16)
            if self.z == 1:
                self.fin[h, q, 0] = self.tot[0]
            else:
                self.fin[h, q, c] = self.tot[c]
                for j in zpeers:
                    send("z" + self.name, self.tot.at[j], self.fin.at[h, q, c], (d, j))

        def halves(self, side, other):
            cut = round_up(self.part // 2, 16)
            rows = pl.ds(0, cut) if side == 0 else pl.ds(cut, self.part - cut)
            return self.fin.at[h, other, slice(None), rows]

        def back(self, side):
            if side == 0 and self.z > 1:
                got("z" + self.name, self.fin.at[h, q, pl.ds(0, C - 1)])
            if side == 1 and self.part <= 16:
                return
            for e in qpeers:
                send(self.name + "back" + str(side), self.halves(side, q), self.halves(side, q), (2 * e + h, c))

        def other(self):
            cut = round_up(self.part // 2, 16)
            got(self.name + "back0", self.fin.at[h, pl.ds(0, Q - 1), slice(None), pl.ds(0, cut)])
            if self.part > 16:
                got(self.name + "back1", self.fin.at[h, pl.ds(0, Q - 1), slice(None), pl.ds(cut, self.part - cut)])
            send(self.name + "pair", self.fin.at[h], self.fin.at[h], (sibling, c))

        def done(self):
            got(self.name + "pair", self.fin.at[0])

    def adam(state, at, grad, rate, decay):
        weight, moment, square, average = (state[(part, *at)] for part in range(4))
        first = beta_one * moment + (1.0 - beta_one) * grad
        second = beta_two * square + (1.0 - beta_two) * grad * grad
        scaled = first * (1.0 / (1.0 - beta_one**STEP))
        root = jnp.sqrt(second * (1.0 / (1.0 - beta_two**STEP))) + adam_eps
        updated = weight - rate * (scaled / root + decay * weight)
        state[(0, *at)] = updated
        state[(1, *at)] = first
        state[(2, *at)] = second
        state[(3, *at)] = ema_rate * average + (1.0 - ema_rate) * updated

    def adam_rows(red, state, rate):
        for j in range(C):
            for first in range(0, ip, 32):
                n = min(32, ip - first)
                adam(state, (slice(first, first + n), slice(j * wp, (j + 1) * wp)), red.take(j, first, n), rate, decay_rate)

    exp_red = Reduction("exp", C, sz.PW)
    spa_red = Reduction("spa", 1, sz.PS)
    red_red = Reduction("red", C, sz.PW)
    for j in range(C):
        exp_red.put(j, 0, tn(act2[:, j * ip : (j + 1) * ip], tg[...]).astype(BF16))
    exp_red.pair()

    exp_red.chips()
    for k in late[:-1]:
        spread_pair(k)
    exp_red.chan()
    add_partials("grad2", p2r)
    inverse_own, shift_own, gain_own, bias_own = (pm2[c, r : r + 1, :] for r in range(4))

    def second_back(rows, carry):
        normed = v2[c, rows, :].astype(F32) * inverse_own + shift_own
        value = gain_own * normed + bias_own
        s = sigmoid(value)
        grad = acc[rows, :] * (s * (1.0 + value * (1.0 - s))) * mask_of(rows, ip)
        d2b[c, rows, :] = grad.astype(BF16)
        return carry[0] + fold_rows(grad), carry[1] + fold_rows(grad * normed)

    zero_ip = jnp.zeros((8, ip), F32)
    sums = over_chunks(second_back, (zero_ip, zero_ip))
    st5[d] = rows_of(total_of(sums[0]), total_of(sums[1]))
    exchange_dp("bk2", st5)
    send_part("dlt2top", d2b, top_rows)
    bias_own2, gain_own2 = sum_dp("bk2", st5)
    pm3[c] = rows_of(bias_own2 / count_ip, gain_own2 / count_ip)
    send_z("dlt2par", pm3)
    send_part("dlt2low", d2b, low_rows)
    for k in late[-1:]:
        spread_chips(k, 1)
    exp_red.back(0)
    exp_red.back(1)
    sgo = v["sgo"]

    def own_second(rows):
        normed = v2[c, rows, :].astype(F32) * inverse_own + shift_own
        back = mask_of(rows, ip) * (pm3[c, 0:1, :] + normed * pm3[c, 1:2, :])
        sgo[rows, :] = (inverse_own * gain_own * (d2b[c, rows, :].astype(F32) - back)).astype(BF16)

    each_chunk(own_second)
    for tap in range(TAPS):
        spa_red.put(0, tap * ip, tn(sgo[...], cols[tap]).astype(BF16))
    spa_red.pair()
    for k in late[-1:]:
        spread_pair(k)
    exp_red.other()
    spa_red.chips()
    for load in state_loads:
        load.wait()
    exp_red.done()
    adam_rows(exp_red, exp_state, 2.0 / math.sqrt(K))
    fag = v["fag"]
    inverse2, shift2, gain2 = (table_row(pm2, r) for r in range(3))
    scale2 = inverse2 * gain2

    def full_second(part):
        bias_part, gain_part = table_row(pm3, 0), table_row(pm3, 1)

        def step(rows):
            normed = joined(v2, rows) * inverse2 + shift2
            back = mask_of(rows, K) * (bias_part + normed * gain_part)
            big[rows, :] = (scale2 * (joined(d2b, rows) - back)).astype(BF16).astype(F32)

        each_chunk(step, part)

    def first_act_grad(cells, first, last):
        rows = out_rows(cells)
        if first == 0:
            fag[rows, :] = jnp.zeros((rows.stop - rows.start, K), F32)

        def step(tap, carry):
            offset = ((2 - lax.div(tap, 3)) * PITCH + 2 - lax.rem(tap, 3)) * I
            weight = jnp.concatenate([weight_of(j, tap) for j in range(C)], axis=0)
            fag[rows, :] += nn(shifted(offset, cells), weight)
            return carry

        lax.fori_loop(first, last, step, 0)

    got_part("dlt2top", d2b, top_rows)
    got_z("dlt2par", pm3)
    full_second(top_part)
    fill_pad(top_cells)
    for k in range(C - 1):
        spread_done(k)
    first_act_grad(top_out, 0, TAPS)
    got_part("dlt2low", d2b, low_rows)
    full_second(low_part)
    fill_pad(low_cells)
    first_act_grad(low_out, 0, TAPS)

    inverse1, shift1, gain1, bias1 = (table_row(pm1, r) for r in range(4))

    def first_back(rows, carry):
        normed = joined(v1, rows) * inverse1 + shift1
        value = gain1 * normed + bias1
        s = sigmoid(value)
        grad = fag[rows, :] * (s * (1.0 + value * (1.0 - s))) * mask_of(rows, K)
        fag[rows, :] = grad
        big[rows, :] = normed
        return carry[0] + fold_rows(grad), carry[1] + fold_rows(grad * normed)

    zero_k = jnp.zeros((8, K), F32)
    sums = over_chunks(first_back, (zero_k, zero_k))
    st6[d] = rows_of(total_of(sums[0]), total_of(sums[1]))
    exchange_dp("bk1", st6)
    spa_red.chan()
    bias_grad1, gain_grad1 = sum_dp("bk1", st6)
    spa_red.back(0)
    scale1 = inverse1 * gain1
    fg = v["fg"]

    def first_step(rows):
        back = mask_of(rows, K) * ((bias_grad1 + big[rows, :] * gain_grad1) / count_k)
        fg[rows, :] = (scale1 * (fag[rows, :] - back)).astype(BF16)

    each_chunk(first_step)
    sent_done("expcore")
    for j in range(C):
        red_red.put(j, 0, tn(fg[:, j * ip : (j + 1) * ip], xb[...]).astype(BF16))
    red_red.pair()
    input_grad[...] = nn(fg[...], w1r[...].reshape(K, wp)) + og[...]
    red_red.chips()

    def adam_spatial(first_tap, last_tap):
        for tap in range(first_tap, last_tap):
            for first in range(0, ip, 32):
                n = min(32, ip - first)
                adam(
                    spa_state, (tap, slice(first, first + n), slice(0, K)), spa_red.take(0, tap * ip + first, n),
                    2.0 / math.sqrt(TAPS * K), decay_rate,
                )

    red_red.chan()
    spa_red.back(1)
    spa_red.other()
    red_red.back(0)
    red_red.back(1)
    spa_red.done()
    adam_spatial(0, TAPS // 2)
    red_red.other()
    adam_spatial(TAPS // 2, TAPS)

    first_grads = own_part(jnp.concatenate([gain_grad1, bias_grad1], axis=0))
    inner_grads = [first_grads[0:1, :], gain_own2, first_grads[1:2, :], bias_own2]
    outer_grads = [gain_grad3, bias_grad3]
    inner_state[0:4, :] = inner_norm[...]
    for m in range(2):
        for r in range(2):
            inner_state[4 + 4 * m + 2 * r : 6 + 4 * m + 2 * r, :] = inner_moments[m, r]
    inner_state[12:16, :] = inner_ema[...]
    outer_state[0:2, :] = outer_norm[...]
    outer_state[2:6, :] = outer_moments[...]
    outer_state[6:8, :] = outer_ema[...]

    def adam_small(state, n, grads):
        grad = jnp.concatenate(grads, axis=0)
        weight, moment, square, average = (state[part * n : (part + 1) * n, :] for part in range(4))
        first = beta_one * moment + (1.0 - beta_one) * grad
        second = beta_two * square + (1.0 - beta_two) * grad * grad
        scaled = first * (1.0 / (1.0 - beta_one**STEP))
        root = jnp.sqrt(second * (1.0 / (1.0 - beta_two**STEP))) + adam_eps
        updated = weight - norm_rate * (scaled / root)
        state[0:n, :] = updated
        state[n : 2 * n, :] = first
        state[2 * n : 3 * n, :] = second
        state[3 * n : 4 * n, :] = ema_rate * average + (1.0 - ema_rate) * updated

    adam_small(inner_state, 4, inner_grads)
    adam_small(outer_state, 2, outer_grads)
    red_red.done()
    adam_rows(red_red, red_state, 2.0 / math.sqrt(sz.W))
    for name, ref in sent:
        wait_bytes(ref, ssem.at[sem_of[name]])


def store_kernel(n, *refs):
    held, places, sem = refs[:7], refs[7 : 7 + n], refs[-1]
    output, input_grad, red_state, spa_state, exp_state, inner_state, outer_state = held
    parts = [output.at[pl.ds(0, places[0].shape[0])], input_grad.at[pl.ds(0, places[1].shape[0])]]
    for state in (red_state, spa_state, exp_state):
        parts += [state.at[part] for part in range(4)]
    copies = [pltpu.make_async_copy(src, dst, sem.at[i]) for i, (src, dst) in enumerate(zip(parts, places))]
    for copy in copies:
        copy.start()
    inner_places, outer_places = places[14:18], places[18:22]
    for part in range(4):
        inner_places[part][...] = inner_state[part * 4 : (part + 1) * 4, :]
        outer_places[part][...] = outer_state[part * 2 : (part + 1) * 2, :]
    for copy in copies:
        copy.wait()


def per_device(
    mesh_dp, mesh_chan,
    images, groups, cotangent, reduce_weight, spatial_weight, expand_weight, inner_norm, outer_norm,
    reduce_moments, spatial_moments, expand_moments, inner_moments, outer_moments,
    reduce_ema, spatial_ema, expand_ema, inner_ema, outer_ema,
):
    sz = Sizes(mesh_dp, mesh_chan, images, reduce_weight)
    ip, wp, K, C = sz.ip, sz.wp, sz.K, sz.C

    def by_cell(a):
        return a.transpose(1, 0, 2).reshape(sz.R, wp)

    def by_tap(a):
        return a.transpose(1, 2, 0, 3).reshape(TAPS, ip, K)

    any_spec, vmem_spec = pl.BlockSpec(memory_space=pl.ANY), pl.BlockSpec(memory_space=pltpu.VMEM)
    states = []
    for weight, moments, ema in (
        (reduce_weight, reduce_moments, reduce_ema),
        (by_tap(spatial_weight), spatial_moments.transpose(0, 2, 3, 1, 4).reshape(2, TAPS, ip, K), by_tap(spatial_ema)),
        (expand_weight, expand_moments, expand_ema),
    ):
        states += [weight, moments, ema]
    held_shapes = (
        (sz.RP, wp), (sz.RP, wp), (4, ip, sz.W), (4, TAPS, ip, K), (4, ip, sz.W), (16, ip), (8, wp),
    )
    held = pl.pallas_call(
        functools.partial(block_kernel, sz),
        out_shape=tuple(pltpu.VMEM(shape, F32) for shape in held_shapes),
        in_specs=[pl.BlockSpec(memory_space=pltpu.SMEM)] + [any_spec] * 2 + [vmem_spec] * 6 + [any_spec] * 9,
        out_specs=(vmem_spec,) * len(held_shapes),
        scratch_shapes=[pltpu.VMEM(shape, dtype) for _, shape, dtype in scratch_table(sz)]
        + [
            pltpu.SemaphoreType.DMA((5,)),
            pltpu.SemaphoreType.DMA((6,)),
            pltpu.SemaphoreType.DMA((len(phases(sz)),)),
            pltpu.SemaphoreType.DMA((len(phases(sz)),)),
        ],
        compiler_params=pltpu.CompilerParams(
            collective_id=0, has_side_effects=True, vmem_limit_bytes=VMEM_TOTAL - sum(vmem_bytes(shape, F32) for shape in held_shapes)
        ),
    )(
        groups, by_cell(images), by_cell(cotangent),
        inner_norm.reshape(4, ip), outer_norm, inner_moments, outer_moments.reshape(4, wp),
        inner_ema.reshape(4, ip), outer_ema, *states,
    )
    held = [pltpu.with_memory_space_constraint(a, pltpu.VMEM) for a in held]
    shapes = [(sz.R, wp)] * 2 + [(ip, sz.W)] * 4 + [(TAPS, ip, K)] * 4 + [(ip, sz.W)] * 4
    small = [(4, ip)] * 4 + [(2, wp)] * 4
    results = pl.pallas_call(
        functools.partial(store_kernel, len(shapes + small)),
        out_shape=tuple(jax.ShapeDtypeStruct(shape, F32) for shape in shapes + small),
        in_specs=[vmem_spec] * len(held),
        out_specs=(any_spec,) * len(shapes) + (vmem_spec,) * len(small),
        scratch_shapes=[pltpu.SemaphoreType.DMA((len(shapes),))],
        compiler_params=pltpu.CompilerParams(vmem_limit_bytes=2 * 2**20),
    )(*held)
    images_of = [a.reshape(PIX, sz.I, wp).transpose(1, 0, 2) for a in results[:2]]
    taps = [a.reshape(3, 3, ip, K).transpose(2, 0, 1, 3) for a in results[6:10]]
    inner = [a.reshape(2, 2, ip) for a in results[14:18]]
    return (*images_of, *results[2:6], *taps, *results[10:14], *inner, *results[18:22])


def solution(mesh):
    placed = (
        P("dp", None, "chan"),
        P("dp"),
        P("dp", None, "chan"),
        P("chan", None),
        P("chan", None, None, None),
        P("chan", None),
        P(None, None, "chan"),
        P(None, "chan"),
        P(None, "chan", None),
        P(None, "chan", None, None, None),
        P(None, "chan", None),
        P(None, None, None, "chan"),
        P(None, None, "chan"),
        P("chan", None),
        P("chan", None, None, None),
        P("chan", None),
        P(None, None, "chan"),
        P(None, "chan"),
    )
    return jax.shard_map(
        functools.partial(per_device, mesh.shape["dp"], mesh.shape["chan"]),
        mesh=mesh,
        in_specs=placed,
        out_specs=(P("dp", None, "chan"),) * 2
        + (P("chan", None),) * 4
        + (P("chan", None, None, None),) * 4
        + (P("chan", None),) * 4
        + (P(None, None, "chan"),) * 4
        + (P(None, "chan"),) * 4,
        check_vma=False,
    )
```

```python
import functools
import math

import jax
import jax.numpy as jnp
from jax import lax
from jax.experimental import pallas as pl
from jax.experimental.pallas import tpu as pltpu
from jax.sharding import PartitionSpec as P

MESH = pl.DeviceIdType.MESH
MAP = 9
PIX = MAP * MAP
TAPS = 9
PITCH = MAP + 1
STEP = 5
LANES = 128
CHUNK = 48
CELLS_TOP = 2
VMEM_TOTAL = 62 * 2**20

norm_eps = 1e-05
adam_eps = 1e-08
beta_one = 0.5
beta_two = 0.5
decay_rate = 0.05
ema_rate = 0.75
norm_rate = 0.3

F32 = jnp.float32
BF16 = jnp.bfloat16


def round_up(value, unit):
    return -(-value // unit) * unit


class Sizes:
    def __init__(self, mesh_dp, mesh_chan, images, reduce_weight):
        self.D, self.C = mesh_dp, mesh_chan
        self.Q = self.D // 2
        self.I, _, self.wp = images.shape
        self.ip, self.W = reduce_weight.shape
        self.K = self.ip * self.C
        self.KB = self.K // LANES
        self.WB = self.wp // LANES
        self.R = PIX * self.I
        self.RS = round_up(self.R, 16)
        self.RP = round_up(self.R, CHUNK)
        self.RT = 6 * CHUNK
        self.NS = TAPS * self.ip
        self.PW = round_up(-(-self.ip // self.D), 16)
        self.PS = round_up(-(-self.NS // self.D), 16)
        self.PADROWS = ((MAP + 2) * PITCH + 2) * self.I


Z_PHASES = ["w2", "pre1", "grad2", "zexp", "zred"]
Z_PHASES += [name + part for name in ("act1", "act2", "dlt2") for part in ("top", "par", "low")]
D_PHASES = ["w2chip", "w2pair", "bn1", "bn2", "bn3", "bk3", "bk2", "bk1"]
R_PHASES = [g + s for g in ("exp", "spa", "red") for s in ("core", "chip", "back0", "back1", "pair")]


def phases(sz):
    each = [name + str(k) for name in ("w1", "w1pair", "wsp", "wchip0", "wchip1", "wpair") for k in range(sz.C - 1)]
    return Z_PHASES + D_PHASES + R_PHASES + each


def nt(a, b):
    return lax.dot_general(a, b, (((1,), (1,)), ((), ())), preferred_element_type=F32)


def nn(a, b):
    return lax.dot_general(a, b, (((1,), (0,)), ((), ())), preferred_element_type=F32)


def tn(a, b):
    return lax.dot_general(a, b, (((0,), (0,)), ((), ())), preferred_element_type=F32)


def sigmoid(v):
    return jax.nn.sigmoid(v)


def vmem_bytes(shape, dtype):
    *lead, rows, width = shape
    return math.prod(lead) * round_up(rows, 8) * round_up(width, LANES) * jnp.dtype(dtype).itemsize


def scratch_table(sz):
    C, D, Q, ip, wp, K, RP, I = sz.C, sz.D, sz.Q, sz.ip, sz.wp, sz.K, sz.RP, sz.I
    table = [
        ("xi", (sz.R, wp), BF16),
        ("coti", (sz.R, wp), BF16),
        ("mask", (RP, LANES), F32),
        ("xb", (RP, wp), BF16),
        ("cotb", (RP, wp), BF16),
        ("w1s", (C, ip, wp), BF16),
        ("w1r", (C, ip, wp), BF16),
        ("w2s", (C, D * sz.PW, wp), BF16),
        ("w2r", (C, D * sz.PW, wp), BF16),
        ("wfull", (C, D * sz.PS, K), BF16),
        ("p1s", (C, RP, ip), BF16),
        ("p1r", (C, RP, ip), BF16),
        ("v1", (C, RP, ip), BF16),
        ("v2", (C, RP, ip), BF16),
        ("d2b", (C, RP, ip), BF16),
        ("pm1", (C, 8, ip), F32),
        ("pm2", (C, 8, ip), F32),
        ("pm3", (C, 8, ip), F32),
        ("own", (C, 8, ip), F32),
        ("st1", (D, 8, ip), F32),
        ("st2", (D, 8, ip), F32),
        ("st3", (D, 4, wp), F32),
        ("st4", (D, 4, wp), F32),
        ("st5", (D, 8, ip), F32),
        ("st6", (D, 4, K), F32),
        ("acc", (RP, ip), F32),
        ("pad", (sz.PADROWS, K), F32),
        ("cols", (TAPS, RP, K), BF16),
        ("act2", (RP, K), BF16),
        ("third", (RP, wp), F32),
        ("og", (RP, wp), F32),
        ("tg", (RP, wp), BF16),
        ("big", (RP, K), F32),
        ("fag", (RP, K), F32),
        ("sgo", (RP, ip), BF16),
        ("fg", (RP, K), BF16),
    ]
    for name, z, part, width in (("exp", C, sz.PW, wp), ("spa", 1, sz.PS, K), ("red", C, sz.PW, wp)):
        table += [
            *([] if name == "red" else [
                (name + "_gs", (2, Q, z, part, width), BF16),
                (name + "_rb", (Q, z, part, width), BF16),
            ]),
            (name + "_sm", (Q, z, part, width), BF16),
            (name + "_rq", (Q, z, part, width), BF16),
            (name + "_tot", (z, part, width), BF16),
            (name + "_fin", (2, Q, z, part, width), BF16),
        ]
    return table


def block_kernel(sz, *refs):
    groups, images, cotangent, inner_norm, outer_norm, inner_moments, outer_moments, inner_ema, outer_ema = refs[:9]
    states_hbm = [refs[9:12], refs[12:15], refs[15:18]]
    output, input_grad, red_state, spa_state, exp_state, inner_state, outer_state = refs[18:25]
    table = scratch_table(sz)
    v = {name: ref for (name, _, _), ref in zip(table, refs[25:])}
    lsem, stsem, ssem, rsem = refs[25 + len(table) :]
    D, C, Q, I, K, KB, WB = sz.D, sz.C, sz.Q, sz.I, sz.K, sz.KB, sz.WB
    ip, wp, R, RS, RP = sz.ip, sz.wp, sz.R, sz.RS, sz.RP
    d = lax.axis_index("dp")
    c = lax.axis_index("chan")
    q = lax.div(d, 2)
    h = lax.rem(d, 2)
    zpeers = [lax.rem(c + k, C) for k in range(1, C)]
    dpeers = [lax.rem(d + k, D) for k in range(1, D)]
    qpeers = [lax.rem(q + k, Q) for k in range(1, Q)]
    sibling = d + 1 - 2 * h
    sem_of = {name: i for i, name in enumerate(phases(sz))}
    sent = []

    def send(name, src, dst, device):
        pltpu.make_async_remote_copy(
            src_ref=src, dst_ref=dst, send_sem=ssem.at[sem_of[name]], recv_sem=rsem.at[sem_of[name]],
            device_id=device, device_id_type=MESH,
        ).start()

    def wait_bytes(ref, sem):
        pltpu.make_async_copy(ref, ref, sem).wait()

    def got(name, ref):
        wait_bytes(ref, rsem.at[sem_of[name]])
        sent.append((name, ref))

    def sent_done(name):
        for entry in [e for e in sent if e[0] == name]:
            wait_bytes(entry[1], ssem.at[sem_of[name]])
            sent.remove(entry)

    barrier = pltpu.get_barrier_semaphore()
    for j in zpeers:
        pl.semaphore_signal(barrier, inc=1, device_id=(d, j), device_id_type=MESH)
    for e in dpeers:
        pl.semaphore_signal(barrier, inc=1, device_id=(e, c), device_id_type=MESH)

    xi, coti, mask, xb, cotb = (v[n] for n in ("xi", "coti", "mask", "xb", "cotb"))
    w1s, w1r, w2s, w2r, wfull = (v[n] for n in ("w1s", "w1r", "w2s", "w2r", "wfull"))
    w1f, wsf, w2f = red_state.at[0], spa_state.at[0], exp_state.at[0]
    loads = [
        pltpu.make_async_copy(states_hbm[0][0], w1f, lsem.at[0]),
        pltpu.make_async_copy(images, xi, lsem.at[1]),
        pltpu.make_async_copy(states_hbm[2][0], w2f, lsem.at[2]),
        pltpu.make_async_copy(states_hbm[1][0], wsf, lsem.at[3]),
        pltpu.make_async_copy(cotangent, coti, lsem.at[4]),
    ]
    for load in loads:
        load.start()
    state_loads = []
    for s, state in enumerate((red_state, spa_state, exp_state)):
        places = (state.at[pl.ds(1, 2)], state.at[3])
        for part, place in enumerate(places):
            state_loads.append(pltpu.make_async_copy(states_hbm[s][part + 1], place, stsem.at[2 * s + part]))

    def columns_of(ref, j):
        return ref[:, pl.ds(pl.multiple_of(j * wp, wp), wp)].astype(BF16)

    loads[0].wait()
    for j in zpeers:
        w1s[j] = columns_of(w1f, j)
    w1r[c] = columns_of(w1f, c)
    pl.semaphore_wait(barrier, C - 1 + D - 1)

    def half(ref, j, side):
        return ref.at[j, pl.ds(pl.multiple_of(side * (ip // 2), 16), ip // 2)]

    for k, j in enumerate(zpeers):
        send("w1" + str(k), half(w1s, j, h), half(w1r, c, h), (d, j))

    row = lax.broadcasted_iota(jnp.int32, (I, LANES), 0)
    side = jnp.zeros((I, LANES), jnp.int32)
    for i in range(I):
        side = jnp.where(row == i, 5 + 2 * groups[i], side)
    cells_here = jnp.zeros((I, LANES), F32)
    for p in range(PIX):
        inside = (side > max(p // MAP, p % MAP)).astype(F32)
        mask[p * I : (p + 1) * I, :] = inside
        cells_here = cells_here + inside
    mask[R:RP, :] = jnp.zeros((RP - R, LANES), F32)
    count_here = jnp.sum(cells_here, axis=0, keepdims=True)

    def by_rows(src, dst):
        full = R // CHUNK * CHUNK

        def step(n, carry):
            rows = pl.ds(pl.multiple_of(n * CHUNK, CHUNK), CHUNK)
            dst[rows, :] = src[rows, :]
            return carry

        lax.fori_loop(0, R // CHUNK, step, 0)
        if RP > full:
            rest = [src[full:R, :].astype(F32)] if R > full else []
            rest.append(jnp.zeros((RP - R, src.shape[1]), F32))
            dst[full:RP, :] = jnp.concatenate(rest, axis=0).astype(BF16)

    def lanes(values, width):
        if width <= LANES:
            return values[:, :width]
        return jnp.concatenate([values] * (width // LANES), axis=1)

    def mask_of(rows, width):
        return lanes(mask[rows, :], width)

    everywhere, top_part, low_part = (0, RP // CHUNK), (0, sz.RT // CHUNK), (sz.RT // CHUNK, RP // CHUNK)

    def over_chunks(body, carry=0, part=everywhere):
        def step(s, carry):
            return body(pl.ds(pl.multiple_of(s * CHUNK, CHUNK), CHUNK), carry)

        return lax.fori_loop(*part, step, carry)

    def each_chunk(body, part=everywhere):
        def step(rows, carry):
            body(rows)
            return carry

        over_chunks(step, part=part)

    def fold_rows(values):
        total = values[0:8]
        for s in range(1, values.shape[0] // 8):
            total = total + values[8 * s : 8 * s + 8]
        return total

    def total_of(values):
        return jnp.sum(values, axis=0, keepdims=True)

    def rows_of(*values):
        height = 8
        if isinstance(values[0], int):
            height, *values = values
        rest = jnp.zeros((height - len(values), values[0].shape[1]), F32)
        return jnp.concatenate(list(values) + [rest], axis=0)

    loads[1].wait()
    by_rows(xi, xb)

    acc, p1s, p1r = v["acc"], v["p1s"], v["p1r"]
    sources = [lax.rem(c - k + C, C) for k in range(1, C)]
    for k, j in enumerate(sources):
        got("w1" + str(k), half(w1r, j, h))
        send("w1pair" + str(k), half(w1r, j, h), half(w1r, j, h), (sibling, c))
    for k, j in enumerate(sources):
        got("w1pair" + str(k), half(w1r, j, 1 - h))
        p1s[j] = nt(xb[...], w1r[j]).astype(BF16)
        send("pre1", p1s.at[j, pl.ds(0, RS)], p1r.at[c, pl.ds(0, RS)], (d, j))
    acc[...] = nt(xb[...], w1r[c])
    loads[2].wait()
    for j in zpeers:
        w2s[j, 0:ip, :] = columns_of(w2f, j)
    w2r[c, 0:ip, :] = columns_of(w2f, c)
    loads[4].wait()
    by_rows(coti, cotb)
    loads[3].wait()
    for t in range(TAPS):
        wfull[c, t * ip : (t + 1) * ip, :] = wsf[t].astype(BF16)
    for load in state_loads:
        load.start()

    def share(ref, j, e, n):
        return ref.at[j, pl.ds(pl.multiple_of(e * n, 16), n)]

    def part_of(j, e):
        return share(wfull, j, e, sz.PS)

    def fetch_spatial(k):
        send("wsp" + str(k), part_of(c, d), part_of(c, d), (d, zpeers[k]))

    cut = round_up(sz.PS // 2, 16)

    def part_side(j, e, side):
        start = pl.multiple_of(e * sz.PS + side * cut, 16)
        return wfull.at[j, pl.ds(start, cut if side == 0 else sz.PS - cut)]

    def spread_chips(k, side):
        j = sources[k]
        if side == 0:
            got("wsp" + str(k), part_of(j, d))
        for e in qpeers:
            send("wchip" + str(side) + str(k), part_side(j, d, side), part_side(j, d, side), (2 * e + h, c))

    def spread_pair(k):
        j = sources[k]
        got("wchip0" + str(k), wfull.at[j, pl.ds(0, (Q - 1) * cut)])
        got("wchip1" + str(k), wfull.at[j, pl.ds(0, (Q - 1) * (sz.PS - cut))])
        for e in range(Q):
            send("wpair" + str(k), part_of(j, 2 * e + h), part_of(j, 2 * e + h), (sibling, c))

    def spread_done(k):
        got("wpair" + str(k), wfull.at[0, pl.ds(0, Q * sz.PS)])

    late = list(reversed(range(1, C - 1)))

    def add_partials(name, recv):
        got(name, recv.at[pl.ds(0, C - 1), pl.ds(0, RS)])
        for j in zpeers:
            acc[0:RS, :] += recv[j, 0:RS, :].astype(F32)

    add_partials("pre1", p1r)

    def moments(src, width):
        def sums(rows, carry):
            return carry + fold_rows(src[rows, :] * mask_of(rows, width))

        mean = total_of(over_chunks(sums, jnp.zeros((8, width), F32))) / lanes(count_here, width)

        def squares(rows, carry):
            centered = src[rows, :] - mean
            return carry + fold_rows(mask_of(rows, width) * centered * centered)

        return mean, total_of(over_chunks(squares, jnp.zeros((8, width), F32)))

    def exchange_dp(name, table):
        for e in dpeers:
            send(name, table.at[d], table.at[d], (e, c))

    def combine(name, table):
        got(name, table.at[pl.ds(0, D - 1)])
        count = table[0, 2:3, :]
        average = count * table[0, 0:1, :]
        for e in range(1, D):
            count = count + table[e, 2:3, :]
            average = average + table[e, 2:3, :] * table[e, 0:1, :]
        average = average / count
        variance = jnp.zeros_like(average)
        for e in range(D):
            off = table[e, 0:1, :] - average
            variance = variance + (table[e, 1:2, :] + table[e, 2:3, :] * off * off)
        return average, lax.rsqrt(variance / count + norm_eps), count

    def sum_dp(name, table):
        got(name, table.at[pl.ds(0, D - 1)])
        total = table[0]
        for e in range(1, D):
            total = total + table[e]
        return total[0:1, :], total[1:2, :]

    def send_z(name, ref, rows=None):
        part = ref.at[c] if rows is None else ref.at[c, pl.ds(0, rows)]
        for j in zpeers:
            send(name, part, part, (d, j))

    def got_z(name, ref, rows=None):
        got(name, ref.at[pl.ds(0, C - 1)] if rows is None else ref.at[pl.ds(0, C - 1), pl.ds(0, rows)])

    def joined(blocks, rows):
        return jnp.concatenate([blocks[j, rows, :].astype(F32) for j in range(C)], axis=1)

    def table_row(par, r):
        return jnp.concatenate([par[j, r : r + 1, :] for j in range(C)], axis=1)

    def own_part(values):
        own = v["own"]
        for j in range(C):
            own[j, 0 : values.shape[0], :] = values[:, j * ip : (j + 1) * ip]
        return own[c, 0 : values.shape[0], :]

    top_rows, low_rows = pl.ds(0, sz.RT), pl.ds(sz.RT, RS - sz.RT)

    def send_part(name, held, rows):
        for j in zpeers:
            send(name, held.at[c, rows], held.at[c, rows], (d, j))

    def got_part(name, held, rows):
        got(name, held.at[pl.ds(0, C - 1), rows])

    def inner_forward(layer, bn, table, held, name, par, top_work, low_work, meanwhile=lambda: None):
        mean, spread = moments(acc, ip)
        table[d] = rows_of(mean, spread, lanes(count_here, ip))
        exchange_dp(bn, table)

        def center(rows):
            held[c, rows, :] = ((acc[rows, :] - mean) * mask_of(rows, ip)).astype(BF16)

        each_chunk(center)
        send_part(name + "top", held, top_rows)
        average, inverse, count = combine(bn, table)
        par[c] = rows_of(
            inverse, (mean - average) * inverse,
            inner_norm[layer : layer + 1, :], inner_norm[2 + layer : 3 + layer, :],
        )
        send_z(name + "par", par)
        send_part(name + "low", held, low_rows)
        meanwhile()
        got_part(name + "top", held, top_rows)
        got_z(name + "par", par)
        top_work()
        got_part(name + "low", held, low_rows)
        low_work()
        return count

    v1, v2, d2b, pm1, pm2, pm3 = (v[n] for n in ("v1", "v2", "d2b", "pm1", "pm2", "pm3"))
    for j in range(C):
        for ref in (v1, v2, d2b):
            ref[j, RS:RP, :] = jnp.zeros((RP - RS, ip), BF16)
    def make_act(held, par, dst, part):
        inverse, shift, gain, bias = (table_row(par, r) for r in range(4))

        def step(rows):
            value = gain * (joined(held, rows) * inverse + shift) + bias
            dst[rows, :] = (value * sigmoid(value) * mask_of(rows, K)).astype(dst.dtype)

        each_chunk(step, part)

    big, pad, cols = v["big"], v["pad"], v["cols"]
    pad[...] = jnp.zeros_like(pad)
    top_cells, low_cells = range(CELLS_TOP + 1), range(CELLS_TOP + 1, MAP)
    top_out, low_out = range(CELLS_TOP), range(CELLS_TOP, MAP)

    def fill_pad(cells):
        for y in cells:
            start = ((y + 1) * PITCH + 1) * I
            pad[start : start + MAP * I, :] = big[y * MAP * I : (y + 1) * MAP * I, :]

    def out_rows(cells):
        return slice(0, CELLS_TOP * MAP * I) if cells is top_out else slice(CELLS_TOP * MAP * I, RP)

    def shifted(offset, cells):
        pieces = [pad[pl.ds(pl.multiple_of(offset + y * PITCH * I, I), MAP * I), :] for y in cells]
        if cells is low_out:
            pieces.append(jnp.zeros((RP - R, K), F32))
        return jnp.concatenate(pieces, axis=0).astype(BF16)

    def weight_of(j, tap):
        return wfull[j, pl.ds(pl.multiple_of(tap * ip, ip), ip), :]

    def second_conv(cells):
        rows = out_rows(cells)
        acc[rows, :] = jnp.zeros((rows.stop - rows.start, ip), F32)

        def second_step(tap, carry):
            cols[tap, rows, :] = shifted((lax.div(tap, 3) * PITCH + lax.rem(tap, 3)) * I, cells)
            acc[rows, :] += nt(cols[tap, rows, :], weight_of(c, tap))
            return carry

        lax.fori_loop(0, TAPS, second_step, 0)

    def first_top():
        make_act(v1, pm1, big, top_part)
        fill_pad(top_cells)
        second_conv(top_out)

    def first_low():
        for j in zpeers:
            send("w2", share(w2s, j, d, sz.PW), share(w2r, c, d, sz.PW), (d, j))
        fetch_spatial(0)
        make_act(v1, pm1, big, low_part)
        fill_pad(low_cells)
        second_conv(low_out)

    count_ip = inner_forward(0, "bn1", v["st1"], v1, "act1", pm1, first_top, first_low)
    count_k = lanes(lanes(count_ip, min(ip, LANES))[:, 0:1] + jnp.zeros((1, LANES), F32), K)

    def hand_on():
        got("w2", w2r.at[pl.ds(0, C - 1), pl.ds(0, sz.PW)])
        for j in zpeers:
            for e in qpeers:
                send("w2chip", share(w2r, j, d, sz.PW), share(w2r, j, d, sz.PW), (2 * e + h, c))
        spread_chips(0, 0)
        spread_chips(0, 1)
        got("w2chip", w2r.at[pl.ds(0, C - 1), pl.ds(0, (Q - 1) * sz.PW)])
        for j in zpeers:
            for e in range(Q):
                send("w2pair", share(w2r, j, 2 * e + h, sz.PW), share(w2r, j, 2 * e + h, sz.PW), (sibling, c))
        spread_pair(0)

    act2 = v["act2"]
    third, og, tg = v["third"], v["og"], v["tg"]

    def third_conv(part):
        make_act(v2, pm2, act2, part)
        rows = slice(part[0] * CHUNK, part[1] * CHUNK)
        third[rows, :] = nn(act2[rows, :], jnp.concatenate([w2r[j, 0:ip, :] for j in range(C)], axis=0))

    def second_top():
        got("w2pair", w2r.at[pl.ds(0, C - 1), pl.ds(0, Q * sz.PW)])
        third_conv(top_part)

    def second_low():
        for k in late:
            fetch_spatial(k)
        third_conv(low_part)

    inner_forward(1, "bn2", v["st2"], v2, "act2", pm2, second_top, second_low, hand_on)
    mean3, spread3 = moments(third, wp)
    st3, st4, st5, st6 = v["st3"], v["st4"], v["st5"], v["st6"]
    st3[d] = rows_of(4, mean3, spread3, lanes(count_here, wp))
    exchange_dp("bn3", st3)
    average3, inverse3, count_wp = combine("bn3", st3)
    gain3, bias3 = outer_norm[0:1, :], outer_norm[1:2, :]

    def last_step(rows, carry):
        m = mask_of(rows, wp)
        normed = (third[rows, :] - average3) * inverse3
        third[rows, :] = normed
        summed = gain3 * normed + bias3 + xb[rows, :].astype(F32)
        s = sigmoid(summed)
        here = summed * s * m
        output[rows, :] = here
        grad = cotb[rows, :].astype(F32) * (s * (1.0 + summed * (1.0 - s))) * m
        og[rows, :] = grad
        return carry[0] + fold_rows(grad), carry[1] + fold_rows(grad * normed)

    zero_wp = jnp.zeros((8, wp), F32)
    sums = over_chunks(last_step, (zero_wp, zero_wp))
    st4[d] = rows_of(4, total_of(sums[0]), total_of(sums[1]))
    exchange_dp("bk3", st4)
    bias_grad3, gain_grad3 = sum_dp("bk3", st4)
    scale3 = inverse3 * gain3

    def third_step(rows):
        back = mask_of(rows, wp) * ((bias_grad3 + third[rows, :] * gain_grad3) / count_wp)
        tg[rows, :] = (scale3 * (og[rows, :] - back)).astype(BF16)

    each_chunk(third_step)

    p2s, p2r = p1s, p1r
    sent_done("pre1")
    for k in range(1, C):
        j = lax.rem(c - k + C, C)
        p2s[j] = nt(tg[...], w2r[j, 0:ip, :]).astype(BF16)
        send("grad2", p2s.at[j, pl.ds(0, RS)], p2r.at[c, pl.ds(0, RS)], (d, j))
    for k in late:
        spread_chips(k, 0)
        if k > 1:
            spread_chips(k, 1)
    acc[...] = nt(tg[...], w2r[c, 0:ip, :])

    class Reduction:
        def __init__(self, name, z, part):
            self.name, self.z, self.part = name, z, part
            self.gs, self.rb, self.sm, self.rq, self.tot, self.fin = (
                v[("exp" if name == "red" and s in ("gs", "rb") else name) + "_" + s]
                for s in ("gs", "rb", "sm", "rq", "tot", "fin")
            )

        def pieces(self, first, rows):
            row, end = first, first + rows
            while row < end:
                owner = row // self.part
                stop = min(end, (owner + 1) * self.part)
                yield owner, row - owner * self.part, row - first, stop - row
                row = stop

        def put(self, zi, first, value):
            for owner, there, here, n in self.pieces(first, value.shape[0]):
                self.gs[owner % 2, owner // 2, zi, there : there + n, :] = value[here : here + n, :]

        def take(self, zi, first, rows):
            found = [
                self.fin[owner % 2, owner // 2, zi, there : there + n, :].astype(F32)
                for owner, there, _, n in self.pieces(first, rows)
            ]
            return jnp.concatenate(found, axis=0)

        def pair(self):
            send(self.name + "core", self.gs.at[1 - h], self.rb, (sibling, c))

        def chips(self):
            got(self.name + "core", self.rb)
            for e in range(Q):
                self.sm[e] = (self.gs[h, e].astype(F32) + self.rb[e].astype(F32)).astype(BF16)
            for e in qpeers:
                send(self.name + "chip", self.sm.at[e], self.rq.at[q], (2 * e + h, c))

        def chan(self):
            got(self.name + "chip", self.rq.at[pl.ds(0, Q - 1)])
            total = self.sm[q].astype(F32)
            for e in qpeers:
                total = total + self.rq[e].astype(F32)
            self.tot[...] = total.astype(BF16)
            if self.z == 1:
                self.fin[h, q, 0] = self.tot[0]
            else:
                self.fin[h, q, c] = self.tot[c]
                for j in zpeers:
                    send("z" + self.name, self.tot.at[j], self.fin.at[h, q, c], (d, j))

        def halves(self, side, other):
            cut = round_up(self.part // 2, 16)
            rows = pl.ds(0, cut) if side == 0 else pl.ds(cut, self.part - cut)
            return self.fin.at[h, other, slice(None), rows]

        def back(self, side):
            if side == 0 and self.z > 1:
                got("z" + self.name, self.fin.at[h, q, pl.ds(0, C - 1)])
            if side == 1 and self.part <= 16:
                return
            for e in qpeers:
                send(self.name + "back" + str(side), self.halves(side, q), self.halves(side, q), (2 * e + h, c))

        def other(self):
            cut = round_up(self.part // 2, 16)
            got(self.name + "back0", self.fin.at[h, pl.ds(0, Q - 1), slice(None), pl.ds(0, cut)])
            if self.part > 16:
                got(self.name + "back1", self.fin.at[h, pl.ds(0, Q - 1), slice(None), pl.ds(cut, self.part - cut)])
            send(self.name + "pair", self.fin.at[h], self.fin.at[h], (sibling, c))

        def done(self):
            got(self.name + "pair", self.fin.at[0])

    def adam(state, at, grad, rate, decay):
        weight, moment, square, average = (state[(part, *at)] for part in range(4))
        first = beta_one * moment + (1.0 - beta_one) * grad
        second = beta_two * square + (1.0 - beta_two) * grad * grad
        scaled = first * (1.0 / (1.0 - beta_one**STEP))
        root = jnp.sqrt(second * (1.0 / (1.0 - beta_two**STEP))) + adam_eps
        updated = weight - rate * (scaled / root + decay * weight)
        state[(0, *at)] = updated
        state[(1, *at)] = first
        state[(2, *at)] = second
        state[(3, *at)] = ema_rate * average + (1.0 - ema_rate) * updated

    def adam_rows(red, state, rate):
        for j in range(C):
            for first in range(0, ip, 32):
                n = min(32, ip - first)
                adam(state, (slice(first, first + n), slice(j * wp, (j + 1) * wp)), red.take(j, first, n), rate, decay_rate)

    exp_red = Reduction("exp", C, sz.PW)
    spa_red = Reduction("spa", 1, sz.PS)
    red_red = Reduction("red", C, sz.PW)
    for j in range(C):
        exp_red.put(j, 0, tn(act2[:, j * ip : (j + 1) * ip], tg[...]).astype(BF16))
    exp_red.pair()

    exp_red.chips()
    for k in late[:-1]:
        spread_pair(k)
    add_partials("grad2", p2r)
    inverse_own, shift_own, gain_own, bias_own = (pm2[c, r : r + 1, :] for r in range(4))

    def second_back(rows, carry):
        normed = v2[c, rows, :].astype(F32) * inverse_own + shift_own
        value = gain_own * normed + bias_own
        s = sigmoid(value)
        grad = acc[rows, :] * (s * (1.0 + value * (1.0 - s))) * mask_of(rows, ip)
        d2b[c, rows, :] = grad.astype(BF16)
        return carry[0] + fold_rows(grad), carry[1] + fold_rows(grad * normed)

    zero_ip = jnp.zeros((8, ip), F32)
    sums = over_chunks(second_back, (zero_ip, zero_ip))
    st5[d] = rows_of(total_of(sums[0]), total_of(sums[1]))
    exchange_dp("bk2", st5)
    send_part("dlt2top", d2b, top_rows)
    bias_own2, gain_own2 = sum_dp("bk2", st5)
    pm3[c] = rows_of(bias_own2 / count_ip, gain_own2 / count_ip)
    send_z("dlt2par", pm3)
    send_part("dlt2low", d2b, low_rows)
    for k in late[-1:]:
        spread_chips(k, 1)
    exp_red.chan()
    sgo = v["sgo"]

    def own_second(rows):
        normed = v2[c, rows, :].astype(F32) * inverse_own + shift_own
        back = mask_of(rows, ip) * (pm3[c, 0:1, :] + normed * pm3[c, 1:2, :])
        sgo[rows, :] = (inverse_own * gain_own * (d2b[c, rows, :].astype(F32) - back)).astype(BF16)

    each_chunk(own_second)
    for tap in range(TAPS):
        spa_red.put(0, tap * ip, tn(sgo[...], cols[tap]).astype(BF16))
    spa_red.pair()
    for k in late[-1:]:
        spread_pair(k)
    spa_red.chips()
    for load in state_loads:
        load.wait()
    fag = v["fag"]
    inverse2, shift2, gain2 = (table_row(pm2, r) for r in range(3))
    scale2 = inverse2 * gain2

    def full_second(part):
        bias_part, gain_part = table_row(pm3, 0), table_row(pm3, 1)

        def step(rows):
            normed = joined(v2, rows) * inverse2 + shift2
            back = mask_of(rows, K) * (bias_part + normed * gain_part)
            big[rows, :] = (scale2 * (joined(d2b, rows) - back)).astype(BF16).astype(F32)

        each_chunk(step, part)

    def first_act_grad(cells, first, last):
        rows = out_rows(cells)
        if first == 0:
            fag[rows, :] = jnp.zeros((rows.stop - rows.start, K), F32)

        def step(tap, carry):
            offset = ((2 - lax.div(tap, 3)) * PITCH + 2 - lax.rem(tap, 3)) * I
            weight = jnp.concatenate([weight_of(j, tap) for j in range(C)], axis=0)
            fag[rows, :] += nn(shifted(offset, cells), weight)
            return carry

        lax.fori_loop(first, last, step, 0)

    got_part("dlt2top", d2b, top_rows)
    got_z("dlt2par", pm3)
    full_second(top_part)
    fill_pad(top_cells)
    for k in range(C - 1):
        spread_done(k)
    first_act_grad(top_out, 0, TAPS)
    got_part("dlt2low", d2b, low_rows)
    full_second(low_part)
    fill_pad(low_cells)
    exp_red.back(0)
    exp_red.back(1)
    first_act_grad(low_out, 0, TAPS)

    inverse1, shift1, gain1, bias1 = (table_row(pm1, r) for r in range(4))

    def first_back(rows, carry):
        normed = joined(v1, rows) * inverse1 + shift1
        value = gain1 * normed + bias1
        s = sigmoid(value)
        grad = fag[rows, :] * (s * (1.0 + value * (1.0 - s))) * mask_of(rows, K)
        fag[rows, :] = grad
        big[rows, :] = normed
        return carry[0] + fold_rows(grad), carry[1] + fold_rows(grad * normed)

    zero_k = jnp.zeros((8, K), F32)
    sums = over_chunks(first_back, (zero_k, zero_k))
    st6[d] = rows_of(4, total_of(sums[0]), total_of(sums[1]))
    exchange_dp("bk1", st6)
    exp_red.other()
    spa_red.chan()
    bias_grad1, gain_grad1 = sum_dp("bk1", st6)
    spa_red.back(0)
    scale1 = inverse1 * gain1
    fg = v["fg"]

    def first_step(rows):
        back = mask_of(rows, K) * ((bias_grad1 + big[rows, :] * gain_grad1) / count_k)
        fg[rows, :] = (scale1 * (fag[rows, :] - back)).astype(BF16)

    each_chunk(first_step)
    sent_done("expcore")
    for j in range(C):
        red_red.put(j, 0, tn(fg[:, j * ip : (j + 1) * ip], xb[...]).astype(BF16))
    red_red.pair()
    input_grad[...] = nn(fg[...], w1r[...].reshape(K, wp)) + og[...]
    red_red.chips()

    def adam_spatial(first_tap, last_tap):
        for tap in range(first_tap, last_tap):
            for first in range(0, ip, 32):
                n = min(32, ip - first)
                adam(
                    spa_state, (tap, slice(first, first + n), slice(0, K)), spa_red.take(0, tap * ip + first, n),
                    2.0 / math.sqrt(TAPS * K), decay_rate,
                )

    red_red.chan()
    spa_red.back(1)
    spa_red.other()
    red_red.back(0)
    red_red.back(1)
    exp_red.done()
    adam_rows(exp_red, exp_state, 2.0 / math.sqrt(K))
    spa_red.done()
    adam_spatial(0, TAPS // 2)
    red_red.other()
    adam_spatial(TAPS // 2, TAPS)

    first_grads = own_part(jnp.concatenate([gain_grad1, bias_grad1], axis=0))
    inner_grads = [first_grads[0:1, :], gain_own2, first_grads[1:2, :], bias_own2]
    outer_grads = [gain_grad3, bias_grad3]
    inner_state[0:4, :] = inner_norm[...]
    for m in range(2):
        for r in range(2):
            inner_state[4 + 4 * m + 2 * r : 6 + 4 * m + 2 * r, :] = inner_moments[m, r]
    inner_state[12:16, :] = inner_ema[...]
    outer_state[0:2, :] = outer_norm[...]
    outer_state[2:6, :] = outer_moments[...]
    outer_state[6:8, :] = outer_ema[...]

    def adam_small(state, n, grads):
        grad = jnp.concatenate(grads, axis=0)
        weight, moment, square, average = (state[part * n : (part + 1) * n, :] for part in range(4))
        first = beta_one * moment + (1.0 - beta_one) * grad
        second = beta_two * square + (1.0 - beta_two) * grad * grad
        scaled = first * (1.0 / (1.0 - beta_one**STEP))
        root = jnp.sqrt(second * (1.0 / (1.0 - beta_two**STEP))) + adam_eps
        updated = weight - norm_rate * (scaled / root)
        state[0:n, :] = updated
        state[n : 2 * n, :] = first
        state[2 * n : 3 * n, :] = second
        state[3 * n : 4 * n, :] = ema_rate * average + (1.0 - ema_rate) * updated

    adam_small(inner_state, 4, inner_grads)
    adam_small(outer_state, 2, outer_grads)
    red_red.done()
    adam_rows(red_red, red_state, 2.0 / math.sqrt(sz.W))
    for name, ref in sent:
        wait_bytes(ref, ssem.at[sem_of[name]])


def store_kernel(n, *refs):
    held, places, sem = refs[:7], refs[7 : 7 + n], refs[-1]
    output, input_grad, red_state, spa_state, exp_state, inner_state, outer_state = held
    parts = [output.at[pl.ds(0, places[0].shape[0])], input_grad.at[pl.ds(0, places[1].shape[0])]]
    for state in (red_state, spa_state, exp_state):
        parts += [state.at[part] for part in range(4)]
    copies = [pltpu.make_async_copy(src, dst, sem.at[i]) for i, (src, dst) in enumerate(zip(parts, places))]
    for copy in copies:
        copy.start()
    inner_places, outer_places = places[14:18], places[18:22]
    for part in range(4):
        inner_places[part][...] = inner_state[part * 4 : (part + 1) * 4, :]
        outer_places[part][...] = outer_state[part * 2 : (part + 1) * 2, :]
    for copy in copies:
        copy.wait()


def per_device(
    mesh_dp, mesh_chan,
    images, groups, cotangent, reduce_weight, spatial_weight, expand_weight, inner_norm, outer_norm,
    reduce_moments, spatial_moments, expand_moments, inner_moments, outer_moments,
    reduce_ema, spatial_ema, expand_ema, inner_ema, outer_ema,
):
    sz = Sizes(mesh_dp, mesh_chan, images, reduce_weight)
    ip, wp, K, C = sz.ip, sz.wp, sz.K, sz.C

    def by_cell(a):
        return a.transpose(1, 0, 2).reshape(sz.R, wp)

    def by_tap(a):
        return a.transpose(1, 2, 0, 3).reshape(TAPS, ip, K)

    any_spec, vmem_spec = pl.BlockSpec(memory_space=pl.ANY), pl.BlockSpec(memory_space=pltpu.VMEM)
    states = []
    for weight, moments, ema in (
        (reduce_weight, reduce_moments, reduce_ema),
        (by_tap(spatial_weight), spatial_moments.transpose(0, 2, 3, 1, 4).reshape(2, TAPS, ip, K), by_tap(spatial_ema)),
        (expand_weight, expand_moments, expand_ema),
    ):
        states += [weight, moments, ema]
    held_shapes = (
        (sz.RP, wp), (sz.RP, wp), (4, ip, sz.W), (4, TAPS, ip, K), (4, ip, sz.W), (16, ip), (8, wp),
    )
    held = pl.pallas_call(
        functools.partial(block_kernel, sz),
        out_shape=tuple(pltpu.VMEM(shape, F32) for shape in held_shapes),
        in_specs=[pl.BlockSpec(memory_space=pltpu.SMEM)] + [any_spec] * 2 + [vmem_spec] * 6 + [any_spec] * 9,
        out_specs=(vmem_spec,) * len(held_shapes),
        scratch_shapes=[pltpu.VMEM(shape, dtype) for _, shape, dtype in scratch_table(sz)]
        + [
            pltpu.SemaphoreType.DMA((5,)),
            pltpu.SemaphoreType.DMA((6,)),
            pltpu.SemaphoreType.DMA((len(phases(sz)),)),
            pltpu.SemaphoreType.DMA((len(phases(sz)),)),
        ],
        compiler_params=pltpu.CompilerParams(
            collective_id=0, has_side_effects=True, vmem_limit_bytes=VMEM_TOTAL - sum(vmem_bytes(shape, F32) for shape in held_shapes)
        ),
    )(
        groups, by_cell(images), by_cell(cotangent),
        inner_norm.reshape(4, ip), outer_norm, inner_moments, outer_moments.reshape(4, wp),
        inner_ema.reshape(4, ip), outer_ema, *states,
    )
    held = [pltpu.with_memory_space_constraint(a, pltpu.VMEM) for a in held]
    shapes = [(sz.R, wp)] * 2 + [(ip, sz.W)] * 4 + [(TAPS, ip, K)] * 4 + [(ip, sz.W)] * 4
    small = [(4, ip)] * 4 + [(2, wp)] * 4
    results = pl.pallas_call(
        functools.partial(store_kernel, len(shapes + small)),
        out_shape=tuple(jax.ShapeDtypeStruct(shape, F32) for shape in shapes + small),
        in_specs=[vmem_spec] * len(held),
        out_specs=(any_spec,) * len(shapes) + (vmem_spec,) * len(small),
        scratch_shapes=[pltpu.SemaphoreType.DMA((len(shapes),))],
        compiler_params=pltpu.CompilerParams(vmem_limit_bytes=2 * 2**20),
    )(*held)
    images_of = [a.reshape(PIX, sz.I, wp).transpose(1, 0, 2) for a in results[:2]]
    taps = [a.reshape(3, 3, ip, K).transpose(2, 0, 1, 3) for a in results[6:10]]
    inner = [a.reshape(2, 2, ip) for a in results[14:18]]
    return (*images_of, *results[2:6], *taps, *results[10:14], *inner, *results[18:22])


def solution(mesh):
    placed = (
        P("dp", None, "chan"),
        P("dp"),
        P("dp", None, "chan"),
        P("chan", None),
        P("chan", None, None, None),
        P("chan", None),
        P(None, None, "chan"),
        P(None, "chan"),
        P(None, "chan", None),
        P(None, "chan", None, None, None),
        P(None, "chan", None),
        P(None, None, None, "chan"),
        P(None, None, "chan"),
        P("chan", None),
        P("chan", None, None, None),
        P("chan", None),
        P(None, None, "chan"),
        P(None, "chan"),
    )
    return jax.shard_map(
        functools.partial(per_device, mesh.shape["dp"], mesh.shape["chan"]),
        mesh=mesh,
        in_specs=placed,
        out_specs=(P("dp", None, "chan"),) * 2
        + (P("chan", None),) * 4
        + (P("chan", None, None, None),) * 4
        + (P("chan", None),) * 4
        + (P(None, None, "chan"),) * 4
        + (P(None, "chan"),) * 4,
        check_vma=False,
    )
```

```python
import functools
import math

import jax
import jax.numpy as jnp
from jax import lax
from jax.experimental import pallas as pl
from jax.experimental.pallas import tpu as pltpu
from jax.sharding import PartitionSpec as P

MESH = pl.DeviceIdType.MESH
MAP = 9
PIX = MAP * MAP
TAPS = 9
PITCH = MAP + 1
STEP = 5
LANES = 128
CHUNK = 48
CELLS_TOP = 2
VMEM_TOTAL = 62 * 2**20

norm_eps = 1e-05
adam_eps = 1e-08
beta_one = 0.5
beta_two = 0.5
decay_rate = 0.05
ema_rate = 0.75
norm_rate = 0.3

F32 = jnp.float32
BF16 = jnp.bfloat16


def round_up(value, unit):
    return -(-value // unit) * unit


class Sizes:
    def __init__(self, mesh_dp, mesh_chan, images, reduce_weight):
        self.D, self.C = mesh_dp, mesh_chan
        self.Q = self.D // 2
        self.I, _, self.wp = images.shape
        self.ip, self.W = reduce_weight.shape
        self.K = self.ip * self.C
        self.KB = self.K // LANES
        self.WB = self.wp // LANES
        self.R = PIX * self.I
        self.RS = round_up(self.R, 16)
        self.RP = round_up(self.R, CHUNK)
        self.RT = 5 * CHUNK
        self.NS = TAPS * self.ip
        self.PW = round_up(-(-self.ip // self.D), 16)
        self.PS = round_up(-(-self.NS // self.D), 16)
        self.PADROWS = ((MAP + 2) * PITCH + 2) * self.I


Z_PHASES = ["w2", "pre1", "grad2", "zexp", "zred"]
Z_PHASES += [name + part for name in ("act1", "act2", "dlt2") for part in ("top", "par", "low")]
D_PHASES = ["w2chip", "w2pair", "bn1", "bn2", "bn3", "bk3", "bk2", "bk1"]
R_PHASES = [g + s for g in ("exp", "spa", "red") for s in ("core", "chip", "back0", "back1", "pair")]


def phases(sz):
    each = [name + str(k) for name in ("w1", "w1pair", "wsp", "wchip0", "wchip1", "wpair") for k in range(sz.C - 1)]
    return Z_PHASES + D_PHASES + R_PHASES + each


def nt(a, b):
    return lax.dot_general(a, b, (((1,), (1,)), ((), ())), preferred_element_type=F32)


def nn(a, b):
    return lax.dot_general(a, b, (((1,), (0,)), ((), ())), preferred_element_type=F32)


def tn(a, b):
    return lax.dot_general(a, b, (((0,), (0,)), ((), ())), preferred_element_type=F32)


def sigmoid(v):
    return jax.nn.sigmoid(v)


def vmem_bytes(shape, dtype):
    *lead, rows, width = shape
    return math.prod(lead) * round_up(rows, 8) * round_up(width, LANES) * jnp.dtype(dtype).itemsize


def scratch_table(sz):
    C, D, Q, ip, wp, K, RP, I = sz.C, sz.D, sz.Q, sz.ip, sz.wp, sz.K, sz.RP, sz.I
    table = [
        ("xi", (sz.R, wp), BF16),
        ("coti", (sz.R, wp), BF16),
        ("mask", (RP, LANES), F32),
        ("xb", (RP, wp), BF16),
        ("cotb", (RP, wp), BF16),
        ("w1s", (C, ip, wp), BF16),
        ("w1r", (C, ip, wp), BF16),
        ("w2s", (C, D * sz.PW, wp), BF16),
        ("w2r", (C, D * sz.PW, wp), BF16),
        ("wfull", (C, D * sz.PS, K), BF16),
        ("p1s", (C, RP, ip), BF16),
        ("p1r", (C, RP, ip), BF16),
        ("v1", (C, RP, ip), BF16),
        ("v2", (C, RP, ip), BF16),
        ("d2b", (C, RP, ip), BF16),
        ("pm1", (C, 8, ip), F32),
        ("pm2", (C, 8, ip), F32),
        ("pm3", (C, 8, ip), F32),
        ("own", (C, 8, ip), F32),
        ("st1", (D, 8, ip), F32),
        ("st2", (D, 8, ip), F32),
        ("st3", (D, 4, wp), F32),
        ("st4", (D, 4, wp), F32),
        ("st5", (D, 8, ip), F32),
        ("st6", (D, 4, K), F32),
        ("acc", (RP, ip), F32),
        ("pad", (sz.PADROWS, K), F32),
        ("cols", (TAPS, RP, K), BF16),
        ("act2", (RP, K), BF16),
        ("third", (RP, wp), F32),
        ("og", (RP, wp), F32),
        ("tg", (RP, wp), BF16),
        ("big", (RP, K), F32),
        ("fag", (RP, K), F32),
        ("sgo", (RP, ip), BF16),
        ("fg", (RP, K), BF16),
    ]
    for name, z, part, width in (("exp", C, sz.PW, wp), ("spa", 1, sz.PS, K), ("red", C, sz.PW, wp)):
        table += [
            *([] if name == "red" else [
                (name + "_gs", (2, Q, z, part, width), BF16),
                (name + "_rb", (Q, z, part, width), BF16),
            ]),
            (name + "_sm", (Q, z, part, width), BF16),
            (name + "_rq", (Q, z, part, width), BF16),
            (name + "_tot", (z, part, width), BF16),
            (name + "_fin", (2, Q, z, part, width), BF16),
        ]
    return table


def block_kernel(sz, *refs):
    groups, images, cotangent, inner_norm, outer_norm, inner_moments, outer_moments, inner_ema, outer_ema = refs[:9]
    states_hbm = [refs[9:12], refs[12:15], refs[15:18]]
    output, input_grad, red_state, spa_state, exp_state, inner_state, outer_state = refs[18:25]
    table = scratch_table(sz)
    v = {name: ref for (name, _, _), ref in zip(table, refs[25:])}
    lsem, stsem, ssem, rsem = refs[25 + len(table) :]
    D, C, Q, I, K, KB, WB = sz.D, sz.C, sz.Q, sz.I, sz.K, sz.KB, sz.WB
    ip, wp, R, RS, RP = sz.ip, sz.wp, sz.R, sz.RS, sz.RP
    d = lax.axis_index("dp")
    c = lax.axis_index("chan")
    q = lax.div(d, 2)
    h = lax.rem(d, 2)
    zpeers = [lax.rem(c + k, C) for k in range(1, C)]
    dpeers = [lax.rem(d + k, D) for k in range(1, D)]
    far_first = sorted(range(1, C), key=lambda k: -min(k, C - k))
    far_first = [lax.rem(c + k, C) for k in far_first]
    qpeers = [lax.rem(q + k, Q) for k in range(1, Q)]
    sibling = d + 1 - 2 * h
    sem_of = {name: i for i, name in enumerate(phases(sz))}
    sent = []

    def send(name, src, dst, device):
        pltpu.make_async_remote_copy(
            src_ref=src, dst_ref=dst, send_sem=ssem.at[sem_of[name]], recv_sem=rsem.at[sem_of[name]],
            device_id=device, device_id_type=MESH,
        ).start()

    def wait_bytes(ref, sem):
        pltpu.make_async_copy(ref, ref, sem).wait()

    def got(name, ref):
        wait_bytes(ref, rsem.at[sem_of[name]])
        sent.append((name, ref))

    def sent_done(name):
        for entry in [e for e in sent if e[0] == name]:
            wait_bytes(entry[1], ssem.at[sem_of[name]])
            sent.remove(entry)

    barrier = pltpu.get_barrier_semaphore()
    for j in zpeers:
        pl.semaphore_signal(barrier, inc=1, device_id=(d, j), device_id_type=MESH)
    for e in dpeers:
        pl.semaphore_signal(barrier, inc=1, device_id=(e, c), device_id_type=MESH)

    xi, coti, mask, xb, cotb = (v[n] for n in ("xi", "coti", "mask", "xb", "cotb"))
    w1s, w1r, w2s, w2r, wfull = (v[n] for n in ("w1s", "w1r", "w2s", "w2r", "wfull"))
    w1f, wsf, w2f = red_state.at[0], spa_state.at[0], exp_state.at[0]
    loads = [
        pltpu.make_async_copy(states_hbm[0][0], w1f, lsem.at[0]),
        pltpu.make_async_copy(images, xi, lsem.at[1]),
        pltpu.make_async_copy(states_hbm[2][0], w2f, lsem.at[2]),
        pltpu.make_async_copy(states_hbm[1][0], wsf, lsem.at[3]),
        pltpu.make_async_copy(cotangent, coti, lsem.at[4]),
    ]
    for load in loads:
        load.start()
    state_loads = []
    for s, state in enumerate((red_state, spa_state, exp_state)):
        places = (state.at[pl.ds(1, 2)], state.at[3])
        for part, place in enumerate(places):
            state_loads.append(pltpu.make_async_copy(states_hbm[s][part + 1], place, stsem.at[2 * s + part]))

    def columns_of(ref, j):
        return ref[:, pl.ds(pl.multiple_of(j * wp, wp), wp)].astype(BF16)

    loads[0].wait()
    for j in zpeers:
        w1s[j] = columns_of(w1f, j)
    w1r[c] = columns_of(w1f, c)
    pl.semaphore_wait(barrier, C - 1 + D - 1)

    def half(ref, j, side):
        return ref.at[j, pl.ds(pl.multiple_of(side * (ip // 2), 16), ip // 2)]

    for k, j in enumerate(zpeers):
        send("w1" + str(k), half(w1s, j, h), half(w1r, c, h), (d, j))

    row = lax.broadcasted_iota(jnp.int32, (I, LANES), 0)
    side = jnp.zeros((I, LANES), jnp.int32)
    for i in range(I):
        side = jnp.where(row == i, 5 + 2 * groups[i], side)
    cells_here = jnp.zeros((I, LANES), F32)
    for p in range(PIX):
        inside = (side > max(p // MAP, p % MAP)).astype(F32)
        mask[p * I : (p + 1) * I, :] = inside
        cells_here = cells_here + inside
    mask[R:RP, :] = jnp.zeros((RP - R, LANES), F32)
    count_here = jnp.sum(cells_here, axis=0, keepdims=True)

    def by_rows(src, dst):
        full = R // CHUNK * CHUNK

        def step(n, carry):
            rows = pl.ds(pl.multiple_of(n * CHUNK, CHUNK), CHUNK)
            dst[rows, :] = src[rows, :]
            return carry

        lax.fori_loop(0, R // CHUNK, step, 0)
        if RP > full:
            rest = [src[full:R, :].astype(F32)] if R > full else []
            rest.append(jnp.zeros((RP - R, src.shape[1]), F32))
            dst[full:RP, :] = jnp.concatenate(rest, axis=0).astype(BF16)

    def lanes(values, width):
        if width <= LANES:
            return values[:, :width]
        return jnp.concatenate([values] * (width // LANES), axis=1)

    def mask_of(rows, width):
        return lanes(mask[rows, :], width)

    everywhere, top_part, low_part = (0, RP // CHUNK), (0, sz.RT // CHUNK), (sz.RT // CHUNK, RP // CHUNK)

    def over_chunks(body, carry=0, part=everywhere):
        def step(s, carry):
            return body(pl.ds(pl.multiple_of(s * CHUNK, CHUNK), CHUNK), carry)

        return lax.fori_loop(*part, step, carry)

    def each_chunk(body, part=everywhere):
        def step(rows, carry):
            body(rows)
            return carry

        over_chunks(step, part=part)

    def fold_rows(values):
        total = values[0:8]
        for s in range(1, values.shape[0] // 8):
            total = total + values[8 * s : 8 * s + 8]
        return total

    def total_of(values):
        return jnp.sum(values, axis=0, keepdims=True)

    def rows_of(*values):
        height = 8
        if isinstance(values[0], int):
            height, *values = values
        rest = jnp.zeros((height - len(values), values[0].shape[1]), F32)
        return jnp.concatenate(list(values) + [rest], axis=0)

    loads[1].wait()
    by_rows(xi, xb)

    acc, p1s, p1r = v["acc"], v["p1s"], v["p1r"]
    sources = [lax.rem(c - k + C, C) for k in range(1, C)]
    for k, j in enumerate(sources):
        got("w1" + str(k), half(w1r, j, h))
        send("w1pair" + str(k), half(w1r, j, h), half(w1r, j, h), (sibling, c))
    for k, j in enumerate(sources):
        got("w1pair" + str(k), half(w1r, j, 1 - h))
        p1s[j] = nt(xb[...], w1r[j]).astype(BF16)
        send("pre1", p1s.at[j, pl.ds(0, RS)], p1r.at[c, pl.ds(0, RS)], (d, j))
    acc[...] = nt(xb[...], w1r[c])
    loads[2].wait()
    for j in zpeers:
        w2s[j, 0:ip, :] = columns_of(w2f, j)
    w2r[c, 0:ip, :] = columns_of(w2f, c)
    loads[4].wait()
    by_rows(coti, cotb)
    loads[3].wait()
    for t in range(TAPS):
        wfull[c, t * ip : (t + 1) * ip, :] = wsf[t].astype(BF16)
    for load in state_loads:
        load.start()

    def share(ref, j, e, n):
        return ref.at[j, pl.ds(pl.multiple_of(e * n, 16), n)]

    def part_of(j, e):
        return share(wfull, j, e, sz.PS)

    def fetch_spatial(k):
        send("wsp" + str(k), part_of(c, d), part_of(c, d), (d, zpeers[k]))

    cut = round_up(sz.PS // 2, 16)

    def part_side(j, e, side):
        start = pl.multiple_of(e * sz.PS + side * cut, 16)
        return wfull.at[j, pl.ds(start, cut if side == 0 else sz.PS - cut)]

    def spread_chips(k, side):
        j = sources[k]
        if side == 0:
            got("wsp" + str(k), part_of(j, d))
        for e in qpeers:
            send("wchip" + str(side) + str(k), part_side(j, d, side), part_side(j, d, side), (2 * e + h, c))

    def spread_pair(k):
        j = sources[k]
        got("wchip0" + str(k), wfull.at[j, pl.ds(0, (Q - 1) * cut)])
        got("wchip1" + str(k), wfull.at[j, pl.ds(0, (Q - 1) * (sz.PS - cut))])
        for e in range(Q):
            send("wpair" + str(k), part_of(j, 2 * e + h), part_of(j, 2 * e + h), (sibling, c))

    def spread_done(k):
        got("wpair" + str(k), wfull.at[0, pl.ds(0, Q * sz.PS)])

    late = list(reversed(range(1, C - 1)))

    def add_partials(name, recv):
        got(name, recv.at[pl.ds(0, C - 1), pl.ds(0, RS)])
        for j in zpeers:
            acc[0:RS, :] += recv[j, 0:RS, :].astype(F32)

    add_partials("pre1", p1r)

    def moments(src, width):
        def sums(rows, carry):
            return carry + fold_rows(src[rows, :] * mask_of(rows, width))

        mean = total_of(over_chunks(sums, jnp.zeros((8, width), F32))) / lanes(count_here, width)

        def squares(rows, carry):
            centered = src[rows, :] - mean
            return carry + fold_rows(mask_of(rows, width) * centered * centered)

        return mean, total_of(over_chunks(squares, jnp.zeros((8, width), F32)))

    def exchange_dp(name, table):
        for e in dpeers:
            send(name, table.at[d], table.at[d], (e, c))

    def combine(name, table):
        got(name, table.at[pl.ds(0, D - 1)])
        count = table[0, 2:3, :]
        average = count * table[0, 0:1, :]
        for e in range(1, D):
            count = count + table[e, 2:3, :]
            average = average + table[e, 2:3, :] * table[e, 0:1, :]
        average = average / count
        variance = jnp.zeros_like(average)
        for e in range(D):
            off = table[e, 0:1, :] - average
            variance = variance + (table[e, 1:2, :] + table[e, 2:3, :] * off * off)
        return average, lax.rsqrt(variance / count + norm_eps), count

    def sum_dp(name, table):
        got(name, table.at[pl.ds(0, D - 1)])
        total = table[0]
        for e in range(1, D):
            total = total + table[e]
        return total[0:1, :], total[1:2, :]

    def send_z(name, ref, rows=None):
        part = ref.at[c] if rows is None else ref.at[c, pl.ds(0, rows)]
        for j in zpeers:
            send(name, part, part, (d, j))

    def got_z(name, ref, rows=None):
        got(name, ref.at[pl.ds(0, C - 1)] if rows is None else ref.at[pl.ds(0, C - 1), pl.ds(0, rows)])

    def joined(blocks, rows):
        return jnp.concatenate([blocks[j, rows, :].astype(F32) for j in range(C)], axis=1)

    def table_row(par, r):
        return jnp.concatenate([par[j, r : r + 1, :] for j in range(C)], axis=1)

    def own_part(values):
        own = v["own"]
        for j in range(C):
            own[j, 0 : values.shape[0], :] = values[:, j * ip : (j + 1) * ip]
        return own[c, 0 : values.shape[0], :]

    top_rows, low_rows = pl.ds(0, sz.RT), pl.ds(sz.RT, RS - sz.RT)

    def send_part(name, held, rows):
        for j in zpeers:
            send(name, held.at[c, rows], held.at[c, rows], (d, j))

    def got_part(name, held, rows):
        got(name, held.at[pl.ds(0, C - 1), rows])

    def inner_forward(layer, bn, table, held, name, par, top_work, low_work, meanwhile=lambda: None):
        mean, spread = moments(acc, ip)
        table[d] = rows_of(mean, spread, lanes(count_here, ip))
        exchange_dp(bn, table)

        def center(rows):
            held[c, rows, :] = ((acc[rows, :] - mean) * mask_of(rows, ip)).astype(BF16)

        each_chunk(center)
        send_part(name + "top", held, top_rows)
        average, inverse, count = combine(bn, table)
        par[c] = rows_of(
            inverse, (mean - average) * inverse,
            inner_norm[layer : layer + 1, :], inner_norm[2 + layer : 3 + layer, :],
        )
        send_z(name + "par", par)
        send_part(name + "low", held, low_rows)
        meanwhile()
        got_part(name + "top", held, top_rows)
        got_z(name + "par", par)
        top_work()
        got_part(name + "low", held, low_rows)
        low_work()
        return count

    v1, v2, d2b, pm1, pm2, pm3 = (v[n] for n in ("v1", "v2", "d2b", "pm1", "pm2", "pm3"))
    for j in range(C):
        for ref in (v1, v2, d2b):
            ref[j, RS:RP, :] = jnp.zeros((RP - RS, ip), BF16)
    def make_act(held, par, dst, part):
        inverse, shift, gain, bias = (table_row(par, r) for r in range(4))

        def step(rows):
            value = gain * (joined(held, rows) * inverse + shift) + bias
            dst[rows, :] = (value * sigmoid(value) * mask_of(rows, K)).astype(dst.dtype)

        each_chunk(step, part)

    big, pad, cols = v["big"], v["pad"], v["cols"]
    pad[...] = jnp.zeros_like(pad)
    top_cells, low_cells = range(CELLS_TOP + 1), range(CELLS_TOP + 1, MAP)
    top_out, low_out = range(CELLS_TOP), range(CELLS_TOP, MAP)

    def fill_pad(cells):
        for y in cells:
            start = ((y + 1) * PITCH + 1) * I
            pad[start : start + MAP * I, :] = big[y * MAP * I : (y + 1) * MAP * I, :]

    def out_rows(cells):
        return slice(0, CELLS_TOP * MAP * I) if cells is top_out else slice(CELLS_TOP * MAP * I, RP)

    def shifted(offset, cells):
        pieces = [pad[pl.ds(pl.multiple_of(offset + y * PITCH * I, I), MAP * I), :] for y in cells]
        if cells is low_out:
            pieces.append(jnp.zeros((RP - R, K), F32))
        return jnp.concatenate(pieces, axis=0).astype(BF16)

    def weight_of(j, tap):
        return wfull[j, pl.ds(pl.multiple_of(tap * ip, ip), ip), :]

    def second_conv(cells):
        rows = out_rows(cells)
        acc[rows, :] = jnp.zeros((rows.stop - rows.start, ip), F32)

        def second_step(tap, carry):
            cols[tap, rows, :] = shifted((lax.div(tap, 3) * PITCH + lax.rem(tap, 3)) * I, cells)
            acc[rows, :] += nt(cols[tap, rows, :], weight_of(c, tap))
            return carry

        lax.fori_loop(0, TAPS, second_step, 0)

    def first_top():
        make_act(v1, pm1, big, top_part)
        fill_pad(top_cells)
        second_conv(top_out)

    def first_low():
        for j in zpeers:
            send("w2", share(w2s, j, d, sz.PW), share(w2r, c, d, sz.PW), (d, j))
        fetch_spatial(0)
        make_act(v1, pm1, big, low_part)
        fill_pad(low_cells)
        second_conv(low_out)

    count_ip = inner_forward(0, "bn1", v["st1"], v1, "act1", pm1, first_top, first_low)
    count_k = lanes(lanes(count_ip, min(ip, LANES))[:, 0:1] + jnp.zeros((1, LANES), F32), K)

    def hand_on():
        got("w2", w2r.at[pl.ds(0, C - 1), pl.ds(0, sz.PW)])
        for j in zpeers:
            for e in qpeers:
                send("w2chip", share(w2r, j, d, sz.PW), share(w2r, j, d, sz.PW), (2 * e + h, c))
        spread_chips(0, 0)
        spread_chips(0, 1)
        got("w2chip", w2r.at[pl.ds(0, C - 1), pl.ds(0, (Q - 1) * sz.PW)])
        for j in zpeers:
            for e in range(Q):
                send("w2pair", share(w2r, j, 2 * e + h, sz.PW), share(w2r, j, 2 * e + h, sz.PW), (sibling, c))
        spread_pair(0)

    act2 = v["act2"]
    third, og, tg = v["third"], v["og"], v["tg"]

    def third_conv(part):
        make_act(v2, pm2, act2, part)
        rows = slice(part[0] * CHUNK, part[1] * CHUNK)
        third[rows, :] = nn(act2[rows, :], jnp.concatenate([w2r[j, 0:ip, :] for j in range(C)], axis=0))

    def second_top():
        got("w2pair", w2r.at[pl.ds(0, C - 1), pl.ds(0, Q * sz.PW)])
        third_conv(top_part)

    def second_low():
        for k in late:
            fetch_spatial(k)
        third_conv(low_part)

    inner_forward(1, "bn2", v["st2"], v2, "act2", pm2, second_top, second_low, hand_on)
    mean3, spread3 = moments(third, wp)
    st3, st4, st5, st6 = v["st3"], v["st4"], v["st5"], v["st6"]
    st3[d] = rows_of(4, mean3, spread3, lanes(count_here, wp))
    exchange_dp("bn3", st3)
    average3, inverse3, count_wp = combine("bn3", st3)
    gain3, bias3 = outer_norm[0:1, :], outer_norm[1:2, :]

    def last_step(rows, carry):
        m = mask_of(rows, wp)
        normed = (third[rows, :] - average3) * inverse3
        third[rows, :] = normed
        summed = gain3 * normed + bias3 + xb[rows, :].astype(F32)
        s = sigmoid(summed)
        here = summed * s * m
        output[rows, :] = here
        grad = cotb[rows, :].astype(F32) * (s * (1.0 + summed * (1.0 - s))) * m
        og[rows, :] = grad
        return carry[0] + fold_rows(grad), carry[1] + fold_rows(grad * normed)

    zero_wp = jnp.zeros((8, wp), F32)
    sums = over_chunks(last_step, (zero_wp, zero_wp))
    st4[d] = rows_of(4, total_of(sums[0]), total_of(sums[1]))
    exchange_dp("bk3", st4)
    bias_grad3, gain_grad3 = sum_dp("bk3", st4)
    scale3 = inverse3 * gain3

    def third_step(rows):
        back = mask_of(rows, wp) * ((bias_grad3 + third[rows, :] * gain_grad3) / count_wp)
        tg[rows, :] = (scale3 * (og[rows, :] - back)).astype(BF16)

    each_chunk(third_step)

    p2s, p2r = p1s, p1r
    sent_done("pre1")
    for j in far_first:
        p2s[j] = nt(tg[...], w2r[j, 0:ip, :]).astype(BF16)
        send("grad2", p2s.at[j, pl.ds(0, RS)], p2r.at[c, pl.ds(0, RS)], (d, j))
    for k in late:
        spread_chips(k, 0)
        if k > 1:
            spread_chips(k, 1)
    acc[...] = nt(tg[...], w2r[c, 0:ip, :])

    class Reduction:
        def __init__(self, name, z, part):
            self.name, self.z, self.part = name, z, part
            self.gs, self.rb, self.sm, self.rq, self.tot, self.fin = (
                v[("exp" if name == "red" and s in ("gs", "rb") else name) + "_" + s]
                for s in ("gs", "rb", "sm", "rq", "tot", "fin")
            )

        def pieces(self, first, rows):
            row, end = first, first + rows
            while row < end:
                owner = row // self.part
                stop = min(end, (owner + 1) * self.part)
                yield owner, row - owner * self.part, row - first, stop - row
                row = stop

        def put(self, zi, first, value):
            for owner, there, here, n in self.pieces(first, value.shape[0]):
                self.gs[owner % 2, owner // 2, zi, there : there + n, :] = value[here : here + n, :]

        def take(self, zi, first, rows):
            found = [
                self.fin[owner % 2, owner // 2, zi, there : there + n, :].astype(F32)
                for owner, there, _, n in self.pieces(first, rows)
            ]
            return jnp.concatenate(found, axis=0)

        def pair(self):
            send(self.name + "core", self.gs.at[1 - h], self.rb, (sibling, c))

        def chips(self):
            got(self.name + "core", self.rb)
            for e in range(Q):
                self.sm[e] = (self.gs[h, e].astype(F32) + self.rb[e].astype(F32)).astype(BF16)
            for e in qpeers:
                send(self.name + "chip", self.sm.at[e], self.rq.at[q], (2 * e + h, c))

        def chan(self):
            got(self.name + "chip", self.rq.at[pl.ds(0, Q - 1)])
            total = self.sm[q].astype(F32)
            for e in qpeers:
                total = total + self.rq[e].astype(F32)
            self.tot[...] = total.astype(BF16)
            if self.z == 1:
                self.fin[h, q, 0] = self.tot[0]
            else:
                self.fin[h, q, c] = self.tot[c]
                for j in zpeers:
                    send("z" + self.name, self.tot.at[j], self.fin.at[h, q, c], (d, j))

        def halves(self, side, other):
            cut = round_up(self.part // 2, 16)
            rows = pl.ds(0, cut) if side == 0 else pl.ds(cut, self.part - cut)
            return self.fin.at[h, other, slice(None), rows]

        def back(self, side):
            if side == 0 and self.z > 1:
                got("z" + self.name, self.fin.at[h, q, pl.ds(0, C - 1)])
            if side == 1 and self.part <= 16:
                return
            for e in qpeers:
                send(self.name + "back" + str(side), self.halves(side, q), self.halves(side, q), (2 * e + h, c))

        def other(self):
            cut = round_up(self.part // 2, 16)
            got(self.name + "back0", self.fin.at[h, pl.ds(0, Q - 1), slice(None), pl.ds(0, cut)])
            if self.part > 16:
                got(self.name + "back1", self.fin.at[h, pl.ds(0, Q - 1), slice(None), pl.ds(cut, self.part - cut)])
            send(self.name + "pair", self.fin.at[h], self.fin.at[h], (sibling, c))

        def done(self):
            got(self.name + "pair", self.fin.at[0])

    def adam(state, at, grad, rate, decay):
        weight, moment, square, average = (state[(part, *at)] for part in range(4))
        first = beta_one * moment + (1.0 - beta_one) * grad
        second = beta_two * square + (1.0 - beta_two) * grad * grad
        scaled = first * (1.0 / (1.0 - beta_one**STEP))
        root = jnp.sqrt(second * (1.0 / (1.0 - beta_two**STEP))) + adam_eps
        updated = weight - rate * (scaled / root + decay * weight)
        state[(0, *at)] = updated
        state[(1, *at)] = first
        state[(2, *at)] = second
        state[(3, *at)] = ema_rate * average + (1.0 - ema_rate) * updated

    def adam_rows(red, state, rate):
        for j in range(C):
            for first in range(0, ip, 32):
                n = min(32, ip - first)
                adam(state, (slice(first, first + n), slice(j * wp, (j + 1) * wp)), red.take(j, first, n), rate, decay_rate)

    exp_red = Reduction("exp", C, sz.PW)
    spa_red = Reduction("spa", 1, sz.PS)
    red_red = Reduction("red", C, sz.PW)
    for j in range(C):
        exp_red.put(j, 0, tn(act2[:, j * ip : (j + 1) * ip], tg[...]).astype(BF16))
    exp_red.pair()

    exp_red.chips()
    for k in late[:-1]:
        spread_pair(k)
    add_partials("grad2", p2r)
    inverse_own, shift_own, gain_own, bias_own = (pm2[c, r : r + 1, :] for r in range(4))

    def second_back(rows, carry):
        normed = v2[c, rows, :].astype(F32) * inverse_own + shift_own
        value = gain_own * normed + bias_own
        s = sigmoid(value)
        grad = acc[rows, :] * (s * (1.0 + value * (1.0 - s))) * mask_of(rows, ip)
        d2b[c, rows, :] = grad.astype(BF16)
        return carry[0] + fold_rows(grad), carry[1] + fold_rows(grad * normed)

    zero_ip = jnp.zeros((8, ip), F32)
    sums = over_chunks(second_back, (zero_ip, zero_ip))
    st5[d] = rows_of(total_of(sums[0]), total_of(sums[1]))
    exchange_dp("bk2", st5)
    send_part("dlt2top", d2b, top_rows)
    bias_own2, gain_own2 = sum_dp("bk2", st5)
    pm3[c] = rows_of(bias_own2 / count_ip, gain_own2 / count_ip)
    send_z("dlt2par", pm3)
    send_part("dlt2low", d2b, low_rows)
    for k in late[-1:]:
        spread_chips(k, 1)
    exp_red.chan()
    sgo = v["sgo"]

    def own_second(rows):
        normed = v2[c, rows, :].astype(F32) * inverse_own + shift_own
        back = mask_of(rows, ip) * (pm3[c, 0:1, :] + normed * pm3[c, 1:2, :])
        sgo[rows, :] = (inverse_own * gain_own * (d2b[c, rows, :].astype(F32) - back)).astype(BF16)

    each_chunk(own_second)
    for tap in range(TAPS):
        spa_red.put(0, tap * ip, tn(sgo[...], cols[tap]).astype(BF16))
    spa_red.pair()
    for k in late[-1:]:
        spread_pair(k)
    spa_red.chips()
    for load in state_loads:
        load.wait()
    fag = v["fag"]
    inverse2, shift2, gain2 = (table_row(pm2, r) for r in range(3))
    scale2 = inverse2 * gain2

    def full_second(part):
        bias_part, gain_part = table_row(pm3, 0), table_row(pm3, 1)

        def step(rows):
            normed = joined(v2, rows) * inverse2 + shift2
            back = mask_of(rows, K) * (bias_part + normed * gain_part)
            big[rows, :] = (scale2 * (joined(d2b, rows) - back)).astype(BF16).astype(F32)

        each_chunk(step, part)

    def first_act_grad(cells, first, last):
        rows = out_rows(cells)
        if first == 0:
            fag[rows, :] = jnp.zeros((rows.stop - rows.start, K), F32)

        def step(tap, carry):
            offset = ((2 - lax.div(tap, 3)) * PITCH + 2 - lax.rem(tap, 3)) * I
            weight = jnp.concatenate([weight_of(j, tap) for j in range(C)], axis=0)
            fag[rows, :] += nn(shifted(offset, cells), weight)
            return carry

        lax.fori_loop(first, last, step, 0)

    got_part("dlt2top", d2b, top_rows)
    got_z("dlt2par", pm3)
    full_second(top_part)
    fill_pad(top_cells)
    for k in range(C - 1):
        spread_done(k)
    first_act_grad(top_out, 0, TAPS)
    got_part("dlt2low", d2b, low_rows)
    full_second(low_part)
    fill_pad(low_cells)
    exp_red.back(0)
    exp_red.back(1)
    first_act_grad(low_out, 0, TAPS)

    inverse1, shift1, gain1, bias1 = (table_row(pm1, r) for r in range(4))

    def first_back(rows, carry):
        normed = joined(v1, rows) * inverse1 + shift1
        value = gain1 * normed + bias1
        s = sigmoid(value)
        grad = fag[rows, :] * (s * (1.0 + value * (1.0 - s))) * mask_of(rows, K)
        fag[rows, :] = grad
        big[rows, :] = normed
        return carry[0] + fold_rows(grad), carry[1] + fold_rows(grad * normed)

    zero_k = jnp.zeros((8, K), F32)
    sums = over_chunks(first_back, (zero_k, zero_k))
    st6[d] = rows_of(4, total_of(sums[0]), total_of(sums[1]))
    exchange_dp("bk1", st6)
    exp_red.other()
    spa_red.chan()
    bias_grad1, gain_grad1 = sum_dp("bk1", st6)
    spa_red.back(0)
    scale1 = inverse1 * gain1
    fg = v["fg"]

    def first_step(rows):
        back = mask_of(rows, K) * ((bias_grad1 + big[rows, :] * gain_grad1) / count_k)
        fg[rows, :] = (scale1 * (fag[rows, :] - back)).astype(BF16)

    each_chunk(first_step)
    sent_done("expcore")
    for j in range(C):
        red_red.put(j, 0, tn(fg[:, j * ip : (j + 1) * ip], xb[...]).astype(BF16))
    red_red.pair()
    input_grad[...] = nn(fg[...], w1r[...].reshape(K, wp)) + og[...]
    red_red.chips()

    def adam_spatial(first_tap, last_tap):
        for tap in range(first_tap, last_tap):
            for first in range(0, ip, 32):
                n = min(32, ip - first)
                adam(
                    spa_state, (tap, slice(first, first + n), slice(0, K)), spa_red.take(0, tap * ip + first, n),
                    2.0 / math.sqrt(TAPS * K), decay_rate,
                )

    red_red.chan()
    spa_red.back(1)
    red_red.back(0)
    red_red.back(1)
    spa_red.other()
    exp_red.done()
    adam_rows(exp_red, exp_state, 2.0 / math.sqrt(K))
    spa_red.done()
    adam_spatial(0, TAPS // 2)
    red_red.other()
    adam_spatial(TAPS // 2, TAPS)

    first_grads = own_part(jnp.concatenate([gain_grad1, bias_grad1], axis=0))
    inner_grads = [first_grads[0:1, :], gain_own2, first_grads[1:2, :], bias_own2]
    outer_grads = [gain_grad3, bias_grad3]
    inner_state[0:4, :] = inner_norm[...]
    for m in range(2):
        for r in range(2):
            inner_state[4 + 4 * m + 2 * r : 6 + 4 * m + 2 * r, :] = inner_moments[m, r]
    inner_state[12:16, :] = inner_ema[...]
    outer_state[0:2, :] = outer_norm[...]
    outer_state[2:6, :] = outer_moments[...]
    outer_state[6:8, :] = outer_ema[...]

    def adam_small(state, n, grads):
        grad = jnp.concatenate(grads, axis=0)
        weight, moment, square, average = (state[part * n : (part + 1) * n, :] for part in range(4))
        first = beta_one * moment + (1.0 - beta_one) * grad
        second = beta_two * square + (1.0 - beta_two) * grad * grad
        scaled = first * (1.0 / (1.0 - beta_one**STEP))
        root = jnp.sqrt(second * (1.0 / (1.0 - beta_two**STEP))) + adam_eps
        updated = weight - norm_rate * (scaled / root)
        state[0:n, :] = updated
        state[n : 2 * n, :] = first
        state[2 * n : 3 * n, :] = second
        state[3 * n : 4 * n, :] = ema_rate * average + (1.0 - ema_rate) * updated

    adam_small(inner_state, 4, inner_grads)
    adam_small(outer_state, 2, outer_grads)
    red_red.done()
    adam_rows(red_red, red_state, 2.0 / math.sqrt(sz.W))
    for name, ref in sent:
        wait_bytes(ref, ssem.at[sem_of[name]])


def store_kernel(n, *refs):
    held, places, sem = refs[:7], refs[7 : 7 + n], refs[-1]
    output, input_grad, red_state, spa_state, exp_state, inner_state, outer_state = held
    parts = [output.at[pl.ds(0, places[0].shape[0])], input_grad.at[pl.ds(0, places[1].shape[0])]]
    for state in (red_state, spa_state, exp_state):
        parts += [state.at[part] for part in range(4)]
    copies = [pltpu.make_async_copy(src, dst, sem.at[i]) for i, (src, dst) in enumerate(zip(parts, places))]
    for copy in copies:
        copy.start()
    inner_places, outer_places = places[14:18], places[18:22]
    for part in range(4):
        inner_places[part][...] = inner_state[part * 4 : (part + 1) * 4, :]
        outer_places[part][...] = outer_state[part * 2 : (part + 1) * 2, :]
    for copy in copies:
        copy.wait()


def per_device(
    mesh_dp, mesh_chan,
    images, groups, cotangent, reduce_weight, spatial_weight, expand_weight, inner_norm, outer_norm,
    reduce_moments, spatial_moments, expand_moments, inner_moments, outer_moments,
    reduce_ema, spatial_ema, expand_ema, inner_ema, outer_ema,
):
    sz = Sizes(mesh_dp, mesh_chan, images, reduce_weight)
    ip, wp, K, C = sz.ip, sz.wp, sz.K, sz.C

    def by_cell(a):
        return a.transpose(1, 0, 2).reshape(sz.R, wp)

    def by_tap(a):
        return a.transpose(1, 2, 0, 3).reshape(TAPS, ip, K)

    any_spec, vmem_spec = pl.BlockSpec(memory_space=pl.ANY), pl.BlockSpec(memory_space=pltpu.VMEM)
    states = []
    for weight, moments, ema in (
        (reduce_weight, reduce_moments, reduce_ema),
        (by_tap(spatial_weight), spatial_moments.transpose(0, 2, 3, 1, 4).reshape(2, TAPS, ip, K), by_tap(spatial_ema)),
        (expand_weight, expand_moments, expand_ema),
    ):
        states += [weight, moments, ema]
    held_shapes = (
        (sz.RP, wp), (sz.RP, wp), (4, ip, sz.W), (4, TAPS, ip, K), (4, ip, sz.W), (16, ip), (8, wp),
    )
    held = pl.pallas_call(
        functools.partial(block_kernel, sz),
        out_shape=tuple(pltpu.VMEM(shape, F32) for shape in held_shapes),
        in_specs=[pl.BlockSpec(memory_space=pltpu.SMEM)] + [any_spec] * 2 + [vmem_spec] * 6 + [any_spec] * 9,
        out_specs=(vmem_spec,) * len(held_shapes),
        scratch_shapes=[pltpu.VMEM(shape, dtype) for _, shape, dtype in scratch_table(sz)]
        + [
            pltpu.SemaphoreType.DMA((5,)),
            pltpu.SemaphoreType.DMA((6,)),
            pltpu.SemaphoreType.DMA((len(phases(sz)),)),
            pltpu.SemaphoreType.DMA((len(phases(sz)),)),
        ],
        compiler_params=pltpu.CompilerParams(
            collective_id=0, has_side_effects=True, vmem_limit_bytes=VMEM_TOTAL - sum(vmem_bytes(shape, F32) for shape in held_shapes)
        ),
    )(
        groups, by_cell(images), by_cell(cotangent),
        inner_norm.reshape(4, ip), outer_norm, inner_moments, outer_moments.reshape(4, wp),
        inner_ema.reshape(4, ip), outer_ema, *states,
    )
    held = [pltpu.with_memory_space_constraint(a, pltpu.VMEM) for a in held]
    shapes = [(sz.R, wp)] * 2 + [(ip, sz.W)] * 4 + [(TAPS, ip, K)] * 4 + [(ip, sz.W)] * 4
    small = [(4, ip)] * 4 + [(2, wp)] * 4
    results = pl.pallas_call(
        functools.partial(store_kernel, len(shapes + small)),
        out_shape=tuple(jax.ShapeDtypeStruct(shape, F32) for shape in shapes + small),
        in_specs=[vmem_spec] * len(held),
        out_specs=(any_spec,) * len(shapes) + (vmem_spec,) * len(small),
        scratch_shapes=[pltpu.SemaphoreType.DMA((len(shapes),))],
        compiler_params=pltpu.CompilerParams(vmem_limit_bytes=2 * 2**20),
    )(*held)
    images_of = [a.reshape(PIX, sz.I, wp).transpose(1, 0, 2) for a in results[:2]]
    taps = [a.reshape(3, 3, ip, K).transpose(2, 0, 1, 3) for a in results[6:10]]
    inner = [a.reshape(2, 2, ip) for a in results[14:18]]
    return (*images_of, *results[2:6], *taps, *results[10:14], *inner, *results[18:22])


def solution(mesh):
    placed = (
        P("dp", None, "chan"),
        P("dp"),
        P("dp", None, "chan"),
        P("chan", None),
        P("chan", None, None, None),
        P("chan", None),
        P(None, None, "chan"),
        P(None, "chan"),
        P(None, "chan", None),
        P(None, "chan", None, None, None),
        P(None, "chan", None),
        P(None, None, None, "chan"),
        P(None, None, "chan"),
        P("chan", None),
        P("chan", None, None, None),
        P("chan", None),
        P(None, None, "chan"),
        P(None, "chan"),
    )
    return jax.shard_map(
        functools.partial(per_device, mesh.shape["dp"], mesh.shape["chan"]),
        mesh=mesh,
        in_specs=placed,
        out_specs=(P("dp", None, "chan"),) * 2
        + (P("chan", None),) * 4
        + (P("chan", None, None, None),) * 4
        + (P("chan", None),) * 4
        + (P(None, None, "chan"),) * 4
        + (P(None, "chan"),) * 4,
        check_vma=False,
    )
```
